128 devices in a mesh: row: 8 (over x, y_hi), col: 16 (over y_lo, z, core).
Axes of the slice: x: 4, y: 4 (y_hi: 2, y_lo: 2; y = y_hi * 2 + y_lo), z: 4, core: 2. Of those that a mesh axis runs over, the one named last changes fastest.
Arguments:
- tokens: bfloat16 [1024, 6144], P('row', 'col'), may hold values from -6 to 6
- weight_in: bfloat16 [6144, 24576], P('col', 'row'), may hold values from -0.078125 to 0.078125
- weight_out: bfloat16 [24576, 6144], P('row', 'col'), may hold values from -0.0390625 to 0.0390625
- cotangent: bfloat16 [1024, 6144], P('row', 'col'), may hold values from -6 to 6
Outputs:
- output: bfloat16 [1024, 6144], P('row', 'col')
- grad_tokens: bfloat16 [1024, 6144], P('row', 'col')
- grad_in: bfloat16 [6144, 24576], P('col', 'row')
- grad_out: bfloat16 [24576, 6144], P('row', 'col')
The draws below stay inside these ranges and needn't reach their ends.
All inputs are finite; a program needn't handle non-finite values.
Results may differ from the reference program's by a relative error of at most 0.0049.
Values may be sent and summed in bfloat16 or wider, within the bound.
A program may use at most 128 MiB of HBM per device.

```python
import jax
import jax.numpy as jnp
from jax import lax

D = 6144
FF = 24576
TOKENS = 1024


def spiked(values, rng, source, target, blocks, factor):
    def block_of(dim):
        return (jnp.arange(values.shape[dim]) // (values.shape[dim] // blocks)).reshape((-1,) + (1,) * (values.ndim - 1 - dim))

    first = jax.random.permutation(rng, blocks)[block_of(target)]
    second = (block_of(target) + blocks // 2) % blocks
    return jnp.where((block_of(source) == first) | (block_of(source) == second), factor * values, values)


def level_of(own_key, extent, split, least, largest):
    def one(dim, blocks):
        steps = jax.random.uniform(jax.random.fold_in(jax.random.fold_in(own_key, 6), dim), (blocks,), jnp.float32, least / len(split), largest / len(split))
        return jnp.repeat(jnp.exp(steps), extent[dim] // blocks).reshape((-1,) + (1,) * (len(extent) - dim - 1))

    gain = one(*split[0])
    for cut in split[1:]:
        gain = gain * one(*cut)
    return gain


def centred(own_key, shape, spread, reach, shards=(), dtype=jnp.bfloat16):
    level = level_of(own_key, shape, shards, -0.22, 0.18) if shards else 1.0
    values = jax.random.normal(own_key, shape, jnp.float32) * spread * level
    return jnp.minimum(jnp.maximum(values, -reach), reach).astype(dtype)


def gaussian_with(key, shape, width, reach, cuts, heavy, dtype=jnp.bfloat16):
    result = width * jax.random.normal(key, shape, jnp.float32)
    if cuts:
        result = result * level_of(key, shape, cuts, -0.22, 0.18)
    return jnp.clip(spiked(result, jax.random.fold_in(key, 3), *heavy), -reach, reach).astype(dtype)


def setup_inputs(seed: int = 0) -> dict:
    seeds = jax.random.split(jax.random.key(seed), 5)
    return {
        "tokens": gaussian_with(seeds[0], (TOKENS, D), 1.0, 6.0, ((0, 8), (1, 16)), (1, 0, 16, 2.0)),
        "weight_in": centred(seeds[1], (D, FF), D ** -0.5, 0.078125, ((0, 16), (1, 8))),
        "weight_out": centred(seeds[2], (FF, D), FF ** -0.5, 0.0390625, ((0, 8), (1, 16))),
        "cotangent": gaussian_with(seeds[3], (TOKENS, D), 1.0, 6.0, ((0, 8), (1, 16)), (1, 0, 16, 2.0)),
    }


def gelu_tanh(values):
    return jax.nn.gelu(values, approximate=True)

def reference(tokens, weight_in, weight_out, cotangent):
    hidden = jnp.dot(tokens, weight_in, preferred_element_type=jnp.float32)
    grad_acts = lax.dot_general(cotangent, weight_out, (((1,), (1,)), ((), ())), preferred_element_type=jnp.float32)
    activated, pullback = jax.vjp(gelu_tanh, hidden)
    acts = activated.astype(jnp.bfloat16)
    output = jnp.dot(acts, weight_out, preferred_element_type=jnp.float32).astype(jnp.bfloat16)
    grad_hidden = pullback(grad_acts)[0].astype(jnp.bfloat16)
    grad_out = lax.dot_general(acts, cotangent, (((0,), (0,)), ((), ())), preferred_element_type=jnp.float32).astype(jnp.bfloat16)
    grad_in = lax.dot_general(tokens, grad_hidden, (((0,), (0,)), ((), ())), preferred_element_type=jnp.float32).astype(jnp.bfloat16)
    grad_tokens = lax.dot_general(grad_hidden, weight_in, (((1,), (1,)), ((), ())), preferred_element_type=jnp.float32).astype(jnp.bfloat16)
    return (output, grad_tokens, grad_in, grad_out)
```

```python
import functools

import jax
import jax.numpy as jnp
from jax import lax
from jax.experimental import pallas as pl
from jax.experimental.pallas import tpu as pltpu
from jax.sharding import PartitionSpec as P

F32 = jnp.float32
BF16 = jnp.bfloat16

TOK = 1024
BLK = 128
DC = 384
DP = 2 * DC
FH = 1536
FA = 768
FB = FH - FA

COPIES = 128
C_GELU = 0.7978845608028654
C_CUBE = 0.044715


def row_loop(rows, chunk, body):
    def step(i, carry):
        body(pl.multiple_of(i * chunk, chunk))
        return carry

    lax.fori_loop(0, rows // chunk, step, 0)


def tiles(count, body):
    def step(i, carry):
        body(i)
        return carry

    lax.fori_loop(0, count, step, 0)


class Links:
    def __init__(self, send, recv):
        self.send, self.recv, self.used, self.started = send, recv, 0, []
        row, col = lax.axis_index("row"), lax.axis_index("col")
        self.x, self.yh = row // 2, row % 2
        self.yl, self.z, self.k = col // 8, (col // 2) % 4, col % 2

    def device(self, **moved):
        at = {n: moved.get(n, getattr(self, n)) for n in ("x", "yh", "yl", "z", "k")}
        return (at["x"] * 2 + at["yh"], at["yl"] * 8 + at["z"] * 2 + at["k"])

    def ring(self, axis, step):
        return self.device(**{axis: lax.rem(getattr(self, axis) + step + 4, 4)})

    def other(self, axis):
        return self.device(**{axis: 1 - getattr(self, axis)})

    def copy(self, src, dst, device):
        i = self.used
        self.used += 1
        c = pltpu.make_async_remote_copy(
            src_ref=src,
            dst_ref=dst,
            send_sem=self.send.at[i],
            recv_sem=self.recv.at[i],
            device_id=device,
            device_id_type=pl.DeviceIdType.MESH,
        )
        c.start()
        self.started.append(c)
        return c

    def place(self, axis, step):
        return lax.rem(getattr(self, axis) + step + 4, 4)


def rows_of(place, member, count=BLK, skip=0):
    return pl.ds(pl.multiple_of(place * (2 * BLK) + member * BLK + skip, 16), count)


class GatherRingLast:
    def __init__(self, links, ring, pair, buf, cols):
        self.l, self.ring, self.pair, self.buf, self.cols = links, ring, pair, buf, cols
        self.me, self.mine = getattr(links, ring), getattr(links, pair)

    def at(self, step, member):
        return self.buf.at[rows_of(self.l.place(self.ring, step), member), self.cols]

    def send(self, ref, device):
        return self.l.copy(ref, ref, device)

    def start(self):
        own = self.at(0, self.mine)
        self.y = self.send(own, self.l.other(self.pair))
        self.own_p = self.send(own, self.l.ring(self.ring, 1))
        self.own_m = self.send(own, self.l.ring(self.ring, -1))

    def second(self):
        self.y.wait_recv()
        theirs = self.at(0, 1 - self.mine)
        self.oth_p = self.send(theirs, self.l.ring(self.ring, 1))
        self.oth_m = self.send(theirs, self.l.ring(self.ring, -1))

    def third(self):
        self.own_p.wait_recv()
        self.far_p = self.send(self.at(-1, self.mine), self.l.ring(self.ring, 1))
        self.own_m.wait_recv()
        self.oth_m.wait_recv()
        self.far_m = self.send(self.at(1, 1 - self.mine), self.l.ring(self.ring, -1))
        self.oth_p.wait_recv()

    def finish(self):
        self.far_p.wait_recv()
        self.far_m.wait_recv()


class GatherRingFirst:
    def __init__(self, links, ring, pair, buf, cols):
        self.l, self.ring, self.pair, self.buf, self.cols = links, ring, pair, buf, cols
        self.mine = getattr(links, pair)

    def at(self, step, count=BLK, skip=0):
        return self.buf.at[rows_of(self.l.place(self.ring, step), self.mine, count, skip), self.cols]

    def send(self, ref, device):
        return self.l.copy(ref, ref, device)

    def across(self, ref):
        return self.send(ref, self.l.other(self.pair))

    def start(self):
        own = self.at(0)
        self.own_p = self.send(own, self.l.ring(self.ring, 1))
        self.own_m = self.send(own, self.l.ring(self.ring, -1))
        self.y0 = self.across(own)

    def second(self):
        self.own_p.wait_recv()
        self.far_p = self.send(self.at(-1, BLK // 2), self.l.ring(self.ring, 1))
        self.yp = self.across(self.at(-1))
        self.own_m.wait_recv()
        self.far_m = self.send(self.at(1, BLK // 2, BLK // 2), self.l.ring(self.ring, -1))
        self.ym = self.across(self.at(1))

    def third(self):
        self.far_p.wait_recv()
        self.yfp = self.across(self.at(2, BLK // 2))
        self.far_m.wait_recv()
        self.yfm = self.across(self.at(2, BLK // 2, BLK // 2))

    def near(self):
        for c in (self.y0, self.yp, self.ym):
            c.wait_recv()

    def finish(self):
        self.yfp.wait_recv()
        self.yfm.wait_recv()


class ReduceRingFirst:
    def __init__(self, links, ring, pair, part, out, col, out_col, width, slots):
        self.l, self.ring, self.pair = links, ring, pair
        self.part, self.out, self.col, self.width, self.slots = part, out, col, width, slots
        self.out_cols = pl.ds(out_col, width)
        self.mine = getattr(links, pair)

    def rows(self, step, member):
        return rows_of(self.l.place(self.ring, step), member)

    def block(self, step, member):
        return self.out.at[self.rows(step, member), self.out_cols]

    def sent(self, step):
        l = self.l
        if step == 2:
            self.p2 = l.copy(self.block(2, 0), self.slots.at[0], l.ring(self.ring, 1))
            self.m2 = l.copy(self.block(2, 1), self.slots.at[1], l.ring(self.ring, -1))
        elif step == 1:
            self.p1 = l.copy(self.block(1, 1), self.slots.at[2], l.ring(self.ring, 1))
        elif step == 3:
            self.m1 = l.copy(self.block(-1, 0), self.slots.at[3], l.ring(self.ring, -1))

    def add(self, dst, rows_start, *slots):
        def body(r):
            total = self.part[pl.ds(rows_start + r, 32), pl.ds(self.col, self.width)]
            for s in slots:
                total = total + self.slots[s, pl.ds(r, 32), :].astype(F32)
            dst(r, total)

        row_loop(BLK, 32, body)

    def start_of(self, step, member):
        return pl.multiple_of(self.l.place(self.ring, step) * (2 * BLK) + member * BLK, BLK)

    def to_slot(self, slot):
        def put(r, total):
            self.slots[slot, pl.ds(r, 32), :] = total.astype(BF16)

        return put

    def combine(self):
        l = self.l
        self.p2.wait_recv()
        self.add(self.to_slot(7), self.start_of(1, 0), 0)
        self.pc = l.copy(self.slots.at[7], self.slots.at[4], l.ring(self.ring, 1))
        self.m2.wait_recv()
        self.add(self.to_slot(8), self.start_of(-1, 1), 1)
        self.mc = l.copy(self.slots.at[8], self.slots.at[5], l.ring(self.ring, -1))

    def across(self):
        for c in (self.p1, self.m1, self.pc, self.mc):
            c.wait_recv()
        for member, slots in ((0, (4, 3)), (1, (2, 5))):
            start = self.start_of(0, member)

            def put(r, total, start=start):
                self.part[pl.ds(start + r, 32), pl.ds(self.col, self.width)] = total

            self.add(put, start, *slots)
        self.add(self.to_slot(9), self.start_of(0, 1 - self.mine))
        self.y = self.l.copy(self.slots.at[9], self.slots.at[6], self.l.other(self.pair))

    def finish(self, put):
        self.y.wait_recv()
        self.add(put, self.start_of(0, self.mine), 6)


class ReducePairFirst:
    def __init__(self, links, ring, pair, part, out, col, width, slots, halves):
        self.l, self.ring, self.pair = links, ring, pair
        self.part, self.out, self.col, self.width = part, out, col, width
        self.slots, self.halves = slots, halves
        self.mine = getattr(links, pair)
        self.y = {}

    def sent(self, step):
        rows = rows_of(self.l.place(self.ring, step), 1 - self.mine)
        block = self.out.at[rows, pl.ds(self.col, self.width)]
        self.y[step] = self.l.copy(block, self.slots.at[step], self.l.other(self.pair))

    def add(self, dst, step, skip, count, *halves):
        start = pl.multiple_of(self.l.place(self.ring, step) * (2 * BLK) + self.mine * BLK + skip, 64)

        def body(r):
            total = self.part[pl.ds(start + r, 32), pl.ds(self.col, self.width)]
            total = total + self.slots[step, pl.ds(skip + r, 32), :].astype(F32)
            for h in halves:
                total = total + self.halves[h, pl.ds(r, 32), :].astype(F32)
            dst(r, total)

        row_loop(count, 32, body)

    def to_half(self, half):
        def put(r, total):
            self.halves[half, pl.ds(r, 32), :] = total.astype(BF16)

        return put

    def ring_copy(self, src, dst, step):
        return self.l.copy(src, self.halves.at[dst], self.l.ring(self.ring, step))

    def pairs(self):
        half = BLK // 2
        self.y[2].wait_recv()

        def put(r, total):
            self.slots[4, pl.ds(r, 32), :] = total.astype(BF16)

        self.add(put, 2, 0, BLK)
        self.p2 = self.ring_copy(self.slots.at[4, pl.ds(0, half)], 0, 1)
        self.m2 = self.ring_copy(self.slots.at[4, pl.ds(half, half)], 1, -1)
        self.y[1].wait_recv()
        self.add(self.to_half(6), 1, half, half)
        self.p1 = self.ring_copy(self.halves.at[6], 2, 1)
        self.y[3].wait_recv()
        self.add(self.to_half(7), 3, 0, half)
        self.m1 = self.ring_copy(self.halves.at[7], 3, -1)

    def combine(self):
        half = BLK // 2
        self.p2.wait_recv()
        self.add(self.to_half(8), 1, 0, half, 0)
        self.pc = self.ring_copy(self.halves.at[8], 4, 1)
        self.m2.wait_recv()
        self.add(self.to_half(9), 3, half, half, 1)
        self.mc = self.ring_copy(self.halves.at[9], 5, -1)

    def finish(self, put):
        half = BLK // 2
        for c in (self.y[0], self.p1, self.m1, self.pc, self.mc):
            c.wait_recv()
        self.add(put, 0, 0, half, 4, 3)
        self.add(lambda r, total: put(half + r, total), 0, half, half, 2, 5)


def dot(a, b, left, right):
    return lax.dot_general(a, b, (((left,), (right,)), ((), ())), preferred_element_type=F32)


def kernel(
    tok_in, wi_in, wo_in, cot_in,
    out_ref, gt_ref, gi_ref, go_ref,
    tok, cot, wi, wo,
    part_h, part_g, send_h, send_g,
    ra_h, ra_g, rb_h, rb_g, rh_h, rh_g,
    hid, gacts, acts, ghid,
    sib_out, sib_in, rbuf, rd,
    gi, go, final,
    send, recv, local,
):
    l = Links(send, recv)
    k = l.k
    sib = l.other("k")

    barrier = pltpu.get_barrier_semaphore()
    near = [sib, l.other("yl"), l.other("yh")]
    near += [l.ring(a, s) for a in ("z", "x") for s in (1, -1)]
    for d in near:
        pl.semaphore_signal(barrier, inc=1, device_id=d, device_id_type=pl.DeviceIdType.MESH)

    my_d = pl.ds(pl.multiple_of(k * DC, 128), DC)
    its_d = pl.ds(pl.multiple_of((1 - k) * DC, 128), DC)
    my_f = pl.ds(pl.multiple_of(k * FH, 128), FH)
    its_f = pl.ds(pl.multiple_of((1 - k) * FH, 128), FH)
    own_rows = rows_of(l.x, l.yh)

    loads = [
        pltpu.make_async_copy(tok_in, tok.at[own_rows, my_d], local.at[0]),
        pltpu.make_async_copy(cot_in, cot.at[own_rows, my_d], local.at[1]),
        pltpu.make_async_copy(wi_in.at[:, my_f], wi.at[my_d], local.at[2]),
        pltpu.make_async_copy(wo_in.at[my_f], wo.at[:, my_d], local.at[3]),
    ]
    for c in loads:
        c.start()
    pl.semaphore_wait(barrier, len(near))

    gather_tok = GatherRingLast(l, "x", "yh", tok, my_d)
    gather_cot = GatherRingLast(l, "x", "yh", cot, my_d)
    loads[0].wait()
    gather_tok.start()
    wi_copy = l.copy(wi_in.at[:, its_f], wi.at[my_d], sib)
    loads[1].wait()
    gather_cot.start()
    wo_copy = l.copy(wo_in.at[its_f], wo.at[:, my_d], sib)

    def share(buf, step):
        ref = buf.at[pl.ds(pl.multiple_of(l.place("x", step) * (2 * BLK), 2 * BLK), 2 * BLK), my_d]
        return l.copy(ref, ref, sib)

    shared_tok, shared_cot = [], []
    gather_tok.second()
    shared_tok.append(share(tok, 0))
    gather_tok.third()
    shared_tok += [share(tok, 1), share(tok, -1)]
    gather_cot.second()
    shared_cot.append(share(cot, 0))
    gather_tok.finish()
    shared_tok.append(share(tok, 2))
    for c in shared_tok:
        c.wait_recv()
    loads[2].wait()
    wi_copy.wait_recv()

    ring = [
        ReduceRingFirst(l, "z", "yl", part, out, 0, 0, FA, slots)
        for part, out, slots in ((part_h, send_h, ra_h), (part_g, send_g, ra_g))
    ]
    pair = [
        ReducePairFirst(l, "z", "yl", part, out, FA, FB, slots, halves)
        for part, out, slots, halves in ((part_h, send_h, rb_h, rh_h), (part_g, send_g, rb_g, rh_g))
    ]

    def pair_rows(axis, step):
        return pl.ds(pl.multiple_of(l.place(axis, step) * (2 * BLK), 2 * BLK), 2 * BLK)

    def partial_hidden(step):
        rows = pair_rows("z", step)

        def tile(n):
            cols = pl.ds(pl.multiple_of(n * 512, 512), 512)
            total = dot(tok[rows, :], wi[:, cols], 1, 0)
            part_h[rows, cols] = total
            send_h[rows, cols] = total.astype(BF16)

        tiles(FH // 512, tile)
        ring[0].sent(step)
        pair[0].sent(step)

    def partial_grad(step):
        rows = pair_rows("z", step)

        def tile(n):
            cols = pl.ds(pl.multiple_of(n * 512, 512), 512)
            total = dot(cot[rows, :], wo[cols, :], 1, 1)
            part_g[rows, cols] = total
            send_g[rows, cols] = total.astype(BF16)

        tiles(FH // 512, tile)
        ring[1].sent(step)
        pair[1].sent(step)

    for step in (2, 1, 3, 0):
        partial_hidden(step)
    gather_cot.third()
    shared_cot += [share(cot, 1), share(cot, -1)]
    gather_cot.finish()
    shared_cot.append(share(cot, 2))

    ring[0].combine()
    pair[0].pairs()
    for c in shared_cot:
        c.wait_recv()
    loads[3].wait()
    wo_copy.wait_recv()
    partial_grad(2)
    pair[0].combine()
    ring[0].across()
    for step in (1, 3, 0):
        partial_grad(step)

    def put_into(buf, col, width):
        def put(r, total):
            buf[pl.ds(r, 32), pl.ds(col, width)] = total

        return put

    own = pl.multiple_of(l.z * (2 * BLK) + l.yl * BLK, BLK)
    ring[0].finish(put_into(hid, 0, FA))
    pair[0].finish(put_into(hid, FA, FB))

    def activate(r):
        h = hid[pl.ds(r, 16), :]
        t = jnp.tanh(C_GELU * (h + C_CUBE * (h * h * h)))
        acts[pl.ds(own + r, 16), :] = (0.5 * h * (1.0 + t)).astype(BF16)

    row_loop(BLK, 16, activate)
    acts_a = GatherRingLast(l, "z", "yl", acts, pl.ds(0, FA))
    acts_b = GatherRingFirst(l, "z", "yl", acts, pl.ds(FA, FB))
    acts_a.start()
    acts_b.start()

    ring[1].combine()
    pair[1].pairs()
    acts_a.second()
    pair[1].combine()
    ring[1].across()
    acts_b.second()
    acts_a.third()
    acts_b.third()
    ring[1].finish(put_into(gacts, 0, FA))
    pair[1].finish(put_into(gacts, FA, FB))

    def pull(r):
        h = hid[pl.ds(r, 16), :]
        square = h * h
        t = jnp.tanh(C_GELU * (h + C_CUBE * (square * h)))
        slope = 0.5 * (1.0 + t) + (0.5 * C_GELU) * h * (1.0 - t * t) * (1.0 + 3.0 * C_CUBE * square)
        ghid[pl.ds(own + r, 16), :] = (gacts[pl.ds(r, 16), :] * slope).astype(BF16)

    row_loop(BLK, 16, pull)
    ghid_a = GatherRingLast(l, "z", "yl", ghid, pl.ds(0, FA))
    ghid_b = GatherRingFirst(l, "z", "yl", ghid, pl.ds(FA, FB))
    ghid_a.start()
    ghid_b.start()

    acts_b.near()
    acts_a.finish()
    acts_b.finish()

    out_pair = ReduceRingFirst(l, "x", "yh", part_h, rbuf.at[0], DP, 0, DC, rd.at[0])
    gt_pair = ReduceRingFirst(l, "x", "yh", part_g, rbuf.at[1], DP, 0, DC, rd.at[1])

    def project(which, part, lhs, weight, right, axis, step):
        rows = pair_rows(axis, step)
        part[rows, pl.ds(0, DP)] = dot(lhs[rows, :], weight[...], 1, right)
        start = pl.multiple_of(l.place(axis, step) * (2 * BLK), 2 * BLK)

        def cast(r):
            sib_out[which, pl.ds(start + r, 32), :] = part[pl.ds(start + r, 32), its_d].astype(BF16)

        row_loop(2 * BLK, 32, cast)
        return l.copy(sib_out.at[which, rows], sib_in.at[which, rows], sib)

    def merge(which, part, copy, step):
        copy.wait_recv()
        start = pl.multiple_of(l.place("x", step) * (2 * BLK), 2 * BLK)

        def body(r):
            at = pl.ds(start + r, 32)
            total = part[at, my_d] + sib_in[which, at, :].astype(F32)
            part[at, pl.ds(DP, DC)] = total
            rbuf[which, at, :] = total.astype(BF16)

        row_loop(2 * BLK, 32, body)

    steps = (2, 1, 3, 0)
    sent_out = [project(0, part_h, acts, wo, 0, "x", s) for s in steps[:2]]
    ghid_a.second()
    ghid_b.second()
    sent_out += [project(0, part_h, acts, wo, 0, "x", s) for s in steps[2:]]
    for s, c in zip(steps, sent_out):
        merge(0, part_h, c, s)
        out_pair.sent(s)
    ghid_a.third()
    ghid_b.third()

    def weight_grad_out(m):
        cols = pl.ds(pl.multiple_of(m * 256, 256), 256)
        go[cols, :] = dot(acts[:, cols], cot[...], 0, 0).astype(BF16)

    tiles(FH // 256, weight_grad_out)
    go_own = pltpu.make_async_copy(go.at[:, my_d], go_ref.at[my_f], local.at[4])
    go_own.start()
    go_sib = l.copy(go.at[:, its_d], go_ref.at[my_f], sib)

    out_pair.combine()
    out_pair.across()

    ghid_b.near()
    ghid_a.finish()
    ghid_b.finish()
    sent_gt = [project(1, part_g, ghid, wi, 1, "x", s) for s in steps]
    for s, c in zip(steps, sent_gt):
        merge(1, part_g, c, s)
        gt_pair.sent(s)

    def put_final(which):
        def put(r, total):
            final[which, pl.ds(r, 32), :] = total.astype(BF16)

        return put

    out_pair.finish(put_final(0))
    out_own = pltpu.make_async_copy(final.at[0], out_ref, local.at[5])
    out_own.start()

    def weight_grad_in(m):
        cols = pl.ds(pl.multiple_of(m * 256, 256), 256)
        gi[cols, :] = dot(tok[:, cols], ghid[...], 0, 0).astype(BF16)

    gt_pair.combine()
    tiles(DP // 256, weight_grad_in)
    gi_own = pltpu.make_async_copy(gi.at[my_d], gi_ref.at[:, my_f], local.at[6])
    gi_own.start()
    gi_sib = l.copy(gi.at[its_d], gi_ref.at[:, my_f], sib)
    gt_pair.across()
    gt_pair.finish(put_final(1))
    gt_own = pltpu.make_async_copy(final.at[1], gt_ref, local.at[7])
    gt_own.start()

    go_sib.wait_recv()
    gi_sib.wait_recv()
    for c in (go_own, out_own, gi_own, gt_own):
        c.wait()
    for c in l.started:
        c.wait_send()


def local(tokens, weight_in, weight_out, cotangent):
    any_space = pl.BlockSpec(memory_space=pl.ANY)
    shape = jax.ShapeDtypeStruct
    vmem = pltpu.VMEM
    return pl.pallas_call(
        kernel,
        out_shape=(
            shape((BLK, DC), BF16),
            shape((BLK, DC), BF16),
            shape((DC, 2 * FH), BF16),
            shape((2 * FH, DC), BF16),
        ),
        in_specs=[any_space] * 4,
        out_specs=(any_space,) * 4,
        scratch_shapes=[
            vmem((TOK, DP), BF16), vmem((TOK, DP), BF16), vmem((DP, FH), BF16), vmem((FH, DP), BF16),
            vmem((TOK, FH), F32), vmem((TOK, FH), F32), vmem((TOK, FH), BF16), vmem((TOK, FH), BF16),
            vmem((10, BLK, FA), BF16), vmem((10, BLK, FA), BF16),
            vmem((5, BLK, FB), BF16), vmem((5, BLK, FB), BF16),
            vmem((10, BLK // 2, FB), BF16), vmem((10, BLK // 2, FB), BF16),
            vmem((BLK, FH), F32), vmem((BLK, FH), F32), vmem((TOK, FH), BF16), vmem((TOK, FH), BF16),
            vmem((2, TOK, DC), BF16), vmem((2, TOK, DC), BF16), vmem((2, TOK, DC), BF16),
            vmem((2, 10, BLK, DC), BF16),
            vmem((DP, FH), BF16), vmem((FH, DP), BF16), vmem((2, BLK, DC), BF16),
            pltpu.SemaphoreType.DMA((COPIES,)), pltpu.SemaphoreType.DMA((COPIES,)),
            pltpu.SemaphoreType.DMA((8,)),
        ],
        compiler_params=pltpu.CompilerParams(
            collective_id=0, has_side_effects=True, vmem_limit_bytes=60 * 1024 * 1024
        ),
        cost_estimate=pl.CostEstimate(flops=14_500_000_000, bytes_accessed=12_000_000, transcendentals=400_000),
    )(tokens, weight_in, weight_out, cotangent)


def solution(mesh):
    placed = (P("row", "col"), P("col", "row"), P("row", "col"), P("row", "col"))
    return jax.shard_map(
        local,
        mesh=mesh,
        in_specs=placed,
        out_specs=(P("row", "col"), P("row", "col"), P("col", "row"), P("row", "col")),
        check_vma=False,
    )
```

```python
import functools

import jax
import jax.numpy as jnp
from jax import lax
from jax.experimental import pallas as pl
from jax.experimental.pallas import tpu as pltpu
from jax.sharding import PartitionSpec as P

F32 = jnp.float32
BF16 = jnp.bfloat16

TOK = 1024
BLK = 128
DC = 384
DP = 2 * DC
FH = 1536
FA = 896
FB = FH - FA

COPIES = 128
C_GELU = 0.7978845608028654
C_CUBE = 0.044715


def row_loop(rows, chunk, body):
    def step(i, carry):
        body(pl.multiple_of(i * chunk, chunk))
        return carry

    lax.fori_loop(0, rows // chunk, step, 0)


def tiles(count, body):
    def step(i, carry):
        body(i)
        return carry

    lax.fori_loop(0, count, step, 0)


class Links:
    def __init__(self, send, recv):
        self.send, self.recv, self.used, self.started = send, recv, 0, []
        row, col = lax.axis_index("row"), lax.axis_index("col")
        self.x, self.yh = row // 2, row % 2
        self.yl, self.z, self.k = col // 8, (col // 2) % 4, col % 2

    def device(self, **moved):
        at = {n: moved.get(n, getattr(self, n)) for n in ("x", "yh", "yl", "z", "k")}
        return (at["x"] * 2 + at["yh"], at["yl"] * 8 + at["z"] * 2 + at["k"])

    def ring(self, axis, step):
        return self.device(**{axis: lax.rem(getattr(self, axis) + step + 4, 4)})

    def other(self, axis):
        return self.device(**{axis: 1 - getattr(self, axis)})

    def copy(self, src, dst, device):
        i = self.used
        self.used += 1
        c = pltpu.make_async_remote_copy(
            src_ref=src,
            dst_ref=dst,
            send_sem=self.send.at[i],
            recv_sem=self.recv.at[i],
            device_id=device,
            device_id_type=pl.DeviceIdType.MESH,
        )
        c.start()
        self.started.append(c)
        return c

    def place(self, axis, step):
        return lax.rem(getattr(self, axis) + step + 4, 4)


def rows_of(place, member, count=BLK, skip=0):
    return pl.ds(pl.multiple_of(place * (2 * BLK) + member * BLK + skip, 16), count)


class GatherRingLast:
    def __init__(self, links, ring, pair, buf, cols):
        self.l, self.ring, self.pair, self.buf, self.cols = links, ring, pair, buf, cols
        self.me, self.mine = getattr(links, ring), getattr(links, pair)

    def at(self, step, member):
        return self.buf.at[rows_of(self.l.place(self.ring, step), member), self.cols]

    def send(self, ref, device):
        return self.l.copy(ref, ref, device)

    def start(self):
        own = self.at(0, self.mine)
        self.y = self.send(own, self.l.other(self.pair))
        self.own_p = self.send(own, self.l.ring(self.ring, 1))
        self.own_m = self.send(own, self.l.ring(self.ring, -1))

    def second(self):
        self.y.wait_recv()
        theirs = self.at(0, 1 - self.mine)
        self.oth_p = self.send(theirs, self.l.ring(self.ring, 1))
        self.oth_m = self.send(theirs, self.l.ring(self.ring, -1))

    def third(self):
        self.own_p.wait_recv()
        self.far_p = self.send(self.at(-1, self.mine), self.l.ring(self.ring, 1))
        self.own_m.wait_recv()
        self.oth_m.wait_recv()
        self.far_m = self.send(self.at(1, 1 - self.mine), self.l.ring(self.ring, -1))
        self.oth_p.wait_recv()

    def finish(self):
        self.far_p.wait_recv()
        self.far_m.wait_recv()


class GatherRingFirst:
    def __init__(self, links, ring, pair, buf, cols):
        self.l, self.ring, self.pair, self.buf, self.cols = links, ring, pair, buf, cols
        self.mine = getattr(links, pair)

    def at(self, step, count=BLK, skip=0):
        return self.buf.at[rows_of(self.l.place(self.ring, step), self.mine, count, skip), self.cols]

    def send(self, ref, device):
        return self.l.copy(ref, ref, device)

    def across(self, ref):
        return self.send(ref, self.l.other(self.pair))

    def start(self):
        own = self.at(0)
        self.own_p = self.send(own, self.l.ring(self.ring, 1))
        self.own_m = self.send(own, self.l.ring(self.ring, -1))
        self.y0 = self.across(own)

    def second(self):
        self.own_p.wait_recv()
        self.far_p = self.send(self.at(-1, BLK // 2), self.l.ring(self.ring, 1))
        self.yp = self.across(self.at(-1))
        self.own_m.wait_recv()
        self.far_m = self.send(self.at(1, BLK // 2, BLK // 2), self.l.ring(self.ring, -1))
        self.ym = self.across(self.at(1))

    def third(self):
        self.far_p.wait_recv()
        self.yfp = self.across(self.at(2, BLK // 2))
        self.far_m.wait_recv()
        self.yfm = self.across(self.at(2, BLK // 2, BLK // 2))

    def near(self):
        for c in (self.y0, self.yp, self.ym):
            c.wait_recv()

    def finish(self):
        self.yfp.wait_recv()
        self.yfm.wait_recv()


class ReduceRingFirst:
    def __init__(self, links, ring, pair, part, out, col, out_col, width, slots):
        self.l, self.ring, self.pair = links, ring, pair
        self.part, self.out, self.col, self.width, self.slots = part, out, col, width, slots
        self.out_cols = pl.ds(out_col, width)
        self.mine = getattr(links, pair)

    def rows(self, step, member):
        return rows_of(self.l.place(self.ring, step), member)

    def block(self, step, member):
        return self.out.at[self.rows(step, member), self.out_cols]

    def sent(self, step):
        l = self.l
        if step == 2:
            self.p2 = l.copy(self.block(2, 0), self.slots.at[0], l.ring(self.ring, 1))
            self.m2 = l.copy(self.block(2, 1), self.slots.at[1], l.ring(self.ring, -1))
        elif step == 1:
            self.p1 = l.copy(self.block(1, 1), self.slots.at[2], l.ring(self.ring, 1))
        elif step == 3:
            self.m1 = l.copy(self.block(-1, 0), self.slots.at[3], l.ring(self.ring, -1))

    def add(self, dst, rows_start, *slots):
        def body(r):
            total = self.part[pl.ds(rows_start + r, 32), pl.ds(self.col, self.width)]
            for s in slots:
                total = total + self.slots[s, pl.ds(r, 32), :].astype(F32)
            dst(r, total)

        row_loop(BLK, 32, body)

    def start_of(self, step, member):
        return pl.multiple_of(self.l.place(self.ring, step) * (2 * BLK) + member * BLK, BLK)

    def to_slot(self, slot):
        def put(r, total):
            self.slots[slot, pl.ds(r, 32), :] = total.astype(BF16)

        return put

    def combine(self):
        l = self.l
        self.p2.wait_recv()
        self.add(self.to_slot(7), self.start_of(1, 0), 0)
        self.pc = l.copy(self.slots.at[7], self.slots.at[4], l.ring(self.ring, 1))
        self.m2.wait_recv()
        self.add(self.to_slot(8), self.start_of(-1, 1), 1)
        self.mc = l.copy(self.slots.at[8], self.slots.at[5], l.ring(self.ring, -1))

    def across(self):
        for c in (self.p1, self.m1, self.pc, self.mc):
            c.wait_recv()
        for member, slots in ((0, (4, 3)), (1, (2, 5))):
            start = self.start_of(0, member)

            def put(r, total, start=start):
                self.part[pl.ds(start + r, 32), pl.ds(self.col, self.width)] = total

            self.add(put, start, *slots)
        self.add(self.to_slot(9), self.start_of(0, 1 - self.mine))
        self.y = self.l.copy(self.slots.at[9], self.slots.at[6], self.l.other(self.pair))

    def finish(self, put):
        self.y.wait_recv()
        self.add(put, self.start_of(0, self.mine), 6)


class ReducePairFirst:
    def __init__(self, links, ring, pair, part, out, col, width, slots, halves):
        self.l, self.ring, self.pair = links, ring, pair
        self.part, self.out, self.col, self.width = part, out, col, width
        self.slots, self.halves = slots, halves
        self.mine = getattr(links, pair)
        self.y = {}

    def sent(self, step):
        rows = rows_of(self.l.place(self.ring, step), 1 - self.mine)
        block = self.out.at[rows, pl.ds(self.col, self.width)]
        self.y[step] = self.l.copy(block, self.slots.at[step], self.l.other(self.pair))

    def add(self, dst, step, skip, count, *halves):
        start = pl.multiple_of(self.l.place(self.ring, step) * (2 * BLK) + self.mine * BLK + skip, 64)

        def body(r):
            total = self.part[pl.ds(start + r, 32), pl.ds(self.col, self.width)]
            total = total + self.slots[step, pl.ds(skip + r, 32), :].astype(F32)
            for h in halves:
                total = total + self.halves[h, pl.ds(r, 32), :].astype(F32)
            dst(r, total)

        row_loop(count, 32, body)

    def to_half(self, half):
        def put(r, total):
            self.halves[half, pl.ds(r, 32), :] = total.astype(BF16)

        return put

    def ring_copy(self, src, dst, step):
        return self.l.copy(src, self.halves.at[dst], self.l.ring(self.ring, step))

    def pairs(self):
        half = BLK // 2
        self.y[2].wait_recv()

        def put(r, total):
            self.slots[4, pl.ds(r, 32), :] = total.astype(BF16)

        self.add(put, 2, 0, BLK)
        self.p2 = self.ring_copy(self.slots.at[4, pl.ds(0, half)], 0, 1)
        self.m2 = self.ring_copy(self.slots.at[4, pl.ds(half, half)], 1, -1)
        self.y[1].wait_recv()
        self.add(self.to_half(6), 1, half, half)
        self.p1 = self.ring_copy(self.halves.at[6], 2, 1)
        self.y[3].wait_recv()
        self.add(self.to_half(7), 3, 0, half)
        self.m1 = self.ring_copy(self.halves.at[7], 3, -1)

    def combine(self):
        half = BLK // 2
        self.p2.wait_recv()
        self.add(self.to_half(8), 1, 0, half, 0)
        self.pc = self.ring_copy(self.halves.at[8], 4, 1)
        self.m2.wait_recv()
        self.add(self.to_half(9), 3, half, half, 1)
        self.mc = self.ring_copy(self.halves.at[9], 5, -1)

    def finish(self, put):
        half = BLK // 2
        for c in (self.y[0], self.p1, self.m1, self.pc, self.mc):
            c.wait_recv()
        self.add(put, 0, 0, half, 4, 3)
        self.add(lambda r, total: put(half + r, total), 0, half, half, 2, 5)


def dot(a, b, left, right):
    return lax.dot_general(a, b, (((left,), (right,)), ((), ())), preferred_element_type=F32)


def kernel(
    tok_in, wi_in, wo_in, cot_in,
    out_ref, gt_ref, gi_ref, go_ref,
    tok, cot, wi, wo,
    part_h, part_g, send_h, send_g,
    ra_h, ra_g, rb_h, rb_g, rh_h, rh_g,
    hid, gacts, acts, ghid,
    sib_out, sib_in, rbuf, rd,
    gi, go, final,
    send, recv, local,
):
    l = Links(send, recv)
    k = l.k
    sib = l.other("k")

    barrier = pltpu.get_barrier_semaphore()
    near = [sib, l.other("yl"), l.other("yh")]
    near += [l.ring(a, s) for a in ("z", "x") for s in (1, -1)]
    for d in near:
        pl.semaphore_signal(barrier, inc=1, device_id=d, device_id_type=pl.DeviceIdType.MESH)

    my_d = pl.ds(pl.multiple_of(k * DC, 128), DC)
    its_d = pl.ds(pl.multiple_of((1 - k) * DC, 128), DC)
    my_f = pl.ds(pl.multiple_of(k * FH, 128), FH)
    its_f = pl.ds(pl.multiple_of((1 - k) * FH, 128), FH)
    own_rows = rows_of(l.x, l.yh)

    loads = [
        pltpu.make_async_copy(tok_in, tok.at[own_rows, my_d], local.at[0]),
        pltpu.make_async_copy(cot_in, cot.at[own_rows, my_d], local.at[1]),
        pltpu.make_async_copy(wi_in.at[:, my_f], wi.at[my_d], local.at[2]),
        pltpu.make_async_copy(wo_in.at[my_f], wo.at[:, my_d], local.at[3]),
    ]
    for c in loads:
        c.start()
    pl.semaphore_wait(barrier, len(near))

    gather_tok = GatherRingLast(l, "x", "yh", tok, my_d)
    gather_cot = GatherRingLast(l, "x", "yh", cot, my_d)
    loads[0].wait()
    gather_tok.start()
    wi_copy = l.copy(wi_in.at[:, its_f], wi.at[my_d], sib)
    loads[1].wait()

    def share(buf, step):
        ref = buf.at[pl.ds(pl.multiple_of(l.place("x", step) * (2 * BLK), 2 * BLK), 2 * BLK), my_d]
        return l.copy(ref, ref, sib)

    shared_tok, shared_cot = [], []
    gather_tok.second()
    shared_tok.append(share(tok, 0))
    gather_tok.third()
    shared_tok += [share(tok, 1), share(tok, -1)]
    gather_cot.start()
    wo_copy = l.copy(wo_in.at[its_f], wo.at[:, my_d], sib)
    gather_tok.finish()
    shared_tok.append(share(tok, 2))
    for c in shared_tok:
        c.wait_recv()
    loads[2].wait()
    wi_copy.wait_recv()

    ring = [
        ReduceRingFirst(l, "z", "yl", part, out, 0, 0, FA, slots)
        for part, out, slots in ((part_h, send_h, ra_h), (part_g, send_g, ra_g))
    ]
    pair = [
        ReducePairFirst(l, "z", "yl", part, out, FA, FB, slots, halves)
        for part, out, slots, halves in ((part_h, send_h, rb_h, rh_h), (part_g, send_g, rb_g, rh_g))
    ]

    def pair_rows(axis, step):
        return pl.ds(pl.multiple_of(l.place(axis, step) * (2 * BLK), 2 * BLK), 2 * BLK)

    def partial_hidden(step):
        rows = pair_rows("z", step)

        def tile(n):
            cols = pl.ds(pl.multiple_of(n * 512, 512), 512)
            total = dot(tok[rows, :], wi[:, cols], 1, 0)
            part_h[rows, cols] = total
            send_h[rows, cols] = total.astype(BF16)

        tiles(FH // 512, tile)
        ring[0].sent(step)
        pair[0].sent(step)

    def partial_grad(step):
        rows = pair_rows("z", step)

        def tile(n):
            cols = pl.ds(pl.multiple_of(n * 512, 512), 512)
            total = dot(cot[rows, :], wo[cols, :], 1, 1)
            part_g[rows, cols] = total
            send_g[rows, cols] = total.astype(BF16)

        tiles(FH // 512, tile)
        ring[1].sent(step)
        pair[1].sent(step)

    partial_hidden(2)
    gather_cot.second()
    shared_cot.append(share(cot, 0))
    for step in (1, 3, 0):
        partial_hidden(step)
    gather_cot.third()
    shared_cot += [share(cot, 1), share(cot, -1)]
    gather_cot.finish()
    shared_cot.append(share(cot, 2))

    ring[0].combine()
    pair[0].pairs()
    for c in shared_cot:
        c.wait_recv()
    loads[3].wait()
    wo_copy.wait_recv()
    partial_grad(2)
    pair[0].combine()
    ring[0].across()
    for step in (1, 3, 0):
        partial_grad(step)

    def put_into(buf, col, width):
        def put(r, total):
            buf[pl.ds(r, 32), pl.ds(col, width)] = total

        return put

    own = pl.multiple_of(l.z * (2 * BLK) + l.yl * BLK, BLK)
    ring[0].finish(put_into(hid, 0, FA))
    pair[0].finish(put_into(hid, FA, FB))

    def activate(r):
        h = hid[pl.ds(r, 16), :]
        t = jnp.tanh(C_GELU * (h + C_CUBE * (h * h * h)))
        acts[pl.ds(own + r, 16), :] = (0.5 * h * (1.0 + t)).astype(BF16)

    row_loop(BLK, 16, activate)
    acts_a = GatherRingLast(l, "z", "yl", acts, pl.ds(0, FA))
    acts_b = GatherRingFirst(l, "z", "yl", acts, pl.ds(FA, FB))
    acts_a.start()
    acts_b.start()

    ring[1].combine()
    pair[1].pairs()
    acts_a.second()
    pair[1].combine()
    ring[1].across()
    acts_b.second()
    acts_a.third()
    acts_b.third()
    ring[1].finish(put_into(gacts, 0, FA))
    pair[1].finish(put_into(gacts, FA, FB))

    def pull(r):
        h = hid[pl.ds(r, 16), :]
        square = h * h
        t = jnp.tanh(C_GELU * (h + C_CUBE * (square * h)))
        slope = 0.5 * (1.0 + t) + (0.5 * C_GELU) * h * (1.0 - t * t) * (1.0 + 3.0 * C_CUBE * square)
        ghid[pl.ds(own + r, 16), :] = (gacts[pl.ds(r, 16), :] * slope).astype(BF16)

    row_loop(BLK, 16, pull)
    ghid_a = GatherRingLast(l, "z", "yl", ghid, pl.ds(0, FA))
    ghid_b = GatherRingFirst(l, "z", "yl", ghid, pl.ds(FA, FB))
    ghid_a.start()
    ghid_b.start()

    acts_b.near()
    acts_a.finish()
    acts_b.finish()

    out_pair = ReduceRingFirst(l, "x", "yh", part_h, rbuf.at[0], DP, 0, DC, rd.at[0])
    gt_pair = ReduceRingFirst(l, "x", "yh", part_g, rbuf.at[1], DP, 0, DC, rd.at[1])

    def project(which, part, lhs, weight, right, axis, step):
        rows = pair_rows(axis, step)
        part[rows, pl.ds(0, DP)] = dot(lhs[rows, :], weight[...], 1, right)
        start = pl.multiple_of(l.place(axis, step) * (2 * BLK), 2 * BLK)

        def cast(r):
            sib_out[which, pl.ds(start + r, 32), :] = part[pl.ds(start + r, 32), its_d].astype(BF16)

        row_loop(2 * BLK, 32, cast)
        return l.copy(sib_out.at[which, rows], sib_in.at[which, rows], sib)

    def merge(which, part, copy, step):
        copy.wait_recv()
        start = pl.multiple_of(l.place("x", step) * (2 * BLK), 2 * BLK)

        def body(r):
            at = pl.ds(start + r, 32)
            total = part[at, my_d] + sib_in[which, at, :].astype(F32)
            part[at, pl.ds(DP, DC)] = total
            rbuf[which, at, :] = total.astype(BF16)

        row_loop(2 * BLK, 32, body)

    steps = (2, 1, 3, 0)
    sent_out = [project(0, part_h, acts, wo, 0, "x", s) for s in steps[:2]]
    ghid_a.second()
    ghid_b.second()
    sent_out += [project(0, part_h, acts, wo, 0, "x", s) for s in steps[2:]]
    for s, c in zip(steps, sent_out):
        merge(0, part_h, c, s)
        out_pair.sent(s)
    ghid_a.third()
    ghid_b.third()

    def weight_grad_out(m):
        cols = pl.ds(pl.multiple_of(m * 256, 256), 256)
        go[cols, :] = dot(acts[:, cols], cot[...], 0, 0).astype(BF16)

    tiles(FH // 256, weight_grad_out)
    go_own = pltpu.make_async_copy(go.at[:, my_d], go_ref.at[my_f], local.at[4])
    go_own.start()
    go_sib = l.copy(go.at[:, its_d], go_ref.at[my_f], sib)

    out_pair.combine()
    out_pair.across()

    ghid_b.near()
    ghid_a.finish()
    ghid_b.finish()
    sent_gt = [project(1, part_g, ghid, wi, 1, "x", s) for s in steps]
    for s, c in zip(steps, sent_gt):
        merge(1, part_g, c, s)
        gt_pair.sent(s)

    def put_final(which):
        def put(r, total):
            final[which, pl.ds(r, 32), :] = total.astype(BF16)

        return put

    out_pair.finish(put_final(0))
    out_own = pltpu.make_async_copy(final.at[0], out_ref, local.at[5])
    out_own.start()

    def weight_grad_in(m):
        cols = pl.ds(pl.multiple_of(m * 256, 256), 256)
        gi[cols, :] = dot(tok[:, cols], ghid[...], 0, 0).astype(BF16)

    gt_pair.combine()
    tiles(DP // 256, weight_grad_in)
    gi_own = pltpu.make_async_copy(gi.at[my_d], gi_ref.at[:, my_f], local.at[6])
    gi_own.start()
    gi_sib = l.copy(gi.at[its_d], gi_ref.at[:, my_f], sib)
    gt_pair.across()
    gt_pair.finish(put_final(1))
    gt_own = pltpu.make_async_copy(final.at[1], gt_ref, local.at[7])
    gt_own.start()

    go_sib.wait_recv()
    gi_sib.wait_recv()
    for c in (go_own, out_own, gi_own, gt_own):
        c.wait()
    for c in l.started:
        c.wait_send()


def hand_over(*refs):
    sems = refs[-1]
    copies = []
    for src, dst in zip(refs[:4], refs[4:8]):
        parts = 4 if src.shape[0] > BLK else 1
        rows = src.shape[0] // parts
        for p in range(parts):
            at = pl.ds(p * rows, rows)
            copies.append(pltpu.make_async_copy(src.at[at], dst.at[at], sems.at[len(copies)]))
    for c in copies:
        c.start()
    for c in copies:
        c.wait()


def local(tokens, weight_in, weight_out, cotangent):
    results = block(tokens, weight_in, weight_out, cotangent)
    any_space = pl.BlockSpec(memory_space=pl.ANY)
    return pl.pallas_call(
        hand_over,
        out_shape=tuple(jax.ShapeDtypeStruct(r.shape, r.dtype) for r in results),
        in_specs=[any_space] * 4,
        out_specs=(any_space,) * 4,
        scratch_shapes=[pltpu.SemaphoreType.DMA((10,))],
        compiler_params=pltpu.CompilerParams(vmem_limit_bytes=60 * 1024 * 1024),
    )(*results)


def block(tokens, weight_in, weight_out, cotangent):
    any_space = pl.BlockSpec(memory_space=pl.ANY)
    shape = jax.ShapeDtypeStruct
    vmem = pltpu.VMEM
    return pl.pallas_call(
        kernel,
        out_shape=(
            shape((BLK, DC), BF16),
            shape((BLK, DC), BF16),
            shape((DC, 2 * FH), BF16),
            shape((2 * FH, DC), BF16),
        ),
        in_specs=[any_space] * 4,
        out_specs=(any_space,) * 4,
        scratch_shapes=[
            vmem((TOK, DP), BF16), vmem((TOK, DP), BF16), vmem((DP, FH), BF16), vmem((FH, DP), BF16),
            vmem((TOK, FH), F32), vmem((TOK, FH), F32), vmem((TOK, FH), BF16), vmem((TOK, FH), BF16),
            vmem((10, BLK, FA), BF16), vmem((10, BLK, FA), BF16),
            vmem((5, BLK, FB), BF16), vmem((5, BLK, FB), BF16),
            vmem((10, BLK // 2, FB), BF16), vmem((10, BLK // 2, FB), BF16),
            vmem((BLK, FH), F32), vmem((BLK, FH), F32), vmem((TOK, FH), BF16), vmem((TOK, FH), BF16),
            vmem((2, TOK, DC), BF16), vmem((2, TOK, DC), BF16), vmem((2, TOK, DC), BF16),
            vmem((2, 10, BLK, DC), BF16),
            vmem((DP, FH), BF16), vmem((FH, DP), BF16), vmem((2, BLK, DC), BF16),
            pltpu.SemaphoreType.DMA((COPIES,)), pltpu.SemaphoreType.DMA((COPIES,)),
            pltpu.SemaphoreType.DMA((8,)),
        ],
        compiler_params=pltpu.CompilerParams(
            collective_id=0, has_side_effects=True, vmem_limit_bytes=60 * 1024 * 1024
        ),
        cost_estimate=pl.CostEstimate(flops=14_500_000_000, bytes_accessed=12_000_000, transcendentals=400_000),
    )(tokens, weight_in, weight_out, cotangent)


def solution(mesh):
    placed = (P("row", "col"), P("col", "row"), P("row", "col"), P("row", "col"))
    return jax.shard_map(
        local,
        mesh=mesh,
        in_specs=placed,
        out_specs=(P("row", "col"), P("row", "col"), P("col", "row"), P("row", "col")),
        check_vma=False,
    )
```

```python
import functools

import jax
import jax.numpy as jnp
from jax import lax
from jax.experimental import pallas as pl
from jax.experimental.pallas import tpu as pltpu
from jax.sharding import PartitionSpec as P

F32 = jnp.float32
BF16 = jnp.bfloat16

TOK = 1024
BLK = 128
DC = 384
DP = 2 * DC
FH = 1536
FA = 896
FB = FH - FA

COPIES = 128
C_GELU = 0.7978845608028654
C_CUBE = 0.044715


def row_loop(rows, chunk, body):
    def step(i, carry):
        body(pl.multiple_of(i * chunk, chunk))
        return carry

    lax.fori_loop(0, rows // chunk, step, 0)


def tiles(count, body):
    def step(i, carry):
        body(i)
        return carry

    lax.fori_loop(0, count, step, 0)


class Links:
    def __init__(self, send, recv):
        self.send, self.recv, self.used = send, recv, 0
        self.started, self.taken = [], []
        row, col = lax.axis_index("row"), lax.axis_index("col")
        self.x, self.yh = row // 2, row % 2
        self.yl, self.z, self.k = col // 8, (col // 2) % 4, col % 2

    def device(self, **moved):
        at = {n: moved.get(n, getattr(self, n)) for n in ("x", "yh", "yl", "z", "k")}
        return (at["x"] * 2 + at["yh"], at["yl"] * 8 + at["z"] * 2 + at["k"])

    def ring(self, axis, step):
        return self.device(**{axis: lax.rem(getattr(self, axis) + step + 4, 4)})

    def other(self, axis):
        return self.device(**{axis: 1 - getattr(self, axis)})

    def copy(self, src, dst, device):
        i = self.used
        self.used += 1
        c = pltpu.make_async_remote_copy(
            src_ref=src,
            dst_ref=dst,
            send_sem=self.send.at[i],
            recv_sem=self.recv.at[i],
            device_id=device,
            device_id_type=pl.DeviceIdType.MESH,
        )
        c.start()
        self.started.append(c)
        return c

    def take(self, c):
        if all(c is not d for d in self.taken):
            c.wait_recv()
            self.taken.append(c)

    def place(self, axis, step):
        return lax.rem(getattr(self, axis) + step + 4, 4)


def rows_of(place, member, count=BLK, skip=0):
    return pl.ds(pl.multiple_of(place * (2 * BLK) + member * BLK + skip, 16), count)


class GatherRingLast:
    def __init__(self, links, ring, pair, buf, cols):
        self.l, self.ring, self.pair, self.buf, self.cols = links, ring, pair, buf, cols
        self.mine = getattr(links, pair)

    def at(self, step, member):
        return self.buf.at[rows_of(self.l.place(self.ring, step), member), self.cols]

    def send(self, ref, step):
        to = self.l.ring(self.ring, step) if step else self.l.other(self.pair)
        return self.l.copy(ref, ref, to)

    def start(self):
        own = self.at(0, self.mine)
        self.y = self.send(own, 0)
        self.own_p = self.send(own, 1)
        self.own_m = self.send(own, -1)

    def second(self):
        theirs = self.at(0, 1 - self.mine)
        self.oth_p = self.send(theirs, 1)
        self.oth_m = self.send(theirs, -1)

    def onward_p(self):
        self.far_p = self.send(self.at(-1, self.mine), 1)

    def onward_m(self):
        self.far_m = self.send(self.at(1, 1 - self.mine), -1)

    def arrived(self, step):
        if step == 0:
            return [self.y]
        if step == 2:
            return [self.far_p, self.far_m]
        return [self.own_p, self.oth_p] if step == -1 else [self.own_m, self.oth_m]

    def tasks(self, t, name, after):
        t.add(name + "0", after, lambda: [], self.start)
        t.add(name + "1", [name + "0"], lambda: [self.y], self.second)
        t.add(name + "p", [name + "0"], lambda: [self.own_p], self.onward_p)
        t.add(name + "m", [name + "1"], lambda: [self.oth_m], self.onward_m)


class GatherRingFirst:
    def __init__(self, links, ring, pair, buf, cols):
        self.l, self.ring, self.pair, self.buf, self.cols = links, ring, pair, buf, cols
        self.mine = getattr(links, pair)

    def at(self, step, count=BLK, skip=0):
        return self.buf.at[rows_of(self.l.place(self.ring, step), self.mine, count, skip), self.cols]

    def send(self, ref, step):
        to = self.l.ring(self.ring, step) if step else self.l.other(self.pair)
        return self.l.copy(ref, ref, to)

    def start(self):
        own = self.at(0)
        self.own_p = self.send(own, 1)
        self.own_m = self.send(own, -1)
        self.y0 = self.send(own, 0)

    def onward_p(self):
        self.far_p = self.send(self.at(-1, BLK // 2), 1)
        self.yp = self.send(self.at(-1), 0)

    def onward_m(self):
        self.far_m = self.send(self.at(1, BLK // 2, BLK // 2), -1)
        self.ym = self.send(self.at(1), 0)

    def across_p(self):
        self.yfp = self.send(self.at(2, BLK // 2), 0)

    def across_m(self):
        self.yfm = self.send(self.at(2, BLK // 2, BLK // 2), 0)

    def arrived(self, step):
        if step == 0:
            return [self.y0]
        if step == 2:
            return [self.yfp, self.yfm]
        return [self.yp] if step == -1 else [self.ym]

    def tasks(self, t, name, after):
        t.add(name + "0", after, lambda: [], self.start)
        t.add(name + "p", [name + "0"], lambda: [self.own_p], self.onward_p)
        t.add(name + "m", [name + "0"], lambda: [self.own_m], self.onward_m)
        t.add(name + "yp", [name + "p"], lambda: [self.far_p], self.across_p)
        t.add(name + "ym", [name + "m"], lambda: [self.far_m], self.across_m)


class ReduceRingFirst:
    def __init__(self, links, ring, pair, part, out, col, out_col, width, slots):
        self.l, self.ring, self.pair = links, ring, pair
        self.part, self.out, self.col, self.width, self.slots = part, out, col, width, slots
        self.out_cols = pl.ds(out_col, width)
        self.mine = getattr(links, pair)

    def block(self, step, member):
        return self.out.at[rows_of(self.l.place(self.ring, step), member), self.out_cols]

    def sent(self, step):
        l = self.l
        if step == 2:
            self.p2 = l.copy(self.block(2, 0), self.slots.at[0], l.ring(self.ring, 1))
            self.m2 = l.copy(self.block(2, 1), self.slots.at[1], l.ring(self.ring, -1))
        elif step == 1:
            self.p1 = l.copy(self.block(1, 1), self.slots.at[2], l.ring(self.ring, 1))
        elif step == -1:
            self.m1 = l.copy(self.block(-1, 0), self.slots.at[3], l.ring(self.ring, -1))

    def add(self, dst, start, *slots):
        def body(r):
            total = self.part[pl.ds(start + r, 32), pl.ds(self.col, self.width)]
            for s in slots:
                total = total + self.slots[s, pl.ds(r, 32), :].astype(F32)
            dst(r, total)

        row_loop(BLK, 32, body)

    def start_of(self, step, member):
        return pl.multiple_of(self.l.place(self.ring, step) * (2 * BLK) + member * BLK, BLK)

    def to_slot(self, slot):
        def put(r, total):
            self.slots[slot, pl.ds(r, 32), :] = total.astype(BF16)

        return put

    def combine_p(self):
        self.add(self.to_slot(7), self.start_of(1, 0), 0)
        self.pc = self.l.copy(self.slots.at[7], self.slots.at[4], self.l.ring(self.ring, 1))

    def combine_m(self):
        self.add(self.to_slot(8), self.start_of(-1, 1), 1)
        self.mc = self.l.copy(self.slots.at[8], self.slots.at[5], self.l.ring(self.ring, -1))

    def across(self):
        for member, slots in ((0, (4, 3)), (1, (2, 5))):
            start = self.start_of(0, member)

            def put(r, total, start=start):
                self.part[pl.ds(start + r, 32), pl.ds(self.col, self.width)] = total

            self.add(put, start, *slots)
        self.add(self.to_slot(9), self.start_of(0, 1 - self.mine))
        self.y = self.l.copy(self.slots.at[9], self.slots.at[6], self.l.other(self.pair))

    def tasks(self, t, name, put, after, first, last, final):
        t.add(name + "p", [after(1), first], lambda: [self.p2], self.combine_p)
        t.add(name + "m", [after(-1), first], lambda: [self.m2], self.combine_m)
        t.add(
            name + "y", [last, name + "p", name + "m"],
            lambda: [self.p1, self.m1, self.pc, self.mc], self.across,
        )
        t.add(
            name + "f", [name + "y"] + final, lambda: [self.y],
            lambda: self.add(put, self.start_of(0, self.mine), 6),
        )


class ReducePairFirst:
    def __init__(self, links, ring, pair, part, out, col, width, slots, halves):
        self.l, self.ring, self.pair = links, ring, pair
        self.part, self.out, self.col, self.width = part, out, col, width
        self.slots, self.halves = slots, halves
        self.mine = getattr(links, pair)
        self.y = {}

    def sent(self, step):
        rows = rows_of(self.l.place(self.ring, step), 1 - self.mine)
        block = self.out.at[rows, pl.ds(self.col, self.width)]
        self.y[step] = self.l.copy(block, self.slots.at[step % 4], self.l.other(self.pair))

    def add(self, dst, step, skip, count, *halves):
        start = pl.multiple_of(self.l.place(self.ring, step) * (2 * BLK) + self.mine * BLK + skip, 64)

        def body(r):
            total = self.part[pl.ds(start + r, 32), pl.ds(self.col, self.width)]
            total = total + self.slots[step % 4, pl.ds(skip + r, 32), :].astype(F32)
            for h in halves:
                total = total + self.halves[h, pl.ds(r, 32), :].astype(F32)
            dst(r, total)

        row_loop(count, 32, body)

    def to_half(self, half):
        def put(r, total):
            self.halves[half, pl.ds(r, 32), :] = total.astype(BF16)

        return put

    def ring_copy(self, src, dst, step):
        return self.l.copy(src, self.halves.at[dst], self.l.ring(self.ring, step))

    def far(self):
        def put(r, total):
            self.slots[4, pl.ds(r, 32), :] = total.astype(BF16)

        self.add(put, 2, 0, BLK)
        self.p2 = self.ring_copy(self.slots.at[4, pl.ds(0, BLK // 2)], 0, 1)
        self.m2 = self.ring_copy(self.slots.at[4, pl.ds(BLK // 2, BLK // 2)], 1, -1)

    def near_p(self):
        self.add(self.to_half(6), 1, BLK // 2, BLK // 2)
        self.p1 = self.ring_copy(self.halves.at[6], 2, 1)

    def near_m(self):
        self.add(self.to_half(7), -1, 0, BLK // 2)
        self.m1 = self.ring_copy(self.halves.at[7], 3, -1)

    def combine_p(self):
        self.add(self.to_half(8), 1, 0, BLK // 2, 0)
        self.pc = self.ring_copy(self.halves.at[8], 4, 1)

    def combine_m(self):
        self.add(self.to_half(9), -1, BLK // 2, BLK // 2, 1)
        self.mc = self.ring_copy(self.halves.at[9], 5, -1)

    def finish(self, put):
        half = BLK // 2
        self.add(put, 0, 0, half, 4, 3)
        self.add(lambda r, total: put(half + r, total), 0, half, half, 2, 5)

    def tasks(self, t, name, put, after, final):
        t.add(name + "2", [after(2)], lambda: [self.y[2]], self.far)
        t.add(name + "1", [after(1)], lambda: [self.y[1]], self.near_p)
        t.add(name + "3", [after(-1)], lambda: [self.y[-1]], self.near_m)
        t.add(name + "p", [name + "2", name + "1"], lambda: [self.p2], self.combine_p)
        t.add(name + "m", [name + "2", name + "3"], lambda: [self.m2], self.combine_m)
        t.add(
            name + "f", [after(0), name + "p", name + "m"] + final,
            lambda: [self.y[0], self.p1, self.m1, self.pc, self.mc],
            lambda: self.finish(put),
        )


class Tasks:
    def __init__(self, links):
        self.l, self.all = links, {}

    def add(self, name, after, waits, do):
        self.all[name] = (after, waits, do)

    def step(self, name):
        _, waits, do = self.all[name]
        for c in waits():
            self.l.take(c)
        do()


ORDER = (
    "t0", "t1", "tp", "ts0", "tm", "ts1", "ts-1", "c0", "ts2", "hpart2", "hpart1", "hpart-1", "hpart0", "c1",
    "cp", "cs0", "cm", "cs1", "cs-1", "ham", "cs2", "hap", "hb2", "gpart2", "gpart1", "gpart-1", "hb1",
    "gpart0", "hb3", "hbp", "hbm", "hbf", "hB0", "gb2", "hay", "gb1", "gb3", "gam", "gap", "gbp", "gbm",
    "haf", "hA0", "hBp", "hBm", "gbf", "gB0", "hA1", "ox0", "om0", "hByp", "hBym", "gay", "hAp", "gBp", "gBm",
    "hAm", "ox1", "gBym", "ox-1", "gByp", "om1", "om-1", "ox2", "go0", "go1", "om2", "or", "go2", "go3",
    "go4", "go5", "gaf", "gA0", "go", "odp", "odm", "ody", "gAp", "gA1", "ix0", "odf", "o", "im0", "gAm",
    "ix1", "im1", "ix-1", "ix2", "im-1", "gi0", "im2", "ir", "gi1", "gi", "gj0", "gj1", "gj", "idp", "idm",
    "idy", "idf", "i",
)


def run_tasks(t):
    done = set()
    for name in ORDER:
        assert done.issuperset(t.all[name][0]), name
        t.step(name)
        done.add(name)
    assert len(done) == len(t.all)


def dot(a, b, left, right):
    return lax.dot_general(a, b, (((left,), (right,)), ((), ())), preferred_element_type=F32)


STEPS = (2, 1, -1, 0)


def kernel(
    tok_in, wi_in, wo_in, cot_in,
    out_ref, gt_ref, gi_ref, go_ref,
    tok, cot, wi, wo,
    part_h, part_g, send_h, send_g,
    ra_h, ra_g, rb_h, rb_g, rh_h, rh_g,
    hid, acts, ghid,
    sib_in, rbuf, rd,
    gi, go, final,
    send, recv, local,
):
    l = Links(send, recv)
    t = Tasks(l)
    k = l.k
    sib = l.other("k")

    barrier = pltpu.get_barrier_semaphore()
    near = [sib, l.other("yl"), l.other("yh")]
    near += [l.ring(a, s) for a in ("z", "x") for s in (1, -1)]
    for d in near:
        pl.semaphore_signal(barrier, inc=1, device_id=d, device_id_type=pl.DeviceIdType.MESH)

    my_d = pl.ds(pl.multiple_of(k * DC, 128), DC)
    its_d = pl.ds(pl.multiple_of((1 - k) * DC, 128), DC)
    my_f = pl.ds(pl.multiple_of(k * FH, 128), FH)
    its_f = pl.ds(pl.multiple_of((1 - k) * FH, 128), FH)
    own_rows = rows_of(l.x, l.yh)

    load_tok = pltpu.make_async_copy(tok_in, tok.at[own_rows, my_d], local.at[0])
    load_cot = pltpu.make_async_copy(cot_in, cot.at[own_rows, my_d], local.at[1])
    load_wi = pltpu.make_async_copy(wi_in.at[:, my_f], wi.at[my_d], local.at[2])
    load_wo = pltpu.make_async_copy(wo_in.at[my_f], wo.at[:, my_d], local.at[3])
    for c in (load_tok, load_wi, load_cot, load_wo):
        c.start()
    pl.semaphore_wait(barrier, len(near))

    def pair_rows(axis, step):
        return pl.ds(pl.multiple_of(l.place(axis, step) * (2 * BLK), 2 * BLK), 2 * BLK)

    shared = {}

    def gather_tokens(name, buf, load, weight, target, after):
        g = GatherRingLast(l, "x", "yh", buf, my_d)

        def start():
            load.wait()
            g.start()
            shared[name + "w"] = l.copy(weight, target, sib)

        g.tasks(t, name, after)
        t.add(name + "0", after, lambda: [], start)

        def share(step):
            def do():
                ref = buf.at[pair_rows("x", step), my_d]
                shared[name + str(step)] = l.copy(ref, ref, sib)

            return do

        for step, before in ((0, ["1"]), (1, ["1"]), (-1, ["1"]), (2, ["p", "m"])):
            t.add(
                name + "s" + str(step), [name + b for b in before],
                lambda step=step: g.arrived(step), share(step),
            )

    gather_tokens("t", tok, load_tok, wi_in.at[:, its_f], wi.at[my_d], [])
    gather_tokens("c", cot, load_cot, wo_in.at[its_f], wo.at[:, my_d], ["ts1", "ts-1"])

    def put_hidden(col, width):
        cols = pl.ds(col, width)

        def put(r, h):
            hid[pl.ds(r, 32), cols] = h
            tanh = jnp.tanh(C_GELU * (h + C_CUBE * (h * h * h)))
            acts[pl.ds(own + r, 32), cols] = (0.5 * h * (1.0 + tanh)).astype(BF16)

        return put

    def put_grad(col, width):
        cols = pl.ds(col, width)

        def put(r, total):
            h = hid[pl.ds(r, 32), cols]
            square = h * h
            tanh = jnp.tanh(C_GELU * (h + C_CUBE * (square * h)))
            slope = 0.5 * (1.0 + tanh)
            slope += (0.5 * C_GELU) * h * (1.0 - tanh * tanh) * (1.0 + 3.0 * C_CUBE * square)
            ghid[pl.ds(own + r, 32), cols] = (total * slope).astype(BF16)

        return put

    own = pl.multiple_of(l.z * (2 * BLK) + l.yl * BLK, BLK)

    def reduction(name, source, load, product, part, out, slots_a, slots_b, halves, put, gathered, final):
        ring = ReduceRingFirst(l, "z", "yl", part, out, 0, 0, FA, slots_a)
        pair = ReducePairFirst(l, "z", "yl", part, out, FA, FB, slots_b, halves)

        def partial(step):
            def do():
                if step == STEPS[0]:
                    load.wait()
                rows = pair_rows("z", step)

                def tile(n):
                    cols = pl.ds(pl.multiple_of(n * 512, 512), 512)
                    total = product(rows, cols)
                    part[rows, cols] = total
                    out[rows, cols] = total.astype(BF16)

                tiles(FH // 512, tile)
                pair.sent(step)
                ring.sent(step)

            return do

        def part_of(step):
            return name + "part" + str(step)

        shares = [source + "s" + str(s) for s in STEPS]
        for i, step in enumerate(STEPS):
            t.add(
                part_of(step), shares if i == 0 else [part_of(STEPS[i - 1])],
                lambda: [shared[source + "w"]] + [shared[source + str(s)] for s in STEPS], partial(step),
            )
        ring.tasks(t, name + "a", put(0, FA), part_of, part_of(2), part_of(0), [f + "af" for f in final])
        pair.tasks(t, name + "b", put(FA, FB), part_of, [f + "bf" for f in final])
        a = GatherRingLast(l, "z", "yl", gathered, pl.ds(0, FA))
        b = GatherRingFirst(l, "z", "yl", gathered, pl.ds(FA, FB))
        a.tasks(t, name + "A", [name + "af"])
        b.tasks(t, name + "B", [name + "bf"])
        return a, b

    gathers_h = reduction(
        "h", "t", load_wi, lambda rows, cols: dot(tok[rows, :], wi[:, cols], 1, 0),
        part_h, send_h, ra_h, rb_h, rh_h, put_hidden, acts, [],
    )
    gathers_g = reduction(
        "g", "c", load_wo, lambda rows, cols: dot(cot[rows, :], wo[cols, :], 1, 1),
        part_g, send_g, ra_g, rb_g, rh_g, put_grad, ghid, ["h"],
    )

    merged = {}

    def projection(name, which, before, gathers, part, lhs, weight, right, target):
        final_sum = ReduceRingFirst(l, "x", "yh", part, rbuf.at[which], DP, 0, DC, rd.at[which])

        def project(step):
            def do():
                rows = pair_rows("z", step)
                part[rows, pl.ds(0, DP)] = dot(lhs[rows, :], weight[...], 1, right)
                merged[name + str(step)] = l.copy(part.at[rows, its_d], sib_in.at[which, rows], sib)

            return do

        def merge(step):
            def do():
                start = pl.multiple_of(l.place("z", step) * (2 * BLK), 2 * BLK)

                def body(r):
                    at = pl.ds(start + r, 32)
                    total = part[at, my_d] + sib_in[which, at, :]
                    part[at, pl.ds(DP, DC)] = total
                    rbuf[which, at, :] = total.astype(BF16)

                row_loop(2 * BLK, 32, body)

            return do

        for step, need in ((0, ["A1", "B0"]), (1, ["A1", "Bm"]), (-1, ["A1", "Bp"]), (2, ["Ap", "Am", "Byp", "Bym"])):
            t.add(
                name + "x" + str(step), [before + n for n in need] + [before + "af", before + "bf"],
                lambda step=step: gathers[0].arrived(step) + gathers[1].arrived(step), project(step),
            )
            t.add(
                name + "m" + str(step), [name + "x" + str(step)],
                lambda step=step: [merged[name + str(step)]], merge(step),
            )

        def go_round():
            for step in STEPS:
                final_sum.sent(step)

        merges = [name + "m" + str(s) for s in STEPS]
        t.add(name + "r", merges, lambda: [], go_round)

        def put(r, total):
            final[which, pl.ds(r, 32), :] = total.astype(BF16)

        final_sum.tasks(t, name + "d", put, lambda s: name + "r", name + "r", name + "r", [])
        return pltpu.make_async_copy(final.at[which], target, local.at[4 + which])

    out_done = projection("o", 0, "h", gathers_h, part_h, acts, wo, 0, out_ref)
    gt_done = projection("i", 1, "g", gathers_g, part_g, ghid, wi, 1, gt_ref)
    t.add("o", ["odf"], lambda: [], out_done.start)
    t.add("i", ["idf"], lambda: [], gt_done.start)

    whole_h = ["ox" + str(s) for s in STEPS] + ["cs" + str(s) for s in STEPS]
    whole_g = ["ix" + str(s) for s in STEPS]
    go_tile = 256

    def grad_out_tile(m):
        def do():
            cols = pl.ds(m * go_tile, go_tile)
            go[cols, :] = dot(acts[:, cols], cot[...], 0, 0).astype(BF16)

        return do

    go_tiles = ["go" + str(m) for m in range(FH // go_tile)]
    for m, name in enumerate(go_tiles):
        t.add(name, whole_h + ["gpart2"], lambda: [], grad_out_tile(m))
    go_done = pltpu.make_async_copy(go.at[:, my_d], go_ref.at[my_f], local.at[6])
    gi_done = pltpu.make_async_copy(gi.at[my_d], gi_ref.at[:, my_f], local.at[7])
    ends = []

    def send_go():
        go_done.start()
        ends.append(l.copy(go.at[:, its_d], go_ref.at[my_f], sib))

    t.add("go", go_tiles, lambda: [], send_go)

    def grad_in_tile(which, n):
        def do():
            cols = pl.ds(n * DP, DP)
            gi[which, cols] = dot(tok[:, which], ghid[:, cols], 0, 0).astype(BF16)

        return do

    for n in range(2):
        t.add("gi" + str(n), whole_g, lambda: [], grad_in_tile(its_d, n))
        t.add("gj" + str(n), whole_g, lambda: [], grad_in_tile(my_d, n))
    t.add("gi", ["gi0", "gi1"], lambda: [], lambda: ends.append(l.copy(gi.at[its_d], gi_ref.at[:, my_f], sib)))
    t.add("gj", ["gj0", "gj1"], lambda: [], gi_done.start)

    run_tasks(t)

    for c in ends:
        l.take(c)
    for c in (go_done, gi_done, out_done, gt_done):
        c.wait()
    for c in l.started:
        c.wait_send()


def hand_over(*refs):
    results, targets, held, (arrive, leave) = refs[:4], refs[4:8], refs[8:12], refs[12:]
    ins, outs = [], []
    for src, dst, mid in zip(results, targets, held):
        parts = 4 if src.shape[0] > BLK else 1
        rows = src.shape[0] // parts
        for p in range(parts):
            at, i = pl.ds(p * rows, rows), len(ins)
            ins.append(pltpu.make_async_copy(src.at[at], mid.at[at], arrive.at[i]))
            outs.append(pltpu.make_async_copy(mid.at[at], dst.at[at], leave.at[i]))
    for c in ins:
        c.start()
    for c, d in zip(ins, outs):
        c.wait()
        d.start()
    for d in outs:
        d.wait()


def local(tokens, weight_in, weight_out, cotangent):
    results = block(tokens, weight_in, weight_out, cotangent)
    any_space = pl.BlockSpec(memory_space=pl.ANY)
    return pl.pallas_call(
        hand_over,
        out_shape=tuple(jax.ShapeDtypeStruct(r.shape, r.dtype) for r in results),
        in_specs=[any_space] * 4,
        out_specs=(any_space,) * 4,
        scratch_shapes=[pltpu.VMEM(r.shape, r.dtype) for r in results] + [pltpu.SemaphoreType.DMA((10,))] * 2,
        compiler_params=pltpu.CompilerParams(vmem_limit_bytes=60 * 1024 * 1024),
    )(*results)


def block(tokens, weight_in, weight_out, cotangent):
    any_space = pl.BlockSpec(memory_space=pl.ANY)
    shape = jax.ShapeDtypeStruct
    vmem = pltpu.VMEM
    return pl.pallas_call(
        kernel,
        out_shape=(
            shape((BLK, DC), BF16),
            shape((BLK, DC), BF16),
            shape((DC, 2 * FH), BF16),
            shape((2 * FH, DC), BF16),
        ),
        in_specs=[any_space] * 4,
        out_specs=(any_space,) * 4,
        scratch_shapes=[
            vmem((TOK, DP), BF16), vmem((TOK, DP), BF16), vmem((DP, FH), BF16), vmem((FH, DP), BF16),
            vmem((TOK, FH), F32), vmem((TOK, FH), F32), vmem((TOK, FH), BF16), vmem((TOK, FH), BF16),
            vmem((10, BLK, FA), BF16), vmem((10, BLK, FA), BF16),
            vmem((5, BLK, FB), BF16), vmem((5, BLK, FB), BF16),
            vmem((10, BLK // 2, FB), BF16), vmem((10, BLK // 2, FB), BF16),
            vmem((BLK, FH), F32), vmem((TOK, FH), BF16), vmem((TOK, FH), BF16),
            vmem((2, TOK, DC), F32), vmem((2, TOK, DC), BF16),
            vmem((2, 10, BLK, DC), BF16),
            vmem((DP, FH), BF16), vmem((FH, DP), BF16), vmem((2, BLK, DC), BF16),
            pltpu.SemaphoreType.DMA((COPIES,)), pltpu.SemaphoreType.DMA((COPIES,)),
            pltpu.SemaphoreType.DMA((8,)),
        ],
        compiler_params=pltpu.CompilerParams(
            collective_id=0, has_side_effects=True, vmem_limit_bytes=60 * 1024 * 1024
        ),
        cost_estimate=pl.CostEstimate(flops=14_500_000_000, bytes_accessed=12_000_000, transcendentals=400_000),
    )(tokens, weight_in, weight_out, cotangent)


def solution(mesh):
    placed = (P("row", "col"), P("col", "row"), P("row", "col"), P("row", "col"))
    return jax.shard_map(
        local,
        mesh=mesh,
        in_specs=placed,
        out_specs=(P("row", "col"), P("row", "col"), P("col", "row"), P("row", "col")),
        check_vma=False,
    )
```

```python
import functools

import jax
import jax.numpy as jnp
from jax import lax
from jax.experimental import pallas as pl
from jax.experimental.pallas import tpu as pltpu
from jax.sharding import PartitionSpec as P

F32 = jnp.float32
BF16 = jnp.bfloat16

TOK = 1024
BLK = 128
DC = 384
DP = 2 * DC
FH = 1536
FA = 896
FB = FH - FA

COPIES = 128
ROWS = 16
C_GELU = 0.7978845608028654
C_CUBE = 0.044715


def row_loop(rows, chunk, body):
    def step(i, carry):
        body(pl.multiple_of(i * chunk, chunk))
        return carry

    lax.fori_loop(0, rows // chunk, step, 0)


def tiles(count, body):
    def step(i, carry):
        body(i)
        return carry

    lax.fori_loop(0, count, step, 0)


class Links:
    def __init__(self, send, recv):
        self.send, self.recv, self.used = send, recv, 0
        self.started, self.taken = [], []
        row, col = lax.axis_index("row"), lax.axis_index("col")
        self.x, self.yh = row // 2, row % 2
        self.yl, self.z, self.k = col // 8, (col // 2) % 4, col % 2

    def device(self, **moved):
        at = {n: moved.get(n, getattr(self, n)) for n in ("x", "yh", "yl", "z", "k")}
        return (at["x"] * 2 + at["yh"], at["yl"] * 8 + at["z"] * 2 + at["k"])

    def ring(self, axis, step):
        return self.device(**{axis: lax.rem(getattr(self, axis) + step + 4, 4)})

    def other(self, axis):
        return self.device(**{axis: 1 - getattr(self, axis)})

    def copy(self, src, dst, device):
        i = self.used
        self.used += 1
        c = pltpu.make_async_remote_copy(
            src_ref=src,
            dst_ref=dst,
            send_sem=self.send.at[i],
            recv_sem=self.recv.at[i],
            device_id=device,
            device_id_type=pl.DeviceIdType.MESH,
        )
        c.start()
        self.started.append(c)
        return c

    def take(self, c):
        if all(c is not d for d in self.taken):
            c.wait_recv()
            self.taken.append(c)

    def place(self, axis, step):
        return lax.rem(getattr(self, axis) + step + 4, 4)


def rows_of(place, member, count=BLK, skip=0):
    return pl.ds(pl.multiple_of(place * (2 * BLK) + member * BLK + skip, 16), count)


class GatherRingLast:
    def __init__(self, links, ring, pair, buf, cols):
        self.l, self.ring, self.pair, self.buf, self.cols = links, ring, pair, buf, cols
        self.mine = getattr(links, pair)

    def at(self, step, member):
        return self.buf.at[rows_of(self.l.place(self.ring, step), member), self.cols]

    def send(self, ref, step):
        to = self.l.ring(self.ring, step) if step else self.l.other(self.pair)
        return self.l.copy(ref, ref, to)

    def start(self):
        own = self.at(0, self.mine)
        self.y = self.send(own, 0)
        self.own_p = self.send(own, 1)
        self.own_m = self.send(own, -1)

    def second(self):
        theirs = self.at(0, 1 - self.mine)
        self.oth_p = self.send(theirs, 1)
        self.oth_m = self.send(theirs, -1)

    def onward_p(self):
        self.far_p = self.send(self.at(-1, self.mine), 1)

    def onward_m(self):
        self.far_m = self.send(self.at(1, 1 - self.mine), -1)

    def arrived(self, step):
        if step == 0:
            return [self.y]
        if step == 2:
            return [self.far_p, self.far_m]
        return [self.own_p, self.oth_p] if step == -1 else [self.own_m, self.oth_m]

    def tasks(self, t, name, after):
        t.add(name + "0", after, lambda: [], self.start)
        t.add(name + "1", [name + "0"], lambda: [self.y], self.second)
        t.add(name + "p", [name + "0"], lambda: [self.own_p], self.onward_p)
        t.add(name + "m", [name + "1"], lambda: [self.oth_m], self.onward_m)


class GatherRingFirst:
    def __init__(self, links, ring, pair, buf, cols):
        self.l, self.ring, self.pair, self.buf, self.cols = links, ring, pair, buf, cols
        self.mine = getattr(links, pair)

    def at(self, step, count=BLK, skip=0):
        return self.buf.at[rows_of(self.l.place(self.ring, step), self.mine, count, skip), self.cols]

    def send(self, ref, step):
        to = self.l.ring(self.ring, step) if step else self.l.other(self.pair)
        return self.l.copy(ref, ref, to)

    def start(self):
        own = self.at(0)
        self.own_p = self.send(own, 1)
        self.own_m = self.send(own, -1)
        self.y0 = self.send(own, 0)

    def onward_p(self):
        self.far_p = self.send(self.at(-1, BLK // 2), 1)
        self.yp = self.send(self.at(-1), 0)

    def onward_m(self):
        self.far_m = self.send(self.at(1, BLK // 2, BLK // 2), -1)
        self.ym = self.send(self.at(1), 0)

    def across_p(self):
        self.yfp = self.send(self.at(2, BLK // 2), 0)

    def across_m(self):
        self.yfm = self.send(self.at(2, BLK // 2, BLK // 2), 0)

    def arrived(self, step):
        if step == 0:
            return [self.y0]
        if step == 2:
            return [self.yfp, self.yfm]
        return [self.yp] if step == -1 else [self.ym]

    def tasks(self, t, name, after):
        t.add(name + "0", after, lambda: [], self.start)
        t.add(name + "p", [name + "0"], lambda: [self.own_p], self.onward_p)
        t.add(name + "m", [name + "0"], lambda: [self.own_m], self.onward_m)
        t.add(name + "yp", [name + "p"], lambda: [self.far_p], self.across_p)
        t.add(name + "ym", [name + "m"], lambda: [self.far_m], self.across_m)


class ReduceRingFirst:
    def __init__(self, links, ring, pair, part, out, col, out_col, width, slots):
        self.l, self.ring, self.pair = links, ring, pair
        self.part, self.out, self.col, self.width, self.slots = part, out, col, width, slots
        self.out_cols = pl.ds(out_col, width)
        self.mine = getattr(links, pair)

    def block(self, step, member):
        return self.out.at[rows_of(self.l.place(self.ring, step), member), self.out_cols]

    def sent(self, step):
        l = self.l
        if step == 2:
            self.p2 = l.copy(self.block(2, 0), self.slots.at[0], l.ring(self.ring, 1))
            self.m2 = l.copy(self.block(2, 1), self.slots.at[1], l.ring(self.ring, -1))
        elif step == 1:
            self.p1 = l.copy(self.block(1, 1), self.slots.at[2], l.ring(self.ring, 1))
        elif step == -1:
            self.m1 = l.copy(self.block(-1, 0), self.slots.at[3], l.ring(self.ring, -1))

    def add(self, dst, start, *slots):
        def body(r):
            total = self.part[pl.ds(start + r, ROWS), pl.ds(self.col, self.width)]
            for s in slots:
                total = total + self.slots[s, pl.ds(r, ROWS), :].astype(F32)
            dst(r, total)

        row_loop(BLK, ROWS, body)

    def start_of(self, step, member):
        return pl.multiple_of(self.l.place(self.ring, step) * (2 * BLK) + member * BLK, BLK)

    def to_slot(self, slot):
        def put(r, total):
            self.slots[slot, pl.ds(r, ROWS), :] = total.astype(BF16)

        return put

    def combine_p(self):
        self.add(self.to_slot(7), self.start_of(1, 0), 0)
        self.pc = self.l.copy(self.slots.at[7], self.slots.at[4], self.l.ring(self.ring, 1))

    def combine_m(self):
        self.add(self.to_slot(8), self.start_of(-1, 1), 1)
        self.mc = self.l.copy(self.slots.at[8], self.slots.at[5], self.l.ring(self.ring, -1))

    def across(self):
        for member, slots in ((0, (4, 3)), (1, (2, 5))):
            start = self.start_of(0, member)

            def put(r, total, start=start):
                self.part[pl.ds(start + r, ROWS), pl.ds(self.col, self.width)] = total

            self.add(put, start, *slots)
        self.add(self.to_slot(9), self.start_of(0, 1 - self.mine))
        self.y = self.l.copy(self.slots.at[9], self.slots.at[6], self.l.other(self.pair))

    def tasks(self, t, name, put, after, first, last, final):
        t.add(name + "p", [after(1), first], lambda: [self.p2], self.combine_p)
        t.add(name + "m", [after(-1), first], lambda: [self.m2], self.combine_m)
        t.add(
            name + "y", [last, name + "p", name + "m"],
            lambda: [self.p1, self.m1, self.pc, self.mc], self.across,
        )
        t.add(
            name + "f", [name + "y"] + final, lambda: [self.y],
            lambda: self.add(put, self.start_of(0, self.mine), 6),
        )


class ReducePairFirst:
    def __init__(self, links, ring, pair, part, out, col, width, slots, halves):
        self.l, self.ring, self.pair = links, ring, pair
        self.part, self.out, self.col, self.width = part, out, col, width
        self.slots, self.halves = slots, halves
        self.mine = getattr(links, pair)
        self.y = {}

    def sent(self, step):
        rows = rows_of(self.l.place(self.ring, step), 1 - self.mine)
        block = self.out.at[rows, pl.ds(self.col, self.width)]
        self.y[step] = self.l.copy(block, self.slots.at[step % 4], self.l.other(self.pair))

    def add(self, dst, step, skip, count, *halves):
        start = pl.multiple_of(self.l.place(self.ring, step) * (2 * BLK) + self.mine * BLK + skip, 64)

        def body(r):
            total = self.part[pl.ds(start + r, ROWS), pl.ds(self.col, self.width)]
            total = total + self.slots[step % 4, pl.ds(skip + r, ROWS), :].astype(F32)
            for h in halves:
                total = total + self.halves[h, pl.ds(r, ROWS), :].astype(F32)
            dst(r, total)

        row_loop(count, ROWS, body)

    def to_half(self, half):
        def put(r, total):
            self.halves[half, pl.ds(r, ROWS), :] = total.astype(BF16)

        return put

    def ring_copy(self, src, dst, step):
        return self.l.copy(src, self.halves.at[dst], self.l.ring(self.ring, step))

    def far(self):
        def put(r, total):
            self.slots[4, pl.ds(r, ROWS), :] = total.astype(BF16)

        self.add(put, 2, 0, BLK)
        self.p2 = self.ring_copy(self.slots.at[4, pl.ds(0, BLK // 2)], 0, 1)
        self.m2 = self.ring_copy(self.slots.at[4, pl.ds(BLK // 2, BLK // 2)], 1, -1)

    def near_p(self):
        self.add(self.to_half(6), 1, BLK // 2, BLK // 2)
        self.p1 = self.ring_copy(self.halves.at[6], 2, 1)

    def near_m(self):
        self.add(self.to_half(7), -1, 0, BLK // 2)
        self.m1 = self.ring_copy(self.halves.at[7], 3, -1)

    def combine_p(self):
        self.add(self.to_half(8), 1, 0, BLK // 2, 0)
        self.pc = self.ring_copy(self.halves.at[8], 4, 1)

    def combine_m(self):
        self.add(self.to_half(9), -1, BLK // 2, BLK // 2, 1)
        self.mc = self.ring_copy(self.halves.at[9], 5, -1)

    def finish(self, put):
        half = BLK // 2
        self.add(put, 0, 0, half, 4, 3)
        self.add(lambda r, total: put(half + r, total), 0, half, half, 2, 5)

    def tasks(self, t, name, put, after, final):
        t.add(name + "2", [after(2)], lambda: [self.y[2]], self.far)
        t.add(name + "1", [after(1)], lambda: [self.y[1]], self.near_p)
        t.add(name + "3", [after(-1)], lambda: [self.y[-1]], self.near_m)
        t.add(name + "p", [name + "2", name + "1"], lambda: [self.p2], self.combine_p)
        t.add(name + "m", [name + "2", name + "3"], lambda: [self.m2], self.combine_m)
        t.add(
            name + "f", [after(0), name + "p", name + "m"] + final,
            lambda: [self.y[0], self.p1, self.m1, self.pc, self.mc],
            lambda: self.finish(put),
        )


class Tasks:
    def __init__(self, links):
        self.l, self.all = links, {}

    def add(self, name, after, waits, do):
        self.all[name] = (after, waits, do)

    def step(self, name):
        _, waits, do = self.all[name]
        for c in waits():
            self.l.take(c)
        do()


ORDER = (
    "t0", "t1", "tp", "ts0", "tm", "ts1", "ts-1", "c0", "ts2", "hpart2", "hpart1", "hpart-1", "hpart0", "c1",
    "cp", "cs0", "turn", "cm", "cs1", "cs-1", "ham", "cs2", "hap", "hb2", "gpart2", "gpart1", "gpart-1",
    "hb1", "gpart0", "hb3", "hbp", "hbm", "hbf", "hB0", "gb2", "gb1", "hay", "gb3", "gam", "gap", "gbm",
    "gbp", "haf", "hA0", "hBp", "hBm", "gbf", "gB0", "hA1", "ox0", "om0", "hByp", "hBym", "gay", "hAp", "gBm",
    "gBp", "hAm", "ox1", "gBym", "ox-1", "gByp", "om1", "om-1", "ox2", "go0", "om2", "or", "go1", "gaf",
    "gA0", "go", "odp", "odm", "ody", "gA1", "gAp", "ix0", "odf", "im0", "o", "gAm", "ix1", "im1", "ix-1",
    "ix2", "gi0", "im-1", "im2", "ir", "gi", "gj0", "gj", "idp", "idm", "idy", "idf", "i",
)


def run_tasks(t):
    done = set()
    for name in ORDER:
        assert done.issuperset(t.all[name][0]), name
        t.step(name)
        done.add(name)
    assert len(done) == len(t.all)


def dot(a, b, left, right):
    return lax.dot_general(a, b, (((left,), (right,)), ((), ())), preferred_element_type=F32)


STEPS = (2, 1, -1, 0)


def kernel(
    tok_in, wi_in, wo_in, cot_in,
    out_ref, gt_ref, gi_ref, go_ref,
    tok, cot, wi, wo,
    part_h, part_g, send_h, send_g,
    ra_h, ra_g, rb_h, rb_g, rh_h, rh_g,
    hid, acts, ghid,
    sib_in, rbuf, rd,
    gi, go, final, turned,
    send, recv, local,
):
    l = Links(send, recv)
    t = Tasks(l)
    k = l.k
    sib = l.other("k")

    barrier = pltpu.get_barrier_semaphore()
    near = [sib, l.other("yl"), l.other("yh")]
    near += [l.ring(a, s) for a in ("z", "x") for s in (1, -1)]
    for d in near:
        pl.semaphore_signal(barrier, inc=1, device_id=d, device_id_type=pl.DeviceIdType.MESH)

    my_d = pl.ds(pl.multiple_of(k * DC, 128), DC)
    its_d = pl.ds(pl.multiple_of((1 - k) * DC, 128), DC)
    my_f = pl.ds(pl.multiple_of(k * FH, 128), FH)
    its_f = pl.ds(pl.multiple_of((1 - k) * FH, 128), FH)
    own_rows = rows_of(l.x, l.yh)

    load_tok = pltpu.make_async_copy(tok_in, tok.at[own_rows, my_d], local.at[0])
    load_cot = pltpu.make_async_copy(cot_in, cot.at[own_rows, my_d], local.at[1])
    load_wi = pltpu.make_async_copy(wi_in.at[:, my_f], wi.at[my_d], local.at[2])
    load_wo = pltpu.make_async_copy(wo_in.at[my_f], wo.at[:, my_d], local.at[3])
    for c in (load_tok, load_wi, load_cot, load_wo):
        c.start()
    pl.semaphore_wait(barrier, len(near))

    def pair_rows(axis, step):
        return pl.ds(pl.multiple_of(l.place(axis, step) * (2 * BLK), 2 * BLK), 2 * BLK)

    shared = {}

    def gather_tokens(name, buf, load, weight, target, after):
        g = GatherRingLast(l, "x", "yh", buf, my_d)

        def start():
            load.wait()
            g.start()
            shared[name + "w"] = l.copy(weight, target, sib)

        g.tasks(t, name, after)
        t.add(name + "0", after, lambda: [], start)

        def share(step):
            def do():
                ref = buf.at[pair_rows("x", step), my_d]
                shared[name + str(step)] = l.copy(ref, ref, sib)

            return do

        for step, before in ((0, ["1"]), (1, ["1"]), (-1, ["1"]), (2, ["p", "m"])):
            t.add(
                name + "s" + str(step), [name + b for b in before],
                lambda step=step: g.arrived(step), share(step),
            )

    gather_tokens("t", tok, load_tok, wi_in.at[:, its_f], wi.at[my_d], [])
    gather_tokens("c", cot, load_cot, wo_in.at[its_f], wo.at[:, my_d], ["ts1", "ts-1"])

    def put_hidden(col, width):
        cols = pl.ds(col, width)

        def put(r, h):
            hid[pl.ds(r, ROWS), cols] = h
            tanh = jnp.tanh(C_GELU * (h + C_CUBE * (h * h * h)))
            acts[pl.ds(own + r, ROWS), cols] = (0.5 * h * (1.0 + tanh)).astype(BF16)

        return put

    def put_grad(col, width):
        cols = pl.ds(col, width)

        def put(r, total):
            h = hid[pl.ds(r, ROWS), cols]
            square = h * h
            tanh = jnp.tanh(C_GELU * (h + C_CUBE * (square * h)))
            slope = 0.5 * (1.0 + tanh)
            slope += (0.5 * C_GELU) * h * (1.0 - tanh * tanh) * (1.0 + 3.0 * C_CUBE * square)
            ghid[pl.ds(own + r, ROWS), cols] = (total * slope).astype(BF16)

        return put

    own = pl.multiple_of(l.z * (2 * BLK) + l.yl * BLK, BLK)

    def reduction(name, source, load, product, part, out, slots_a, slots_b, halves, put, gathered, final):
        ring = ReduceRingFirst(l, "z", "yl", part, out, 0, 0, FA, slots_a)
        pair = ReducePairFirst(l, "z", "yl", part, out, FA, FB, slots_b, halves)

        def partial(step):
            def do():
                if step == STEPS[0]:
                    load.wait()
                rows = pair_rows("z", step)

                def tile(n):
                    cols = pl.ds(pl.multiple_of(n * 256, 256), 256)
                    total = product(rows, cols)
                    part[rows, cols] = total
                    out[rows, cols] = total.astype(BF16)

                tiles(FH // 256, tile)
                pair.sent(step)
                ring.sent(step)

            return do

        def part_of(step):
            return name + "part" + str(step)

        shares = [source + "s" + str(s) for s in STEPS]
        for i, step in enumerate(STEPS):
            t.add(
                part_of(step), shares if i == 0 else [part_of(STEPS[i - 1])],
                lambda: [shared[source + "w"]] + [shared[source + str(s)] for s in STEPS], partial(step),
            )
        ring.tasks(t, name + "a", put(0, FA), part_of, part_of(2), part_of(0), [f + "af" for f in final])
        pair.tasks(t, name + "b", put(FA, FB), part_of, [f + "bf" for f in final])
        a = GatherRingLast(l, "z", "yl", gathered, pl.ds(0, FA))
        b = GatherRingFirst(l, "z", "yl", gathered, pl.ds(FA, FB))
        a.tasks(t, name + "A", [name + "af"])
        b.tasks(t, name + "B", [name + "bf"])
        return a, b

    gathers_h = reduction(
        "h", "t", load_wi, lambda rows, cols: dot(tok[rows, :], wi[:, cols], 1, 0),
        part_h, send_h, ra_h, rb_h, rh_h, put_hidden, acts, [],
    )
    gathers_g = reduction(
        "g", "c", load_wo, lambda rows, cols: dot(cot[rows, :], wo[cols, :], 1, 1),
        part_g, send_g, ra_g, rb_g, rh_g, put_grad, ghid, ["h"],
    )

    merged = {}

    def projection(name, which, before, gathers, part, lhs, weight, right, target):
        final_sum = ReduceRingFirst(l, "x", "yh", part, rbuf.at[which], DP, 0, DC, rd.at[which])

        def project(step):
            def do():
                rows = pair_rows("z", step)

                def tile(n):
                    cols = pl.ds(pl.multiple_of(n * 256, 256), 256)
                    part[rows, cols] = dot(lhs[rows, :], weight[(cols, slice(None))[::2 * right - 1]], 1, right)

                tiles(DP // 256, tile)
                merged[name + str(step)] = l.copy(part.at[rows, its_d], sib_in.at[which, rows], sib)

            return do

        def merge(step):
            def do():
                start = pl.multiple_of(l.place("z", step) * (2 * BLK), 2 * BLK)

                def body(r):
                    at = pl.ds(start + r, ROWS)
                    total = part[at, my_d] + sib_in[which, at, :]
                    part[at, pl.ds(DP, DC)] = total
                    rbuf[which, at, :] = total.astype(BF16)

                row_loop(2 * BLK, ROWS, body)

            return do

        for step, need in ((0, ["A1", "B0"]), (1, ["A1", "Bm"]), (-1, ["A1", "Bp"]), (2, ["Ap", "Am", "Byp", "Bym"])):
            t.add(
                name + "x" + str(step), [before + n for n in need] + [before + "af", before + "bf"],
                lambda step=step: gathers[0].arrived(step) + gathers[1].arrived(step), project(step),
            )
            t.add(
                name + "m" + str(step), [name + "x" + str(step)],
                lambda step=step: [merged[name + str(step)]], merge(step),
            )

        def go_round():
            for step in STEPS:
                final_sum.sent(step)

        merges = [name + "m" + str(s) for s in STEPS]
        t.add(name + "r", merges, lambda: [], go_round)

        def put(r, total):
            final[which, pl.ds(r, ROWS), :] = total.astype(BF16)

        final_sum.tasks(t, name + "d", put, lambda s: name + "r", name + "r", name + "r", [])
        return pltpu.make_async_copy(final.at[which], target, local.at[4 + which])

    out_done = projection("o", 0, "h", gathers_h, part_h, acts, wo, 0, out_ref)
    gt_done = projection("i", 1, "g", gathers_g, part_g, ghid, wi, 1, gt_ref)
    t.add("o", ["odf"], lambda: [], out_done.start)
    t.add("i", ["idf"], lambda: [], gt_done.start)

    whole_h = ["ox" + str(s) for s in STEPS] + ["cs" + str(s) for s in STEPS]
    whole_g = ["ix" + str(s) for s in STEPS]

    def grad_out_tiles(half):
        def tile(n):
            cols = pl.ds(pl.multiple_of(half * (FH // 2) + n * 256, 256), 256)
            go[cols, :] = dot(acts[:, cols], cot[...], 0, 0).astype(BF16)

        return lambda: tiles(FH // 512, tile)

    for half in range(2):
        t.add("go" + str(half), whole_h + ["gpart2"], lambda: [], grad_out_tiles(half))
    go_done = pltpu.make_async_copy(go.at[:, my_d], go_ref.at[my_f], local.at[6])
    gi_done = pltpu.make_async_copy(gi.at[my_d], gi_ref.at[:, my_f], local.at[7])
    ends = []

    def send_go():
        go_done.start()
        ends.append(l.copy(go.at[:, its_d], go_ref.at[my_f], sib))

    t.add("go", ["go0", "go1"], lambda: [], send_go)

    def turn_tokens():
        def tile(n):
            cols = pl.ds(pl.multiple_of(n * 128, 128), 128)
            turned[cols, :] = tok[:, cols].T

        tiles(DP // 128, tile)

    t.add("turn", ["hpart0"], lambda: [], turn_tokens)

    def grad_in_tiles(rows):
        def tile(n):
            cols = pl.ds(pl.multiple_of(n * 256, 256), 256)
            gi[rows, cols] = dot(turned[rows, :], ghid[:, cols], 1, 0).astype(BF16)

        return lambda: tiles(FH // 256, tile)

    t.add("gi0", whole_g + ["turn"], lambda: [], grad_in_tiles(its_d))
    t.add("gj0", whole_g + ["turn"], lambda: [], grad_in_tiles(my_d))
    t.add("gi", ["gi0"], lambda: [], lambda: ends.append(l.copy(gi.at[its_d], gi_ref.at[:, my_f], sib)))
    t.add("gj", ["gj0"], lambda: [], gi_done.start)

    run_tasks(t)

    for c in ends:
        l.take(c)
    for c in (go_done, gi_done, out_done, gt_done):
        c.wait()
    for c in l.started:
        c.wait_send()


def hand_over(*refs):
    results, targets, held, (arrive, leave) = refs[:4], refs[4:8], refs[8:12], refs[12:]
    ins, outs = [], []
    for src, dst, mid in zip(results, targets, held):
        parts = 4 if src.shape[0] > BLK else 1
        rows = src.shape[0] // parts
        for p in range(parts):
            at, i = pl.ds(p * rows, rows), len(ins)
            ins.append(pltpu.make_async_copy(src.at[at], mid.at[at], arrive.at[i]))
            outs.append(pltpu.make_async_copy(mid.at[at], dst.at[at], leave.at[i]))
    for c in ins:
        c.start()
    for c, d in zip(ins, outs):
        c.wait()
        d.start()
    for d in outs:
        d.wait()


def local(tokens, weight_in, weight_out, cotangent):
    results = block(tokens, weight_in, weight_out, cotangent)
    any_space = pl.BlockSpec(memory_space=pl.ANY)
    return pl.pallas_call(
        hand_over,
        out_shape=tuple(jax.ShapeDtypeStruct(r.shape, r.dtype) for r in results),
        in_specs=[any_space] * 4,
        out_specs=(any_space,) * 4,
        scratch_shapes=[pltpu.VMEM(r.shape, r.dtype) for r in results] + [pltpu.SemaphoreType.DMA((10,))] * 2,
        compiler_params=pltpu.CompilerParams(vmem_limit_bytes=60 * 1024 * 1024),
    )(*results)


def block(tokens, weight_in, weight_out, cotangent):
    any_space = pl.BlockSpec(memory_space=pl.ANY)
    shape = jax.ShapeDtypeStruct
    vmem = pltpu.VMEM
    return pl.pallas_call(
        kernel,
        out_shape=(
            shape((BLK, DC), BF16),
            shape((BLK, DC), BF16),
            shape((DC, 2 * FH), BF16),
            shape((2 * FH, DC), BF16),
        ),
        in_specs=[any_space] * 4,
        out_specs=(any_space,) * 4,
        scratch_shapes=[
            vmem((TOK, DP), BF16), vmem((TOK, DP), BF16), vmem((DP, FH), BF16), vmem((FH, DP), BF16),
            vmem((TOK, FH), F32), vmem((TOK, FH), F32), vmem((TOK, FH), BF16), vmem((TOK, FH), BF16),
            vmem((10, BLK, FA), BF16), vmem((10, BLK, FA), BF16),
            vmem((5, BLK, FB), BF16), vmem((5, BLK, FB), BF16),
            vmem((10, BLK // 2, FB), BF16), vmem((10, BLK // 2, FB), BF16),
            vmem((BLK, FH), F32), vmem((TOK, FH), BF16), vmem((TOK, FH), BF16),
            vmem((2, TOK, DC), F32), vmem((2, TOK, DC), BF16),
            vmem((2, 10, BLK, DC), BF16),
            vmem((DP, FH), BF16), vmem((FH, DP), BF16), vmem((2, BLK, DC), BF16), vmem((DP, TOK), BF16),
            pltpu.SemaphoreType.DMA((COPIES,)), pltpu.SemaphoreType.DMA((COPIES,)),
            pltpu.SemaphoreType.DMA((8,)),
        ],
        compiler_params=pltpu.CompilerParams(
            collective_id=0, has_side_effects=True, vmem_limit_bytes=60 * 1024 * 1024
        ),
        cost_estimate=pl.CostEstimate(flops=14_500_000_000, bytes_accessed=12_000_000, transcendentals=400_000),
    )(tokens, weight_in, weight_out, cotangent)


def solution(mesh):
    placed = (P("row", "col"), P("col", "row"), P("row", "col"), P("row", "col"))
    return jax.shard_map(
        local,
        mesh=mesh,
        in_specs=placed,
        out_specs=(P("row", "col"), P("row", "col"), P("col", "row"), P("row", "col")),
        check_vma=False,
    )
```

```python
import functools

import jax
import jax.numpy as jnp
from jax import lax
from jax.experimental import pallas as pl
from jax.experimental.pallas import tpu as pltpu
from jax.sharding import PartitionSpec as P

F32 = jnp.float32
BF16 = jnp.bfloat16

TOK = 1024
BLK = 128
DC = 384
DP = 2 * DC
FH = 1536
FA = 896
FB = FH - FA

COPIES = 128
ROWS = 16
C_GELU = 0.7978845608028654
C_CUBE = 0.044715


def row_loop(rows, chunk, body):
    def step(i, carry):
        body(pl.multiple_of(i * chunk, chunk))
        return carry

    lax.fori_loop(0, rows // chunk, step, 0)


def tiles(count, body):
    def step(i, carry):
        body(i)
        return carry

    lax.fori_loop(0, count, step, 0)


class Links:
    def __init__(self, send, recv):
        self.send, self.recv, self.used = send, recv, 0
        self.started, self.taken = [], []
        row, col = lax.axis_index("row"), lax.axis_index("col")
        self.x, self.yh = row // 2, row % 2
        self.yl, self.z, self.k = col // 8, (col // 2) % 4, col % 2

    def device(self, **moved):
        at = {n: moved.get(n, getattr(self, n)) for n in ("x", "yh", "yl", "z", "k")}
        return (at["x"] * 2 + at["yh"], at["yl"] * 8 + at["z"] * 2 + at["k"])

    def ring(self, axis, step):
        return self.device(**{axis: lax.rem(getattr(self, axis) + step + 4, 4)})

    def other(self, axis):
        return self.device(**{axis: 1 - getattr(self, axis)})

    def copy(self, src, dst, device):
        i = self.used
        self.used += 1
        c = pltpu.make_async_remote_copy(
            src_ref=src,
            dst_ref=dst,
            send_sem=self.send.at[i],
            recv_sem=self.recv.at[i],
            device_id=device,
            device_id_type=pl.DeviceIdType.MESH,
        )
        c.start()
        self.started.append(c)
        return c

    def take(self, c):
        if all(c is not d for d in self.taken):
            c.wait_recv()
            self.taken.append(c)

    def place(self, axis, step):
        return lax.rem(getattr(self, axis) + step + 4, 4)


def rows_of(place, member, count=BLK, skip=0):
    return pl.ds(pl.multiple_of(place * (2 * BLK) + member * BLK + skip, 16), count)


class GatherRingLast:
    def __init__(self, links, ring, pair, buf, cols):
        self.l, self.ring, self.pair, self.buf, self.cols = links, ring, pair, buf, cols
        self.mine = getattr(links, pair)

    def at(self, step, member):
        return self.buf.at[rows_of(self.l.place(self.ring, step), member), self.cols]

    def send(self, ref, step):
        to = self.l.ring(self.ring, step) if step else self.l.other(self.pair)
        return self.l.copy(ref, ref, to)

    def start(self):
        own = self.at(0, self.mine)
        self.y = self.send(own, 0)
        self.own_p = self.send(own, 1)
        self.own_m = self.send(own, -1)

    def second(self):
        theirs = self.at(0, 1 - self.mine)
        self.oth_p = self.send(theirs, 1)
        self.oth_m = self.send(theirs, -1)

    def onward_p(self):
        self.far_p = self.send(self.at(-1, self.mine), 1)

    def onward_m(self):
        self.far_m = self.send(self.at(1, 1 - self.mine), -1)

    def arrived(self, step):
        if step == 0:
            return [self.y]
        if step == 2:
            return [self.far_p, self.far_m]
        return [self.own_p, self.oth_p] if step == -1 else [self.own_m, self.oth_m]

    def tasks(self, t, name, after):
        t.add(name + "0", after, lambda: [], self.start)
        t.add(name + "1", [name + "0"], lambda: [self.y], self.second)
        t.add(name + "p", [name + "0"], lambda: [self.own_p], self.onward_p)
        t.add(name + "m", [name + "1"], lambda: [self.oth_m], self.onward_m)


class GatherRingFirst:
    def __init__(self, links, ring, pair, buf, cols):
        self.l, self.ring, self.pair, self.buf, self.cols = links, ring, pair, buf, cols
        self.mine = getattr(links, pair)

    def at(self, step, count=BLK, skip=0):
        return self.buf.at[rows_of(self.l.place(self.ring, step), self.mine, count, skip), self.cols]

    def send(self, ref, step):
        to = self.l.ring(self.ring, step) if step else self.l.other(self.pair)
        return self.l.copy(ref, ref, to)

    def start(self):
        own = self.at(0)
        self.own_p = self.send(own, 1)
        self.own_m = self.send(own, -1)
        self.y0 = self.send(own, 0)

    def onward_p(self):
        self.far_p = self.send(self.at(-1, BLK // 2), 1)
        self.yp = self.send(self.at(-1), 0)

    def onward_m(self):
        self.far_m = self.send(self.at(1, BLK // 2, BLK // 2), -1)
        self.ym = self.send(self.at(1), 0)

    def across_p(self):
        self.yfp = self.send(self.at(2, BLK // 2), 0)

    def across_m(self):
        self.yfm = self.send(self.at(2, BLK // 2, BLK // 2), 0)

    def arrived(self, step):
        if step == 0:
            return [self.y0]
        if step == 2:
            return [self.yfp, self.yfm]
        return [self.yp] if step == -1 else [self.ym]

    def tasks(self, t, name, after):
        t.add(name + "0", after, lambda: [], self.start)
        t.add(name + "p", [name + "0"], lambda: [self.own_p], self.onward_p)
        t.add(name + "m", [name + "0"], lambda: [self.own_m], self.onward_m)
        t.add(name + "yp", [name + "p"], lambda: [self.far_p], self.across_p)
        t.add(name + "ym", [name + "m"], lambda: [self.far_m], self.across_m)


class ReduceRingFirst:
    def __init__(self, links, ring, pair, part, out, col, out_col, width, slots):
        self.l, self.ring, self.pair = links, ring, pair
        self.part, self.out, self.col, self.width, self.slots = part, out, col, width, slots
        self.out_cols = pl.ds(out_col, width)
        self.mine = getattr(links, pair)

    def block(self, step, member):
        return self.out.at[rows_of(self.l.place(self.ring, step), member), self.out_cols]

    def sent(self, step):
        l = self.l
        if step == 2:
            self.p2 = l.copy(self.block(2, 0), self.slots.at[0], l.ring(self.ring, 1))
            self.m2 = l.copy(self.block(2, 1), self.slots.at[1], l.ring(self.ring, -1))
        elif step == 1:
            self.p1 = l.copy(self.block(1, 1), self.slots.at[2], l.ring(self.ring, 1))
        elif step == -1:
            self.m1 = l.copy(self.block(-1, 0), self.slots.at[3], l.ring(self.ring, -1))

    def add(self, dst, start, *slots):
        def body(r):
            total = self.part[pl.ds(start + r, ROWS), pl.ds(self.col, self.width)]
            for s in slots:
                total = total + self.slots[s, pl.ds(r, ROWS), :].astype(F32)
            dst(r, total)

        row_loop(BLK, ROWS, body)

    def start_of(self, step, member):
        return pl.multiple_of(self.l.place(self.ring, step) * (2 * BLK) + member * BLK, BLK)

    def to_slot(self, slot):
        def put(r, total):
            self.slots[slot, pl.ds(r, ROWS), :] = total.astype(BF16)

        return put

    def combine_p(self):
        self.add(self.to_slot(7), self.start_of(1, 0), 0)
        self.pc = self.l.copy(self.slots.at[7], self.slots.at[4], self.l.ring(self.ring, 1))

    def combine_m(self):
        self.add(self.to_slot(8), self.start_of(-1, 1), 1)
        self.mc = self.l.copy(self.slots.at[8], self.slots.at[5], self.l.ring(self.ring, -1))

    def across(self):
        for member, slots in ((0, (4, 3)), (1, (2, 5))):
            start = self.start_of(0, member)

            def put(r, total, start=start):
                self.part[pl.ds(start + r, ROWS), pl.ds(self.col, self.width)] = total

            self.add(put, start, *slots)
        self.add(self.to_slot(9), self.start_of(0, 1 - self.mine))
        self.y = self.l.copy(self.slots.at[9], self.slots.at[6], self.l.other(self.pair))

    def tasks(self, t, name, put, after, first, last, final):
        t.add(name + "p", [after(1), first], lambda: [self.p2], self.combine_p)
        t.add(name + "m", [after(-1), first], lambda: [self.m2], self.combine_m)
        t.add(
            name + "y", [last, name + "p", name + "m"],
            lambda: [self.p1, self.m1, self.pc, self.mc], self.across,
        )
        t.add(
            name + "f", [name + "y"] + final, lambda: [self.y],
            lambda: self.add(put, self.start_of(0, self.mine), 6),
        )


class ReducePairFirst:
    def __init__(self, links, ring, pair, part, out, col, width, slots, halves):
        self.l, self.ring, self.pair = links, ring, pair
        self.part, self.out, self.col, self.width = part, out, col, width
        self.slots, self.halves = slots, halves
        self.mine = getattr(links, pair)
        self.y = {}

    def sent(self, step):
        rows = rows_of(self.l.place(self.ring, step), 1 - self.mine)
        block = self.out.at[rows, pl.ds(self.col, self.width)]
        self.y[step] = self.l.copy(block, self.slots.at[step % 4], self.l.other(self.pair))

    def add(self, dst, step, skip, count, *halves):
        start = pl.multiple_of(self.l.place(self.ring, step) * (2 * BLK) + self.mine * BLK + skip, 64)

        def body(r):
            total = self.part[pl.ds(start + r, ROWS), pl.ds(self.col, self.width)]
            total = total + self.slots[step % 4, pl.ds(skip + r, ROWS), :].astype(F32)
            for h in halves:
                total = total + self.halves[h, pl.ds(r, ROWS), :].astype(F32)
            dst(r, total)

        row_loop(count, ROWS, body)

    def to_half(self, half):
        def put(r, total):
            self.halves[half, pl.ds(r, ROWS), :] = total.astype(BF16)

        return put

    def ring_copy(self, src, dst, step):
        return self.l.copy(src, self.halves.at[dst], self.l.ring(self.ring, step))

    def far(self):
        def put(r, total):
            self.slots[4, pl.ds(r, ROWS), :] = total.astype(BF16)

        self.add(put, 2, 0, BLK)
        self.p2 = self.ring_copy(self.slots.at[4, pl.ds(0, BLK // 2)], 0, 1)
        self.m2 = self.ring_copy(self.slots.at[4, pl.ds(BLK // 2, BLK // 2)], 1, -1)

    def near_p(self):
        self.add(self.to_half(6), 1, BLK // 2, BLK // 2)
        self.p1 = self.ring_copy(self.halves.at[6], 2, 1)

    def near_m(self):
        self.add(self.to_half(7), -1, 0, BLK // 2)
        self.m1 = self.ring_copy(self.halves.at[7], 3, -1)

    def combine_p(self):
        self.add(self.to_half(8), 1, 0, BLK // 2, 0)
        self.pc = self.ring_copy(self.halves.at[8], 4, 1)

    def combine_m(self):
        self.add(self.to_half(9), -1, BLK // 2, BLK // 2, 1)
        self.mc = self.ring_copy(self.halves.at[9], 5, -1)

    def finish(self, put):
        half = BLK // 2
        self.add(put, 0, 0, half, 4, 3)
        self.add(lambda r, total: put(half + r, total), 0, half, half, 2, 5)

    def tasks(self, t, name, put, after, final):
        t.add(name + "2", [after(2)], lambda: [self.y[2]], self.far)
        t.add(name + "1", [after(1)], lambda: [self.y[1]], self.near_p)
        t.add(name + "3", [after(-1)], lambda: [self.y[-1]], self.near_m)
        t.add(name + "p", [name + "2", name + "1"], lambda: [self.p2], self.combine_p)
        t.add(name + "m", [name + "2", name + "3"], lambda: [self.m2], self.combine_m)
        t.add(
            name + "f", [after(0), name + "p", name + "m"] + final,
            lambda: [self.y[0], self.p1, self.m1, self.pc, self.mc],
            lambda: self.finish(put),
        )


class Tasks:
    def __init__(self, links):
        self.l, self.all = links, {}

    def add(self, name, after, waits, do):
        self.all[name] = (after, waits, do)

    def step(self, name):
        _, waits, do = self.all[name]
        for c in waits():
            self.l.take(c)
        do()


ORDER = (
    "cs", "ts", "t0", "tw", "t1", "tp", "c0", "c1", "tm", "cm", "cp", "hpart2", "cw", "hpart1", "hpart-1",
    "hpart0", "ham", "hb2", "turn", "hap", "hb1", "hbp", "hb3", "hbm", "hbf", "hay", "hB0", "gpart2",
    "gpart1", "gpart-1", "gpart0", "hBp", "hBm", "gam", "gap", "hByp", "hBym", "haf", "hA0", "gay", "gb2",
    "hAp", "gb1", "gbp", "gb3", "gbm", "gbf", "gB0", "hA1", "ox0", "gaf", "gA0", "gBp", "gBm", "gByp", "gBym",
    "hAm", "ox1", "gA1", "gAp", "ix0", "ox-1", "ox2", "gAm", "ix1", "ix-1", "or", "go0", "ix2", "ir", "gi0",
    "odp", "odm", "gi1", "go1", "gj0", "idp", "idm", "ody", "gj1", "idy", "odf", "os", "idf", "is", "o", "i",
)


def run_tasks(t):
    done = set()
    for name in ORDER:
        assert done.issuperset(t.all[name][0]), name
        t.step(name)
        done.add(name)
    assert len(done) == len(t.all)


def dot(a, b, left, right):
    return lax.dot_general(a, b, (((left,), (right,)), ((), ())), preferred_element_type=F32)


STEPS = (2, 1, -1, 0)


def kernel(
    tok_in, wi_in, wo_in, cot_in,
    out_ref, gt_ref, gi_ref, go_ref,
    tok, cot, wi, wo,
    part_h, part_g, send_h, send_g,
    ra_h, ra_g, rb_h, rb_g, rh_h, rh_g,
    hid, acts, ghid,
    summed, summed_in, rbuf, rd,
    gi, go, final, turned,
    send, recv, local,
):
    l = Links(send, recv)
    t = Tasks(l)
    k = l.k
    sib = l.other("k")

    barrier = pltpu.get_barrier_semaphore()
    near = [sib, l.other("yl"), l.other("yh")]
    near += [l.ring(a, s) for a in ("z", "x") for s in (1, -1)]
    for d in near:
        pl.semaphore_signal(barrier, inc=1, device_id=d, device_id_type=pl.DeviceIdType.MESH)

    my_d = pl.ds(pl.multiple_of(k * DC, 128), DC)
    its_d = pl.ds(pl.multiple_of((1 - k) * DC, 128), DC)
    my_f = pl.ds(pl.multiple_of(k * FH, 128), FH)
    its_f = pl.ds(pl.multiple_of((1 - k) * FH, 128), FH)
    own_rows = rows_of(l.x, l.yh)

    load_tok = pltpu.make_async_copy(tok_in, tok.at[own_rows, my_d], local.at[0])
    load_cot = pltpu.make_async_copy(cot_in, cot.at[own_rows, my_d], local.at[1])
    load_wi = pltpu.make_async_copy(wi_in.at[:, my_f], wi.at[my_d], local.at[2])
    load_wo = pltpu.make_async_copy(wo_in.at[my_f], wo.at[:, my_d], local.at[3])
    for c in (load_tok, load_wi, load_cot, load_wo):
        c.start()
    pl.semaphore_wait(barrier, len(near))

    def pair_rows(axis, step):
        return pl.ds(pl.multiple_of(l.place(axis, step) * (2 * BLK), 2 * BLK), 2 * BLK)

    def to_sibling(pairs):
        return [l.copy(src, dst, sib) for src, dst in pairs]

    shared = {}

    def gather_tokens(name, buf, load, weights, after, weights_after):
        g = GatherRingLast(l, "x", "yh", buf, pl.ds(0, DP))

        def share():
            load.wait()
            piece = buf.at[own_rows, my_d]
            shared[name] = to_sibling([(piece, piece)])

        def send_weights():
            shared[name + "w"] = to_sibling(weights)

        t.add(name + "s", [], lambda: [], share)
        g.tasks(t, name, [name + "s"] + after)
        t.add(name + "0", [name + "s"] + after, lambda: shared[name], g.start)
        t.add(name + "w", weights_after, lambda: [], send_weights)
        return g

    def split(start, count, parts):
        return [pl.ds(pl.multiple_of(start + i * (count // parts), 16), count // parts) for i in range(parts)]

    rows_in = zip(split(0, DC, 4), split(k * DC, DC, 4))
    wi_copies = [(wi_in.at[a, its_f], wi.at[b]) for a, b in rows_in]
    rows_out = zip(split((1 - k) * FH, FH, 4), split(0, FH, 4))
    wo_copies = [(wo_in.at[a], wo.at[b, my_d]) for a, b in rows_out]
    gather_t = gather_tokens("t", tok, load_tok, wi_copies, [], ["t0"])
    gather_c = gather_tokens("c", cot, load_cot, wo_copies, ["t1"], ["hpart2"])

    def put_hidden(col, width):
        cols = pl.ds(col, width)

        def put(r, h):
            hid[pl.ds(r, ROWS), cols] = h
            tanh = jnp.tanh(C_GELU * (h + C_CUBE * (h * h * h)))
            acts[pl.ds(own + r, ROWS), cols] = (0.5 * h * (1.0 + tanh)).astype(BF16)

        return put

    def put_grad(col, width):
        cols = pl.ds(col, width)

        def put(r, total):
            h = hid[pl.ds(r, ROWS), cols]
            square = h * h
            tanh = jnp.tanh(C_GELU * (h + C_CUBE * (square * h)))
            slope = 0.5 * (1.0 + tanh)
            slope += (0.5 * C_GELU) * h * (1.0 - tanh * tanh) * (1.0 + 3.0 * C_CUBE * square)
            ghid[pl.ds(own + r, ROWS), cols] = (total * slope).astype(BF16)

        return put

    own = pl.multiple_of(l.z * (2 * BLK) + l.yl * BLK, BLK)

    def reduction(name, source, tokens_of, load, product, part, out, slots_a, slots_b, halves, put, gathered, final):
        ring = ReduceRingFirst(l, "z", "yl", part, out, 0, 0, FA, slots_a)
        pair = ReducePairFirst(l, "z", "yl", part, out, FA, FB, slots_b, halves)

        def partial(step):
            def do():
                if step == STEPS[0]:
                    load.wait()
                rows = pair_rows("z", step)

                def tile(n):
                    cols = pl.ds(pl.multiple_of(n * 256, 256), 256)
                    total = product(rows, cols)
                    part[rows, cols] = total
                    out[rows, cols] = total.astype(BF16)

                tiles(FH // 256, tile)
                pair.sent(step)
                ring.sent(step)

            return do

        def part_of(step):
            return name + "part" + str(step)

        before = [source + s for s in ("s", "p", "m", "w")]
        for i, step in enumerate(STEPS):
            t.add(
                part_of(step), before if i == 0 else [part_of(STEPS[i - 1])],
                lambda: shared[source + "w"] + [c for s in STEPS for c in tokens_of.arrived(s)], partial(step),
            )
        ring.tasks(t, name + "a", put(0, FA), part_of, part_of(2), part_of(0), [f + "af" for f in final])
        pair.tasks(t, name + "b", put(FA, FB), part_of, [f + "bf" for f in final])
        a = GatherRingLast(l, "z", "yl", gathered, pl.ds(0, FA))
        b = GatherRingFirst(l, "z", "yl", gathered, pl.ds(FA, FB))
        a.tasks(t, name + "A", [name + "af"])
        b.tasks(t, name + "B", [name + "bf"])
        return a, b

    gathers_h = reduction(
        "h", "t", gather_t, load_wi, lambda rows, cols: dot(tok[rows, :], wi[:, cols], 1, 0),
        part_h, send_h, ra_h, rb_h, rh_h, put_hidden, acts, [],
    )
    gathers_g = reduction(
        "g", "c", gather_c, load_wo, lambda rows, cols: dot(cot[rows, :], wo[cols, :], 1, 1),
        part_g, send_g, ra_g, rb_g, rh_g, put_grad, ghid, ["h"],
    )

    def projection(name, which, before, gathers, part, lhs, weight, right, target):
        final_sum = ReduceRingFirst(l, "x", "yh", part, rbuf.at[which], 0, 0, DP, rd.at[which])

        def project(step):
            def do():
                rows = pair_rows("z", step)

                def tile(n):
                    cols = pl.ds(pl.multiple_of(n * 256, 256), 256)
                    total = dot(lhs[rows, :], weight[(cols, slice(None))[:: 2 * right - 1]], 1, right)
                    part[rows, cols] = total
                    rbuf[which, rows, cols] = total.astype(BF16)

                tiles(DP // 256, tile)

            return do

        for step, need in ((0, ["A1", "B0"]), (1, ["A1", "Bm"]), (-1, ["A1", "Bp"]), (2, ["Ap", "Am", "Byp", "Bym"])):
            t.add(
                name + "x" + str(step), [before + n for n in need] + [before + "af", before + "bf"],
                lambda step=step: gathers[0].arrived(step) + gathers[1].arrived(step), project(step),
            )

        def go_round():
            for step in STEPS:
                final_sum.sent(step)

        t.add(name + "r", [name + "x" + str(s) for s in STEPS], lambda: [], go_round)

        def put(r, total):
            summed[which, pl.ds(r, ROWS), :] = total

        final_sum.tasks(t, name + "d", put, lambda s: name + "r", name + "r", name + "r", [])
        done = pltpu.make_async_copy(final.at[which], target, local.at[4 + which])

        def exchange():
            shared[name] = to_sibling([(summed.at[which, :, its_d], summed_in.at[which])])

        def conclude():
            def body(r):
                at = pl.ds(r, ROWS)
                final[which, at, :] = (summed[which, at, my_d] + summed_in[which, at, :]).astype(BF16)

            row_loop(BLK, ROWS, body)
            done.start()

        t.add(name + "s", [name + "df"], lambda: [], exchange)
        t.add(name, [name + "s"], lambda: shared[name], conclude)
        return done

    out_done = projection("o", 0, "h", gathers_h, part_h, acts, wo, 0, out_ref)
    gt_done = projection("i", 1, "g", gathers_g, part_g, ghid, wi, 1, gt_ref)

    whole_h = ["ox" + str(s) for s in STEPS]
    whole_g = ["ix" + str(s) for s in STEPS]

    go_done = pltpu.make_async_copy(go.at[:, my_d], go_ref.at[my_f], local.at[6])
    gi_done = pltpu.make_async_copy(gi.at[my_d], gi_ref.at[:, my_f], local.at[7])
    ends = []

    def grad_out_tiles(half):
        def tile(n):
            cols = pl.ds(pl.multiple_of(half * (FH // 2) + n * 256, 256), 256)
            go[cols, :] = dot(acts[:, cols], cot[...], 0, 0).astype(BF16)

        def do():
            tiles(FH // 512, tile)
            here, there = split(half * (FH // 2), FH // 2, 2), split(k * FH + half * (FH // 2), FH // 2, 2)
            ends.extend(to_sibling([(go.at[a, its_d], go_ref.at[b]) for a, b in zip(here, there)]))
            if half == 1:
                go_done.start()

        return do

    t.add("go0", whole_h + ["gpart2"], lambda: [], grad_out_tiles(0))
    t.add("go1", ["go0"], lambda: [], grad_out_tiles(1))

    def turn_tokens():
        def tile(n):
            cols = pl.ds(pl.multiple_of(n * 128, 128), 128)
            turned[cols, :] = tok[:, cols].T

        tiles(DP // 128, tile)

    t.add("turn", ["hpart0"], lambda: [], turn_tokens)

    def grad_in_tiles(rows, half, last):
        def tile(n):
            cols = pl.ds(pl.multiple_of(half * DP + n * 256, 256), 256)
            gi[rows, cols] = dot(turned[rows, :], ghid[:, cols], 1, 0).astype(BF16)

        def do():
            tiles(DP // 256, tile)
            last(half)

        return do

    def send_gi(half):
        here, there = pl.ds(half * DP, DP), pl.ds(pl.multiple_of(k * FH + half * DP, 128), DP)
        parts = zip(split((1 - k) * DC, DC, 2), split(0, DC, 2))
        ends.extend(to_sibling([(gi.at[a, here], gi_ref.at[b, there]) for a, b in parts]))

    def store_gi(half):
        if half == 1:
            gi_done.start()

    for name, rows, last in (("gi", its_d, send_gi), ("gj", my_d, store_gi)):
        t.add(name + "0", whole_g + ["turn"], lambda: [], grad_in_tiles(rows, 0, last))
        t.add(name + "1", [name + "0"], lambda: [], grad_in_tiles(rows, 1, last))

    run_tasks(t)

    for c in ends:
        l.take(c)
    for c in (go_done, gi_done, out_done, gt_done):
        c.wait()
    for c in l.started:
        c.wait_send()


def hand_over(*refs):
    results, targets, held, (arrive, leave) = refs[:4], refs[4:8], refs[8:12], refs[12:]
    ins, outs = [], []
    for src, dst, mid in zip(results, targets, held):
        parts = 4 if src.shape[0] > BLK else 1
        rows = src.shape[0] // parts
        for p in range(parts):
            at, i = pl.ds(p * rows, rows), len(ins)
            ins.append(pltpu.make_async_copy(src.at[at], mid.at[at], arrive.at[i]))
            outs.append(pltpu.make_async_copy(mid.at[at], dst.at[at], leave.at[i]))
    for c in ins:
        c.start()
    for c, d in zip(ins, outs):
        c.wait()
        d.start()
    for d in outs:
        d.wait()


def local(tokens, weight_in, weight_out, cotangent):
    results = block(tokens, weight_in, weight_out, cotangent)
    any_space = pl.BlockSpec(memory_space=pl.ANY)
    return pl.pallas_call(
        hand_over,
        out_shape=tuple(jax.ShapeDtypeStruct(r.shape, r.dtype) for r in results),
        in_specs=[any_space] * 4,
        out_specs=(any_space,) * 4,
        scratch_shapes=[pltpu.VMEM(r.shape, r.dtype) for r in results] + [pltpu.SemaphoreType.DMA((10,))] * 2,
        compiler_params=pltpu.CompilerParams(vmem_limit_bytes=60 * 1024 * 1024),
    )(*results)


def block(tokens, weight_in, weight_out, cotangent):
    any_space = pl.BlockSpec(memory_space=pl.ANY)
    shape = jax.ShapeDtypeStruct
    vmem = pltpu.VMEM
    return pl.pallas_call(
        kernel,
        out_shape=(
            shape((BLK, DC), BF16),
            shape((BLK, DC), BF16),
            shape((DC, 2 * FH), BF16),
            shape((2 * FH, DC), BF16),
        ),
        in_specs=[any_space] * 4,
        out_specs=(any_space,) * 4,
        scratch_shapes=[
            vmem((TOK, DP), BF16), vmem((TOK, DP), BF16), vmem((DP, FH), BF16), vmem((FH, DP), BF16),
            vmem((TOK, FH), F32), vmem((TOK, FH), F32), vmem((TOK, FH), BF16), vmem((TOK, FH), BF16),
            vmem((10, BLK, FA), BF16), vmem((10, BLK, FA), BF16),
            vmem((5, BLK, FB), BF16), vmem((5, BLK, FB), BF16),
            vmem((10, BLK // 2, FB), BF16), vmem((10, BLK // 2, FB), BF16),
            vmem((BLK, FH), F32), vmem((TOK, FH), BF16), vmem((TOK, FH), BF16),
            vmem((2, BLK, DP), F32), vmem((2, BLK, DC), F32), vmem((2, TOK, DP), BF16),
            vmem((2, 10, BLK, DP), BF16),
            vmem((DP, FH), BF16), vmem((FH, DP), BF16), vmem((2, BLK, DC), BF16), vmem((DP, TOK), BF16),
            pltpu.SemaphoreType.DMA((COPIES,)), pltpu.SemaphoreType.DMA((COPIES,)),
            pltpu.SemaphoreType.DMA((8,)),
        ],
        compiler_params=pltpu.CompilerParams(
            collective_id=0, has_side_effects=True, vmem_limit_bytes=60 * 1024 * 1024
        ),
        cost_estimate=pl.CostEstimate(flops=14_500_000_000, bytes_accessed=12_000_000, transcendentals=400_000),
    )(tokens, weight_in, weight_out, cotangent)


def solution(mesh):
    placed = (P("row", "col"), P("col", "row"), P("row", "col"), P("row", "col"))
    return jax.shard_map(
        local,
        mesh=mesh,
        in_specs=placed,
        out_specs=(P("row", "col"), P("row", "col"), P("col", "row"), P("row", "col")),
        check_vma=False,
    )
```

```python
import functools

import jax
import jax.numpy as jnp
from jax import lax
from jax.experimental import pallas as pl
from jax.experimental.pallas import tpu as pltpu
from jax.sharding import PartitionSpec as P

F32 = jnp.float32
BF16 = jnp.bfloat16

TOK = 1024
BLK = 128
DC = 384
DP = 2 * DC
FH = 1536
FA = 896
FB = FH - FA

COPIES = 128
ROWS = 16
C_GELU = 0.7978845608028654
C_CUBE = 0.044715


def row_loop(rows, chunk, body):
    def step(i, carry):
        body(pl.multiple_of(i * chunk, chunk))
        return carry

    lax.fori_loop(0, rows // chunk, step, 0)


def tiles(count, body):
    def step(i, carry):
        body(i)
        return carry

    lax.fori_loop(0, count, step, 0)


class Links:
    def __init__(self, send, recv):
        self.send, self.recv, self.used = send, recv, 0
        self.started, self.taken = [], []
        row, col = lax.axis_index("row"), lax.axis_index("col")
        self.x, self.yh = row // 2, row % 2
        self.yl, self.z, self.k = col // 8, (col // 2) % 4, col % 2

    def device(self, **moved):
        at = {n: moved.get(n, getattr(self, n)) for n in ("x", "yh", "yl", "z", "k")}
        return (at["x"] * 2 + at["yh"], at["yl"] * 8 + at["z"] * 2 + at["k"])

    def ring(self, axis, step):
        return self.device(**{axis: lax.rem(getattr(self, axis) + step + 4, 4)})

    def other(self, axis):
        return self.device(**{axis: 1 - getattr(self, axis)})

    def copy(self, src, dst, device):
        i = self.used
        self.used += 1
        c = pltpu.make_async_remote_copy(
            src_ref=src,
            dst_ref=dst,
            send_sem=self.send.at[i],
            recv_sem=self.recv.at[i],
            device_id=device,
            device_id_type=pl.DeviceIdType.MESH,
        )
        c.start()
        self.started.append(c)
        return c

    def take(self, c):
        if all(c is not d for d in self.taken):
            c.wait_recv()
            self.taken.append(c)

    def place(self, axis, step):
        return lax.rem(getattr(self, axis) + step + 4, 4)


def rows_of(place, member, count=BLK, skip=0):
    return pl.ds(pl.multiple_of(place * (2 * BLK) + member * BLK + skip, 16), count)


class GatherRingLast:
    def __init__(self, links, ring, pair, buf, cols, source=None):
        self.l, self.ring, self.pair, self.buf, self.cols = links, ring, pair, buf, cols
        self.mine, self.source = getattr(links, pair), source

    def at(self, step, member):
        return self.buf.at[rows_of(self.l.place(self.ring, step), member), self.cols]

    def send(self, ref, step, source=None):
        to = self.l.ring(self.ring, step) if step else self.l.other(self.pair)
        return self.l.copy(ref if source is None else source, ref, to)

    def start(self):
        own = self.at(0, self.mine)
        self.y = self.send(own, 0, self.source)
        self.own_p = self.send(own, 1, self.source)
        self.own_m = self.send(own, -1, self.source)

    def second(self):
        theirs = self.at(0, 1 - self.mine)
        self.oth_p = self.send(theirs, 1)
        self.oth_m = self.send(theirs, -1)

    def onward_p(self):
        self.far_p = self.send(self.at(-1, self.mine), 1)

    def onward_m(self):
        self.far_m = self.send(self.at(1, 1 - self.mine), -1)

    def arrived(self, step):
        if step == 0:
            return [self.y]
        if step == 2:
            return [self.far_p, self.far_m]
        return [self.own_p, self.oth_p] if step == -1 else [self.own_m, self.oth_m]

    def tasks(self, t, name, after):
        t.add(name + "0", after, lambda: [], self.start)
        t.add(name + "1", [name + "0"], lambda: [self.y], self.second)
        t.add(name + "p", [name + "0"], lambda: [self.own_p], self.onward_p)
        t.add(name + "m", [name + "1"], lambda: [self.oth_m], self.onward_m)


class GatherRingFirst:
    def __init__(self, links, ring, pair, buf, cols):
        self.l, self.ring, self.pair, self.buf, self.cols = links, ring, pair, buf, cols
        self.mine = getattr(links, pair)

    def at(self, step, count=BLK, skip=0):
        return self.buf.at[rows_of(self.l.place(self.ring, step), self.mine, count, skip), self.cols]

    def send(self, ref, step):
        to = self.l.ring(self.ring, step) if step else self.l.other(self.pair)
        return self.l.copy(ref, ref, to)

    def start(self):
        own = self.at(0)
        self.own_p = self.send(own, 1)
        self.own_m = self.send(own, -1)
        self.y0 = self.send(own, 0)

    def onward_p(self):
        self.far_p = self.send(self.at(-1, BLK // 2), 1)
        self.yp = self.send(self.at(-1), 0)

    def onward_m(self):
        self.far_m = self.send(self.at(1, BLK // 2, BLK // 2), -1)
        self.ym = self.send(self.at(1), 0)

    def across_p(self):
        self.yfp = self.send(self.at(2, BLK // 2), 0)

    def across_m(self):
        self.yfm = self.send(self.at(2, BLK // 2, BLK // 2), 0)

    def arrived(self, step):
        if step == 0:
            return [self.y0]
        if step == 2:
            return [self.yfp, self.yfm]
        return [self.yp] if step == -1 else [self.ym]

    def tasks(self, t, name, after):
        t.add(name + "0", after, lambda: [], self.start)
        t.add(name + "p", [name + "0"], lambda: [self.own_p], self.onward_p)
        t.add(name + "m", [name + "0"], lambda: [self.own_m], self.onward_m)
        t.add(name + "yp", [name + "p"], lambda: [self.far_p], self.across_p)
        t.add(name + "ym", [name + "m"], lambda: [self.far_m], self.across_m)


class ReduceRingFirst:
    def __init__(self, links, ring, pair, part, out, col, out_col, width, slots):
        self.l, self.ring, self.pair = links, ring, pair
        self.part, self.out, self.col, self.width, self.slots = part, out, col, width, slots
        self.out_cols = pl.ds(out_col, width)
        self.mine = getattr(links, pair)

    def block(self, step, member):
        return self.out.at[rows_of(self.l.place(self.ring, step), member), self.out_cols]

    def sent(self, step):
        l = self.l
        if step == 2:
            self.p2 = l.copy(self.block(2, 0), self.slots.at[0], l.ring(self.ring, 1))
            self.m2 = l.copy(self.block(2, 1), self.slots.at[1], l.ring(self.ring, -1))
        elif step == 1:
            self.p1 = l.copy(self.block(1, 1), self.slots.at[2], l.ring(self.ring, 1))
        elif step == -1:
            self.m1 = l.copy(self.block(-1, 0), self.slots.at[3], l.ring(self.ring, -1))

    def add(self, dst, start, *slots):
        def body(r):
            total = self.part[pl.ds(start + r, ROWS), pl.ds(self.col, self.width)]
            for s in slots:
                total = total + self.slots[s, pl.ds(r, ROWS), :].astype(F32)
            dst(r, total)

        row_loop(BLK, ROWS, body)

    def start_of(self, step, member):
        return pl.multiple_of(self.l.place(self.ring, step) * (2 * BLK) + member * BLK, BLK)

    def to_slot(self, slot):
        def put(r, total):
            self.slots[slot, pl.ds(r, ROWS), :] = total.astype(BF16)

        return put

    def combine_p(self):
        self.add(self.to_slot(7), self.start_of(1, 0), 0)
        self.pc = self.l.copy(self.slots.at[7], self.slots.at[4], self.l.ring(self.ring, 1))

    def combine_m(self):
        self.add(self.to_slot(8), self.start_of(-1, 1), 1)
        self.mc = self.l.copy(self.slots.at[8], self.slots.at[5], self.l.ring(self.ring, -1))

    def across(self):
        for member, slots in ((0, (4, 3)), (1, (2, 5))):
            start = self.start_of(0, member)

            def put(r, total, start=start):
                self.part[pl.ds(start + r, ROWS), pl.ds(self.col, self.width)] = total

            self.add(put, start, *slots)
        self.add(self.to_slot(9), self.start_of(0, 1 - self.mine))
        self.y = self.l.copy(self.slots.at[9], self.slots.at[6], self.l.other(self.pair))

    def tasks(self, t, name, put, after, first, last, final):
        t.add(name + "p", [after(1), first], lambda: [self.p2], self.combine_p)
        t.add(name + "m", [after(-1), first], lambda: [self.m2], self.combine_m)
        t.add(
            name + "y", [last, name + "p", name + "m"],
            lambda: [self.p1, self.m1, self.pc, self.mc], self.across,
        )
        t.add(
            name + "f", [name + "y"] + final, lambda: [self.y],
            lambda: self.add(put, self.start_of(0, self.mine), 6),
        )


class ReducePairFirst:
    def __init__(self, links, ring, pair, part, out, col, width, slots, halves):
        self.l, self.ring, self.pair = links, ring, pair
        self.part, self.out, self.col, self.width = part, out, col, width
        self.slots, self.halves = slots, halves
        self.mine = getattr(links, pair)
        self.y = {}

    def sent(self, step):
        rows = rows_of(self.l.place(self.ring, step), 1 - self.mine)
        block = self.out.at[rows, pl.ds(self.col, self.width)]
        self.y[step] = self.l.copy(block, self.slots.at[step % 4], self.l.other(self.pair))

    def add(self, dst, step, skip, count, *halves):
        start = pl.multiple_of(self.l.place(self.ring, step) * (2 * BLK) + self.mine * BLK + skip, 64)

        def body(r):
            total = self.part[pl.ds(start + r, ROWS), pl.ds(self.col, self.width)]
            total = total + self.slots[step % 4, pl.ds(skip + r, ROWS), :].astype(F32)
            for h in halves:
                total = total + self.halves[h, pl.ds(r, ROWS), :].astype(F32)
            dst(r, total)

        row_loop(count, ROWS, body)

    def to_half(self, half):
        def put(r, total):
            self.halves[half, pl.ds(r, ROWS), :] = total.astype(BF16)

        return put

    def ring_copy(self, src, dst, step):
        return self.l.copy(src, self.halves.at[dst], self.l.ring(self.ring, step))

    def far(self):
        def put(r, total):
            self.slots[4, pl.ds(r, ROWS), :] = total.astype(BF16)

        self.add(put, 2, 0, BLK)
        self.p2 = self.ring_copy(self.slots.at[4, pl.ds(0, BLK // 2)], 0, 1)
        self.m2 = self.ring_copy(self.slots.at[4, pl.ds(BLK // 2, BLK // 2)], 1, -1)

    def near_p(self):
        self.add(self.to_half(6), 1, BLK // 2, BLK // 2)
        self.p1 = self.ring_copy(self.halves.at[6], 2, 1)

    def near_m(self):
        self.add(self.to_half(7), -1, 0, BLK // 2)
        self.m1 = self.ring_copy(self.halves.at[7], 3, -1)

    def combine_p(self):
        self.add(self.to_half(8), 1, 0, BLK // 2, 0)
        self.pc = self.ring_copy(self.halves.at[8], 4, 1)

    def combine_m(self):
        self.add(self.to_half(9), -1, BLK // 2, BLK // 2, 1)
        self.mc = self.ring_copy(self.halves.at[9], 5, -1)

    def finish(self, put):
        half = BLK // 2
        self.add(put, 0, 0, half, 4, 3)
        self.add(lambda r, total: put(half + r, total), 0, half, half, 2, 5)

    def tasks(self, t, name, put, after, final):
        t.add(name + "2", [after(2)], lambda: [self.y[2]], self.far)
        t.add(name + "1", [after(1)], lambda: [self.y[1]], self.near_p)
        t.add(name + "3", [after(-1)], lambda: [self.y[-1]], self.near_m)
        t.add(name + "p", [name + "2", name + "1"], lambda: [self.p2], self.combine_p)
        t.add(name + "m", [name + "2", name + "3"], lambda: [self.m2], self.combine_m)
        t.add(
            name + "f", [after(0), name + "p", name + "m"] + final,
            lambda: [self.y[0], self.p1, self.m1, self.pc, self.mc],
            lambda: self.finish(put),
        )


class Tasks:
    def __init__(self, links):
        self.l, self.all = links, {}

    def add(self, name, after, waits, do):
        self.all[name] = (after, waits, do)

    def step(self, name):
        _, waits, do = self.all[name]
        for c in waits():
            self.l.take(c)
        do()


ORDER = (
    "t0", "t1", "ts0", "c0", "tp", "ts-1", "ts1", "tm", "ts2", "c1", "cp", "hpart2", "cm", "hpart1",
    "hpart-1", "hpart0", "cs0", "cs-1", "cs2", "turn", "hb2", "hap", "ham", "cs1", "gpart2", "gpart1", "hb1",
    "gpart-1", "gpart0", "hb3", "hbp", "hbm", "hay", "gb2", "gb1", "gam", "gb3", "gap", "hbf", "hB0", "gbp",
    "gbm", "haf", "hA0", "gay", "hA1", "ox0", "hBm", "hBp", "gbf", "gB0", "gaf", "hAp", "ox-1", "ox1", "hAm",
    "gA0", "hByp", "om-1", "om1", "hBym", "gBm", "gBp", "om0", "gA1", "ix0", "im0", "ox2", "go1", "om2", "or",
    "gAp", "gBym", "go0", "gAm", "ix1", "odp", "odm", "gByp", "ix-1", "im1", "ody", "im-1", "ix2", "gi0",
    "im2", "ir", "odf", "gi", "gj0", "gj", "idp", "o", "go", "idm", "idy", "idf", "i",
)


def run_tasks(t):
    done = set()
    for name in ORDER:
        assert done.issuperset(t.all[name][0]), name
        t.step(name)
        done.add(name)
    assert len(done) == len(t.all)


def dot(a, b, left, right):
    return lax.dot_general(a, b, (((left,), (right,)), ((), ())), preferred_element_type=F32)


STEPS = (2, 1, -1, 0)


def kernel(
    tok_in, wi_in, wo_in, cot_in,
    out_ref, gt_ref, gi_ref, go_ref,
    tok, cot, wi, wo,
    part_h, part_g, send_h, send_g,
    ra_h, ra_g, rb_h, rb_g, rh_h, rh_g,
    hid, acts, ghid,
    sib_in, rbuf, rd,
    gi, go, final, turned,
    send, recv, local,
):
    l = Links(send, recv)
    t = Tasks(l)
    k = l.k
    sib = l.other("k")

    barrier = pltpu.get_barrier_semaphore()
    near = [sib, l.other("yl"), l.other("yh")]
    near += [l.ring(a, s) for a in ("z", "x") for s in (1, -1)]
    for d in near:
        pl.semaphore_signal(barrier, inc=1, device_id=d, device_id_type=pl.DeviceIdType.MESH)

    my_d = pl.ds(pl.multiple_of(k * DC, 128), DC)
    its_d = pl.ds(pl.multiple_of((1 - k) * DC, 128), DC)
    my_f = pl.ds(pl.multiple_of(k * FH, 128), FH)
    its_f = pl.ds(pl.multiple_of((1 - k) * FH, 128), FH)
    own_rows = rows_of(l.x, l.yh)

    load_tok = pltpu.make_async_copy(tok_in, tok.at[own_rows, my_d], local.at[0])
    load_cot = pltpu.make_async_copy(cot_in, cot.at[own_rows, my_d], local.at[1])
    load_wi = pltpu.make_async_copy(wi_in.at[:, my_f], wi.at[my_d], local.at[2])
    load_wo = pltpu.make_async_copy(wo_in.at[my_f], wo.at[:, my_d], local.at[3])
    for c in (load_tok, load_wi, load_cot, load_wo):
        c.start()
    pl.semaphore_wait(barrier, len(near))

    def pair_rows(axis, step):
        return pl.ds(pl.multiple_of(l.place(axis, step) * (2 * BLK), 2 * BLK), 2 * BLK)

    shared = {}

    def gather_tokens(name, buf, source, load, weight, target, after):
        g = GatherRingLast(l, "x", "yh", buf, my_d, source)

        def start():
            g.start()
            shared[name + "w"] = l.copy(weight, target, sib)

        g.tasks(t, name, after)
        t.add(name + "0", after, lambda: [], start)

        def share(step):
            def do():
                if step == 0:
                    load.wait()
                ref = buf.at[pair_rows("x", step), my_d]
                shared[name + str(step)] = l.copy(ref, ref, sib)

            return do

        for step, before in ((0, ["1"]), (1, ["1"]), (-1, ["1"]), (2, ["p", "m"])):
            t.add(
                name + "s" + str(step), [name + b for b in before],
                lambda step=step: g.arrived(step), share(step),
            )

    gather_tokens("t", tok, tok_in, load_tok, wi_in.at[:, its_f], wi.at[my_d], [])
    gather_tokens("c", cot, cot_in, load_cot, wo_in.at[its_f], wo.at[:, my_d], ["t1"])

    def put_hidden(col, width):
        cols = pl.ds(col, width)

        def put(r, h):
            hid[pl.ds(r, ROWS), cols] = h
            tanh = jnp.tanh(C_GELU * (h + C_CUBE * (h * h * h)))
            acts[pl.ds(own + r, ROWS), cols] = (0.5 * h * (1.0 + tanh)).astype(BF16)

        return put

    def put_grad(col, width):
        cols = pl.ds(col, width)

        def put(r, total):
            h = hid[pl.ds(r, ROWS), cols]
            square = h * h
            tanh = jnp.tanh(C_GELU * (h + C_CUBE * (square * h)))
            slope = 0.5 * (1.0 + tanh)
            slope += (0.5 * C_GELU) * h * (1.0 - tanh * tanh) * (1.0 + 3.0 * C_CUBE * square)
            ghid[pl.ds(own + r, ROWS), cols] = (total * slope).astype(BF16)

        return put

    own = pl.multiple_of(l.z * (2 * BLK) + l.yl * BLK, BLK)

    def reduction(name, source, load, product, part, out, slots_a, slots_b, halves, put, gathered, final):
        ring = ReduceRingFirst(l, "z", "yl", part, out, 0, 0, FA, slots_a)
        pair = ReducePairFirst(l, "z", "yl", part, out, FA, FB, slots_b, halves)

        def partial(step):
            def do():
                if step == STEPS[0]:
                    load.wait()
                rows = pair_rows("z", step)

                def tile(n):
                    cols = pl.ds(pl.multiple_of(n * 256, 256), 256)
                    total = product(rows, cols)
                    part[rows, cols] = total
                    out[rows, cols] = total.astype(BF16)

                tiles(FH // 256, tile)
                pair.sent(step)
                ring.sent(step)

            return do

        def part_of(step):
            return name + "part" + str(step)

        shares = [source + "s" + str(s) for s in STEPS]
        for i, step in enumerate(STEPS):
            t.add(
                part_of(step), shares if i == 0 else [part_of(STEPS[i - 1])],
                lambda: [shared[source + "w"]] + [shared[source + str(s)] for s in STEPS], partial(step),
            )
        ring.tasks(t, name + "a", put(0, FA), part_of, part_of(2), part_of(0), [f + "af" for f in final])
        pair.tasks(t, name + "b", put(FA, FB), part_of, [f + "bf" for f in final])
        a = GatherRingLast(l, "z", "yl", gathered, pl.ds(0, FA))
        b = GatherRingFirst(l, "z", "yl", gathered, pl.ds(FA, FB))
        a.tasks(t, name + "A", [name + "af"])
        b.tasks(t, name + "B", [name + "bf"])
        return a, b

    gathers_h = reduction(
        "h", "t", load_wi, lambda rows, cols: dot(tok[rows, :], wi[:, cols], 1, 0),
        part_h, send_h, ra_h, rb_h, rh_h, put_hidden, acts, [],
    )
    gathers_g = reduction(
        "g", "c", load_wo, lambda rows, cols: dot(cot[rows, :], wo[cols, :], 1, 1),
        part_g, send_g, ra_g, rb_g, rh_g, put_grad, ghid, ["h"],
    )

    merged = {}

    def projection(name, which, before, gathers, part, lhs, weight, right, target):
        final_sum = ReduceRingFirst(l, "x", "yh", part, rbuf.at[which], DP, 0, DC, rd.at[which])

        def project(step):
            def do():
                rows = pair_rows("z", step)

                def tile(n):
                    cols = pl.ds(pl.multiple_of(n * 256, 256), 256)
                    part[rows, cols] = dot(lhs[rows, :], weight[(cols, slice(None))[::2 * right - 1]], 1, right)

                tiles(DP // 256, tile)
                merged[name + str(step)] = l.copy(part.at[rows, its_d], sib_in.at[which, rows], sib)

            return do

        def merge(step):
            def do():
                start = pl.multiple_of(l.place("z", step) * (2 * BLK), 2 * BLK)

                def body(r):
                    at = pl.ds(start + r, ROWS)
                    total = part[at, my_d] + sib_in[which, at, :]
                    part[at, pl.ds(DP, DC)] = total
                    rbuf[which, at, :] = total.astype(BF16)

                row_loop(2 * BLK, ROWS, body)

            return do

        for step, need in ((0, ["A1", "B0"]), (1, ["A1", "Bm"]), (-1, ["A1", "Bp"]), (2, ["Ap", "Am", "Byp", "Bym"])):
            t.add(
                name + "x" + str(step), [before + n for n in need] + [before + "af", before + "bf"],
                lambda step=step: gathers[0].arrived(step) + gathers[1].arrived(step), project(step),
            )
            t.add(
                name + "m" + str(step), [name + "x" + str(step)],
                lambda step=step: [merged[name + str(step)]], merge(step),
            )

        def go_round():
            for step in STEPS:
                final_sum.sent(step)

        merges = [name + "m" + str(s) for s in STEPS]
        t.add(name + "r", merges, lambda: [], go_round)

        def put(r, total):
            final[which, pl.ds(r, ROWS), :] = total.astype(BF16)

        final_sum.tasks(t, name + "d", put, lambda s: name + "r", name + "r", name + "r", [])
        return pltpu.make_async_copy(final.at[which], target, local.at[4 + which])

    out_done = projection("o", 0, "h", gathers_h, part_h, acts, wo, 0, out_ref)
    gt_done = projection("i", 1, "g", gathers_g, part_g, ghid, wi, 1, gt_ref)
    t.add("o", ["odf"], lambda: [], out_done.start)
    t.add("i", ["idf"], lambda: [], gt_done.start)

    whole_h = ["ox" + str(s) for s in STEPS] + ["cs" + str(s) for s in STEPS]
    whole_g = ["ix" + str(s) for s in STEPS]

    def grad_out_tiles(half):
        def tile(n):
            cols = pl.ds(pl.multiple_of(half * (FH // 2) + n * 256, 256), 256)
            go[cols, :] = dot(acts[:, cols], cot[...], 0, 0).astype(BF16)

        return lambda: tiles(FH // 512, tile)

    for half in range(2):
        t.add("go" + str(half), whole_h + ["gpart2"], lambda: [], grad_out_tiles(half))
    go_done = pltpu.make_async_copy(go.at[:, my_d], go_ref.at[my_f], local.at[6])
    gi_done = pltpu.make_async_copy(gi.at[my_d], gi_ref.at[:, my_f], local.at[7])
    ends = []

    def send_go():
        go_done.start()
        ends.append(l.copy(go.at[:, its_d], go_ref.at[my_f], sib))

    t.add("go", ["go0", "go1"], lambda: [], send_go)

    def turn_tokens():
        def tile(n):
            cols = pl.ds(pl.multiple_of(n * 128, 128), 128)
            turned[cols, :] = tok[:, cols].T

        tiles(DP // 128, tile)

    t.add("turn", ["hpart0"], lambda: [], turn_tokens)

    def grad_in_tiles(rows):
        def tile(n):
            cols = pl.ds(pl.multiple_of(n * 256, 256), 256)
            gi[rows, cols] = dot(turned[rows, :], ghid[:, cols], 1, 0).astype(BF16)

        return lambda: tiles(FH // 256, tile)

    t.add("gi0", whole_g + ["turn"], lambda: [], grad_in_tiles(its_d))
    t.add("gj0", whole_g + ["turn"], lambda: [], grad_in_tiles(my_d))
    t.add("gi", ["gi0"], lambda: [], lambda: ends.append(l.copy(gi.at[its_d], gi_ref.at[:, my_f], sib)))
    t.add("gj", ["gj0"], lambda: [], gi_done.start)

    run_tasks(t)

    for c in ends:
        l.take(c)
    for c in (go_done, gi_done, out_done, gt_done):
        c.wait()
    for c in l.started:
        c.wait_send()


def hand_over(*refs):
    results, targets, held, (arrive, leave) = refs[:4], refs[4:8], refs[8:12], refs[12:]
    ins, outs = [], []
    for src, dst, mid in zip(results, targets, held):
        parts = 4 if src.shape[0] > BLK else 1
        rows = src.shape[0] // parts
        for p in range(parts):
            at, i = pl.ds(p * rows, rows), len(ins)
            ins.append(pltpu.make_async_copy(src.at[at], mid.at[at], arrive.at[i]))
            outs.append(pltpu.make_async_copy(mid.at[at], dst.at[at], leave.at[i]))
    for c in ins:
        c.start()
    for c, d in zip(ins, outs):
        c.wait()
        d.start()
    for d in outs:
        d.wait()


def local(tokens, weight_in, weight_out, cotangent):
    results = block(tokens, weight_in, weight_out, cotangent)
    any_space = pl.BlockSpec(memory_space=pl.ANY)
    return pl.pallas_call(
        hand_over,
        out_shape=tuple(jax.ShapeDtypeStruct(r.shape, r.dtype) for r in results),
        in_specs=[any_space] * 4,
        out_specs=(any_space,) * 4,
        scratch_shapes=[pltpu.VMEM(r.shape, r.dtype) for r in results] + [pltpu.SemaphoreType.DMA((10,))] * 2,
        compiler_params=pltpu.CompilerParams(vmem_limit_bytes=60 * 1024 * 1024),
    )(*results)


def block(tokens, weight_in, weight_out, cotangent):
    any_space = pl.BlockSpec(memory_space=pl.ANY)
    shape = jax.ShapeDtypeStruct
    vmem = pltpu.VMEM
    return pl.pallas_call(
        kernel,
        out_shape=(
            shape((BLK, DC), BF16),
            shape((BLK, DC), BF16),
            shape((DC, 2 * FH), BF16),
            shape((2 * FH, DC), BF16),
        ),
        in_specs=[any_space] * 4,
        out_specs=(any_space,) * 4,
        scratch_shapes=[
            vmem((TOK, DP), BF16), vmem((TOK, DP), BF16), vmem((DP, FH), BF16), vmem((FH, DP), BF16),
            vmem((TOK, FH), F32), vmem((TOK, FH), F32), vmem((TOK, FH), BF16), vmem((TOK, FH), BF16),
            vmem((10, BLK, FA), BF16), vmem((10, BLK, FA), BF16),
            vmem((5, BLK, FB), BF16), vmem((5, BLK, FB), BF16),
            vmem((10, BLK // 2, FB), BF16), vmem((10, BLK // 2, FB), BF16),
            vmem((BLK, FH), F32), vmem((TOK, FH), BF16), vmem((TOK, FH), BF16),
            vmem((2, TOK, DC), F32), vmem((2, TOK, DC), BF16),
            vmem((2, 10, BLK, DC), BF16),
            vmem((DP, FH), BF16), vmem((FH, DP), BF16), vmem((2, BLK, DC), BF16), vmem((DP, TOK), BF16),
            pltpu.SemaphoreType.DMA((COPIES,)), pltpu.SemaphoreType.DMA((COPIES,)),
            pltpu.SemaphoreType.DMA((8,)),
        ],
        compiler_params=pltpu.CompilerParams(
            collective_id=0, has_side_effects=True, vmem_limit_bytes=60 * 1024 * 1024
        ),
        cost_estimate=pl.CostEstimate(flops=14_500_000_000, bytes_accessed=12_000_000, transcendentals=400_000),
    )(tokens, weight_in, weight_out, cotangent)


def solution(mesh):
    placed = (P("row", "col"), P("col", "row"), P("row", "col"), P("row", "col"))
    return jax.shard_map(
        local,
        mesh=mesh,
        in_specs=placed,
        out_specs=(P("row", "col"), P("row", "col"), P("col", "row"), P("row", "col")),
        check_vma=False,
    )
```

```python
import functools

import jax
import jax.numpy as jnp
from jax import lax
from jax.experimental import pallas as pl
from jax.experimental.pallas import tpu as pltpu
from jax.sharding import PartitionSpec as P

F32 = jnp.float32
BF16 = jnp.bfloat16

TOK = 1024
BLK = 128
DC = 384
DP = 2 * DC
FH = 1536
FA = 768
FB = FH - FA

COPIES = 128
ROWS = 16
C_GELU = 0.7978845608028654
C_CUBE = 0.044715


def row_loop(rows, chunk, body):
    def step(i, carry):
        body(pl.multiple_of(i * chunk, chunk))
        return carry

    lax.fori_loop(0, rows // chunk, step, 0)


def tiles(count, body):
    def step(i, carry):
        body(i)
        return carry

    lax.fori_loop(0, count, step, 0)


class Links:
    def __init__(self, send, recv):
        self.send, self.recv, self.used = send, recv, 0
        self.started, self.taken = [], []
        row, col = lax.axis_index("row"), lax.axis_index("col")
        self.x, self.yh = row // 2, row % 2
        self.yl, self.z, self.k = col // 8, (col // 2) % 4, col % 2

    def device(self, **moved):
        at = {n: moved.get(n, getattr(self, n)) for n in ("x", "yh", "yl", "z", "k")}
        return (at["x"] * 2 + at["yh"], at["yl"] * 8 + at["z"] * 2 + at["k"])

    def ring(self, axis, step):
        return self.device(**{axis: lax.rem(getattr(self, axis) + step + 4, 4)})

    def other(self, axis):
        return self.device(**{axis: 1 - getattr(self, axis)})

    def copy(self, src, dst, device):
        c = self.plan(src, dst, device)
        c.start()
        return c

    def plan(self, src, dst, device, slot=None):
        i = self.used if slot is None else slot
        self.used += slot is None
        c = pltpu.make_async_remote_copy(
            src_ref=src,
            dst_ref=dst,
            send_sem=self.send.at[i],
            recv_sem=self.recv.at[i],
            device_id=device,
            device_id_type=pl.DeviceIdType.MESH,
        )
        if slot is None:
            self.started.append(c)
        return c

    def take(self, c):
        if all(c is not d for d in self.taken):
            c.wait_recv()
            self.taken.append(c)

    def place(self, axis, step):
        return lax.rem(getattr(self, axis) + step + 4, 4)


def rows_of(place, member, count=BLK, skip=0):
    return pl.ds(pl.multiple_of(place * (2 * BLK) + member * BLK + skip, 16), count)


class GatherRingLast:
    def __init__(self, links, ring, pair, buf, cols, source=None):
        self.l, self.ring, self.pair, self.buf, self.cols = links, ring, pair, buf, cols
        self.mine, self.source = getattr(links, pair), source

    def at(self, step, member):
        return self.buf.at[rows_of(self.l.place(self.ring, step), member), self.cols]

    def send(self, ref, step, source=None):
        to = self.l.ring(self.ring, step) if step else self.l.other(self.pair)
        return self.l.copy(ref if source is None else source, ref, to)

    def start(self):
        own = self.at(0, self.mine)
        self.y = self.send(own, 0, self.source)
        self.own_p = self.send(own, 1, self.source)
        self.own_m = self.send(own, -1, self.source)

    def second(self):
        theirs = self.at(0, 1 - self.mine)
        self.oth_p = self.send(theirs, 1)
        self.oth_m = self.send(theirs, -1)

    def onward_p(self):
        self.far_p = self.send(self.at(-1, self.mine), 1)

    def onward_m(self):
        self.far_m = self.send(self.at(1, 1 - self.mine), -1)

    def arrived(self, step):
        if step == 0:
            return [self.y]
        if step == 2:
            return [self.far_p, self.far_m]
        return [self.own_p, self.oth_p] if step == -1 else [self.own_m, self.oth_m]

    def tasks(self, t, name, after):
        t.add(name + "0", after, lambda: [], self.start)
        t.add(name + "1", [name + "0"], lambda: [self.y], self.second)
        t.add(name + "p", [name + "0"], lambda: [self.own_p], self.onward_p)
        t.add(name + "m", [name + "1"], lambda: [self.oth_m], self.onward_m)


class GatherRingFirst:
    def __init__(self, links, ring, pair, buf, cols):
        self.l, self.ring, self.pair, self.buf, self.cols = links, ring, pair, buf, cols
        self.mine = getattr(links, pair)

    def at(self, step, count=BLK, skip=0):
        return self.buf.at[rows_of(self.l.place(self.ring, step), self.mine, count, skip), self.cols]

    def send(self, ref, step):
        to = self.l.ring(self.ring, step) if step else self.l.other(self.pair)
        return self.l.copy(ref, ref, to)

    def start(self):
        own = self.at(0)
        self.own_p = self.send(own, 1)
        self.own_m = self.send(own, -1)
        self.y0 = self.send(own, 0)

    def onward_p(self):
        self.far_p = self.send(self.at(-1, BLK // 2), 1)
        self.yp = self.send(self.at(-1), 0)

    def onward_m(self):
        self.far_m = self.send(self.at(1, BLK // 2, BLK // 2), -1)
        self.ym = self.send(self.at(1), 0)

    def across_p(self):
        self.yfp = self.send(self.at(2, BLK // 2), 0)

    def across_m(self):
        self.yfm = self.send(self.at(2, BLK // 2, BLK // 2), 0)

    def arrived(self, step):
        if step == 0:
            return [self.y0]
        if step == 2:
            return [self.yfp, self.yfm]
        return [self.yp] if step == -1 else [self.ym]

    def tasks(self, t, name, after):
        t.add(name + "0", after, lambda: [], self.start)
        t.add(name + "p", [name + "0"], lambda: [self.own_p], self.onward_p)
        t.add(name + "m", [name + "0"], lambda: [self.own_m], self.onward_m)
        t.add(name + "yp", [name + "p"], lambda: [self.far_p], self.across_p)
        t.add(name + "ym", [name + "m"], lambda: [self.far_m], self.across_m)


class ReduceRingFirst:
    def __init__(self, links, ring, pair, part, out, col, out_col, width, slots):
        self.l, self.ring, self.pair = links, ring, pair
        self.part, self.out, self.col, self.width, self.slots = part, out, col, width, slots
        self.out_cols = pl.ds(out_col, width)
        self.mine = getattr(links, pair)

    def block(self, step, member):
        return self.out.at[rows_of(self.l.place(self.ring, step), member), self.out_cols]

    def plan(self):
        l = self.l
        self.p2 = l.plan(self.block(2, 0), self.slots.at[0], l.ring(self.ring, 1))
        self.m2 = l.plan(self.block(2, 1), self.slots.at[1], l.ring(self.ring, -1))
        self.p1 = l.plan(self.block(1, 1), self.slots.at[2], l.ring(self.ring, 1))
        self.m1 = l.plan(self.block(-1, 0), self.slots.at[3], l.ring(self.ring, -1))

    def sent(self):
        for c in (self.p2, self.m2, self.p1, self.m1):
            c.start()

    def sent_pair(self, place):
        step = lax.rem(place - getattr(self.l, self.ring) + 4, 4)

        @pl.when(step == 2)
        def _():
            self.p2.start()
            self.m2.start()

        @pl.when(step == 1)
        def _():
            self.p1.start()

        @pl.when(step == 3)
        def _():
            self.m1.start()

    def add(self, dst, start, *slots):
        def body(r):
            total = self.part[pl.ds(start + r, ROWS), pl.ds(self.col, self.width)]
            for s in slots:
                total = total + self.slots[s, pl.ds(r, ROWS), :].astype(F32)
            dst(r, total)

        row_loop(BLK, ROWS, body)

    def start_of(self, step, member):
        return pl.multiple_of(self.l.place(self.ring, step) * (2 * BLK) + member * BLK, BLK)

    def to_slot(self, slot):
        def put(r, total):
            self.slots[slot, pl.ds(r, ROWS), :] = total.astype(BF16)

        return put

    def combine_p(self):
        self.add(self.to_slot(7), self.start_of(1, 0), 0)
        self.pc = self.l.copy(self.slots.at[7], self.slots.at[4], self.l.ring(self.ring, 1))

    def combine_m(self):
        self.add(self.to_slot(8), self.start_of(-1, 1), 1)
        self.mc = self.l.copy(self.slots.at[8], self.slots.at[5], self.l.ring(self.ring, -1))

    def across(self):
        for member, slots in ((0, (4, 3)), (1, (2, 5))):
            start = self.start_of(0, member)

            def put(r, total, start=start):
                self.part[pl.ds(start + r, ROWS), pl.ds(self.col, self.width)] = total

            self.add(put, start, *slots)
        self.add(self.to_slot(9), self.start_of(0, 1 - self.mine))
        self.y = self.l.copy(self.slots.at[9], self.slots.at[6], self.l.other(self.pair))

    def tasks(self, t, name, put, after, final):
        t.add(name + "p", [after], lambda: [self.p2], self.combine_p)
        t.add(name + "m", [after], lambda: [self.m2], self.combine_m)
        t.add(
            name + "y", [after, name + "p", name + "m"],
            lambda: [self.p1, self.m1, self.pc, self.mc], self.across,
        )
        t.add(
            name + "f", [name + "y"] + final, lambda: [self.y],
            lambda: self.add(put, self.start_of(0, self.mine), 6),
        )


class ReducePairFirst:
    def __init__(self, links, ring, pair, part, out, col, width, slots, halves):
        self.l, self.ring, self.pair = links, ring, pair
        self.part, self.out, self.col, self.width = part, out, col, width
        self.slots, self.halves = slots, halves
        self.mine = getattr(links, pair)

    def plan(self):
        self.y = [self.to_pair(self.l.place("x", i), i) for i in range(4)]
        self.first = self.l.used - 4

    def to_pair(self, place, i, slot=None):
        block = self.out.at[rows_of(place, 1 - self.mine), pl.ds(self.col, self.width)]
        return self.l.plan(block, self.slots.at[i], self.l.other(self.pair), slot)

    def from_x(self, step):
        return lax.rem(self.l.place(self.ring, step) - self.l.x + 4, 4)

    def came(self, step):
        i = self.from_x(step)
        return [self.to_pair(self.l.place(self.ring, step), i, self.first + i)]

    def add(self, dst, step, skip, count, *halves):
        start = pl.multiple_of(self.l.place(self.ring, step) * (2 * BLK) + self.mine * BLK + skip, 64)
        slot = self.from_x(step)

        def body(r):
            total = self.part[pl.ds(start + r, ROWS), pl.ds(self.col, self.width)]
            total = total + self.slots[slot, pl.ds(skip + r, ROWS), :].astype(F32)
            for h in halves:
                total = total + self.halves[h, pl.ds(r, ROWS), :].astype(F32)
            dst(r, total)

        row_loop(count, ROWS, body)

    def to_half(self, half):
        def put(r, total):
            self.halves[half, pl.ds(r, ROWS), :] = total.astype(BF16)

        return put

    def ring_copy(self, src, dst, step):
        return self.l.copy(src, self.halves.at[dst], self.l.ring(self.ring, step))

    def far(self):
        def put(r, total):
            self.slots[4, pl.ds(r, ROWS), :] = total.astype(BF16)

        self.add(put, 2, 0, BLK)
        self.p2 = self.ring_copy(self.slots.at[4, pl.ds(0, BLK // 2)], 0, 1)
        self.m2 = self.ring_copy(self.slots.at[4, pl.ds(BLK // 2, BLK // 2)], 1, -1)

    def near_p(self):
        self.add(self.to_half(6), 1, BLK // 2, BLK // 2)
        self.p1 = self.ring_copy(self.halves.at[6], 2, 1)

    def near_m(self):
        self.add(self.to_half(7), -1, 0, BLK // 2)
        self.m1 = self.ring_copy(self.halves.at[7], 3, -1)

    def combine_p(self):
        self.add(self.to_half(8), 1, 0, BLK // 2, 0)
        self.pc = self.ring_copy(self.halves.at[8], 4, 1)

    def combine_m(self):
        self.add(self.to_half(9), -1, BLK // 2, BLK // 2, 1)
        self.mc = self.ring_copy(self.halves.at[9], 5, -1)

    def finish(self, put):
        half = BLK // 2
        self.add(put, 0, 0, half, 4, 3)
        self.add(lambda r, total: put(half + r, total), 0, half, half, 2, 5)

    def tasks(self, t, name, put, after, final):
        t.add(name + "2", [after], lambda: self.came(2), self.far)
        t.add(name + "1", [after], lambda: self.came(1), self.near_p)
        t.add(name + "3", [after], lambda: self.came(-1), self.near_m)
        t.add(name + "p", [name + "2", name + "1"], lambda: [self.p2], self.combine_p)
        t.add(name + "m", [name + "2", name + "3"], lambda: [self.m2], self.combine_m)
        t.add(
            name + "f", [after, name + "p", name + "m"] + final,
            lambda: self.came(0) + [self.p1, self.m1, self.pc, self.mc],
            lambda: self.finish(put),
        )


class Tasks:
    def __init__(self, links):
        self.l, self.all = links, {}

    def add(self, name, after, waits, do):
        self.all[name] = (after, waits, do)

    def step(self, name):
        _, waits, do = self.all[name]
        for c in waits():
            self.l.take(c)
        do()


ORDER = (
    "t0", "tp", "t1", "ts0", "c0", "hpart0", "ts1", "tm", "ts-1", "cp", "c1", "cs0", "hpart1", "ts2",
    "hpart-1", "cs1", "hpart2", "cs-1", "cm", "turn", "gpart0", "gpart1", "cs2", "gpart-1", "hb1", "gpart2",
    "hap", "hb3", "ham", "hb2", "gam", "gap", "gb1", "hay", "hbp", "gb3", "hbm", "gb2", "gay", "haf", "hA0",
    "hbf", "hB0", "gbp", "gaf", "gbm", "hBm", "gA0", "hAp", "hA1", "hBp", "ox0", "gbf", "gB0", "gA1", "hAm",
    "hBym", "ox1", "ox-1", "hByp", "gBm", "ix0", "om0", "om-1", "gBp", "im0", "om1", "gAp", "gAm", "ox2",
    "ix1", "gBym", "go0", "om2", "or", "gByp", "ix-1", "go1", "odp", "im-1", "odm", "ix2", "im1", "im2", "ir",
    "ody", "go", "gj0", "gj", "idp", "idm", "odf", "gi0", "o", "gi", "idy", "idf", "i",
)


def run_tasks(t):
    done = set()
    for name in ORDER:
        assert done.issuperset(t.all[name][0]), name
        t.step(name)
        done.add(name)
    assert len(done) == len(t.all)


def dot(a, b, left, right):
    return lax.dot_general(a, b, (((left,), (right,)), ((), ())), preferred_element_type=F32)


STEPS = (2, 1, -1, 0)
ARRIVAL = (0, 1, -1, 2)


def kernel(
    tok_in, wi_in, wo_in, cot_in,
    out_ref, gt_ref, gi_ref, go_ref,
    tok, cot, wi, wo,
    part_h, part_g, send_h, send_g,
    ra_h, ra_g, rb_h, rb_g, rh_h, rh_g,
    hid, acts, ghid,
    sib_in, rbuf, rd,
    gi, go, final, turned,
    send, recv, local,
):
    l = Links(send, recv)
    t = Tasks(l)
    k = l.k
    sib = l.other("k")

    barrier = pltpu.get_barrier_semaphore()
    near = [sib, l.other("yl"), l.other("yh")]
    near += [l.ring(a, s) for a in ("z", "x") for s in (1, -1)]
    for d in near:
        pl.semaphore_signal(barrier, inc=1, device_id=d, device_id_type=pl.DeviceIdType.MESH)

    my_d = pl.ds(pl.multiple_of(k * DC, 128), DC)
    its_d = pl.ds(pl.multiple_of((1 - k) * DC, 128), DC)
    my_f = pl.ds(pl.multiple_of(k * FH, 128), FH)
    its_f = pl.ds(pl.multiple_of((1 - k) * FH, 128), FH)
    own_rows = rows_of(l.x, l.yh)

    load_tok = pltpu.make_async_copy(tok_in, tok.at[own_rows, my_d], local.at[0])
    load_cot = pltpu.make_async_copy(cot_in, cot.at[own_rows, my_d], local.at[1])
    load_wi = pltpu.make_async_copy(wi_in.at[:, my_f], wi.at[my_d], local.at[2])
    load_wo = pltpu.make_async_copy(wo_in.at[my_f], wo.at[:, my_d], local.at[3])
    for c in (load_tok, load_wi, load_cot, load_wo):
        c.start()
    pl.semaphore_wait(barrier, len(near))

    def pair_rows(axis, step):
        return pl.ds(pl.multiple_of(l.place(axis, step) * (2 * BLK), 2 * BLK), 2 * BLK)

    shared = {}

    def gather_tokens(name, buf, source, load, weight, target, after):
        g = GatherRingLast(l, "x", "yh", buf, my_d, source)

        def start():
            g.start()
            shared[name + "w"] = l.copy(weight, target, sib)

        g.tasks(t, name, after)
        t.add(name + "0", after, lambda: [], start)

        def share(step):
            def do():
                if step == 0:
                    load.wait()
                ref = buf.at[pair_rows("x", step), my_d]
                shared[name + str(step)] = l.copy(ref, ref, sib)

            return do

        for step, before in ((0, ["1"]), (1, ["1"]), (-1, ["1"]), (2, ["p", "m"])):
            t.add(
                name + "s" + str(step), [name + b for b in before],
                lambda step=step: g.arrived(step), share(step),
            )

    gather_tokens("t", tok, tok_in, load_tok, wi_in.at[:, its_f], wi.at[my_d], [])
    gather_tokens("c", cot, cot_in, load_cot, wo_in.at[its_f], wo.at[:, my_d], ["t1"])

    def put_hidden(col, width):
        cols = pl.ds(col, width)

        def put(r, h):
            hid[pl.ds(r, ROWS), cols] = h
            tanh = jnp.tanh(C_GELU * (h + C_CUBE * (h * h * h)))
            acts[pl.ds(own + r, ROWS), cols] = (0.5 * h * (1.0 + tanh)).astype(BF16)

        return put

    def put_grad(col, width):
        cols = pl.ds(col, width)

        def put(r, total):
            h = hid[pl.ds(r, ROWS), cols]
            square = h * h
            tanh = jnp.tanh(C_GELU * (h + C_CUBE * (square * h)))
            slope = 0.5 * (1.0 + tanh)
            slope += (0.5 * C_GELU) * h * (1.0 - tanh * tanh) * (1.0 + 3.0 * C_CUBE * square)
            ghid[pl.ds(own + r, ROWS), cols] = (total * slope).astype(BF16)

        return put

    own = pl.multiple_of(l.z * (2 * BLK) + l.yl * BLK, BLK)

    def reduction(name, source, load, product, part, out, slots_a, slots_b, halves, put, gathered, final):
        ring = ReduceRingFirst(l, "z", "yl", part, out, 0, 0, FA, slots_a)
        pair = ReducePairFirst(l, "z", "yl", part, out, FA, FB, slots_b, halves)

        def partial(step):
            def do():
                if step == ARRIVAL[0]:
                    load.wait()
                    ring.plan()
                    pair.plan()
                rows = pair_rows("x", step)

                def tile(n):
                    cols = pl.ds(pl.multiple_of(n * 256, 256), 256)
                    total = product(rows, cols)
                    part[rows, cols] = total
                    out[rows, cols] = total.astype(BF16)

                tiles(FH // 256, tile)
                pair.y[step % 4].start()
                ring.sent_pair(l.place("x", step))

            return do

        for i, step in enumerate(ARRIVAL):
            before = [source + "s" + str(step)] + [name + "part" + str(ARRIVAL[i - 1])] * (i > 0)
            t.add(
                name + "part" + str(step), before,
                lambda step=step: [shared[source + "w"], shared[source + str(step)]], partial(step),
            )
        last = name + "part" + str(ARRIVAL[-1])
        ring.tasks(t, name + "a", put(0, FA), last, [f + "af" for f in final])
        pair.tasks(t, name + "b", put(FA, FB), last, [f + "bf" for f in final])
        a = GatherRingLast(l, "z", "yl", gathered, pl.ds(0, FA))
        b = GatherRingFirst(l, "z", "yl", gathered, pl.ds(FA, FB))
        a.tasks(t, name + "A", [name + "af"])
        b.tasks(t, name + "B", [name + "bf"])
        return a, b

    gathers_h = reduction(
        "h", "t", load_wi, lambda rows, cols: dot(tok[rows, :], wi[:, cols], 1, 0),
        part_h, send_h, ra_h, rb_h, rh_h, put_hidden, acts, [],
    )
    gathers_g = reduction(
        "g", "c", load_wo, lambda rows, cols: dot(cot[rows, :], wo[cols, :], 1, 1),
        part_g, send_g, ra_g, rb_g, rh_g, put_grad, ghid, ["h"],
    )

    merged = {}

    def projection(name, which, before, gathers, part, lhs, weight, right, target):
        final_sum = ReduceRingFirst(l, "x", "yh", part, rbuf.at[which], DP, 0, DC, rd.at[which])

        def project(step):
            def do():
                rows = pair_rows("z", step)

                def tile(n):
                    cols = pl.ds(pl.multiple_of(n * 256, 256), 256)
                    part[rows, cols] = dot(lhs[rows, :], weight[(cols, slice(None))[::2 * right - 1]], 1, right)

                tiles(DP // 256, tile)
                merged[name + str(step)] = l.copy(part.at[rows, its_d], sib_in.at[which, rows], sib)

            return do

        def merge(step):
            def do():
                start = pl.multiple_of(l.place("z", step) * (2 * BLK), 2 * BLK)

                def body(r):
                    at = pl.ds(start + r, ROWS)
                    total = part[at, my_d] + sib_in[which, at, :]
                    part[at, pl.ds(DP, DC)] = total
                    rbuf[which, at, :] = total.astype(BF16)

                row_loop(2 * BLK, ROWS, body)

            return do

        for step, need in ((0, ["A1", "B0"]), (1, ["A1", "Bm"]), (-1, ["A1", "Bp"]), (2, ["Ap", "Am", "Byp", "Bym"])):
            t.add(
                name + "x" + str(step), [before + n for n in need] + [before + "af", before + "bf"],
                lambda step=step: gathers[0].arrived(step) + gathers[1].arrived(step), project(step),
            )
            t.add(
                name + "m" + str(step), [name + "x" + str(step)],
                lambda step=step: [merged[name + str(step)]], merge(step),
            )

        def go_round():
            final_sum.plan()
            final_sum.sent()

        merges = [name + "m" + str(s) for s in STEPS]
        t.add(name + "r", merges, lambda: [], go_round)

        def put(r, total):
            final[which, pl.ds(r, ROWS), :] = total.astype(BF16)

        final_sum.tasks(t, name + "d", put, name + "r", [])
        return pltpu.make_async_copy(final.at[which], target, local.at[4 + which])

    out_done = projection("o", 0, "h", gathers_h, part_h, acts, wo, 0, out_ref)
    gt_done = projection("i", 1, "g", gathers_g, part_g, ghid, wi, 1, gt_ref)
    t.add("o", ["odf"], lambda: [], out_done.start)
    t.add("i", ["idf"], lambda: [], gt_done.start)

    whole_h = ["ox" + str(s) for s in STEPS] + ["cs" + str(s) for s in STEPS]
    whole_g = ["ix" + str(s) for s in STEPS]

    def grad_out_tiles(half):
        def tile(n):
            cols = pl.ds(pl.multiple_of(half * (FH // 2) + n * 256, 256), 256)
            go[cols, :] = dot(acts[:, cols], cot[...], 0, 0).astype(BF16)

        return lambda: tiles(FH // 512, tile)

    for half in range(2):
        t.add("go" + str(half), whole_h + ["gpart2"], lambda: [], grad_out_tiles(half))
    go_done = pltpu.make_async_copy(go.at[:, my_d], go_ref.at[my_f], local.at[6])
    gi_done = pltpu.make_async_copy(gi.at[my_d], gi_ref.at[:, my_f], local.at[7])
    ends = []

    def send_go():
        go_done.start()
        ends.append(l.copy(go.at[:, its_d], go_ref.at[my_f], sib))

    t.add("go", ["go0", "go1"], lambda: [], send_go)

    def turn_tokens():
        def tile(n):
            cols = pl.ds(pl.multiple_of(n * 128, 128), 128)
            turned[cols, :] = tok[:, cols].T

        tiles(DP // 128, tile)

    t.add("turn", ["hpart2"], lambda: [], turn_tokens)

    def grad_in_tiles(rows):
        def tile(n):
            cols = pl.ds(pl.multiple_of(n * 256, 256), 256)
            gi[rows, cols] = dot(turned[rows, :], ghid[:, cols], 1, 0).astype(BF16)

        return lambda: tiles(FH // 256, tile)

    t.add("gi0", whole_g + ["turn"], lambda: [], grad_in_tiles(its_d))
    t.add("gj0", whole_g + ["turn"], lambda: [], grad_in_tiles(my_d))
    t.add("gi", ["gi0"], lambda: [], lambda: ends.append(l.copy(gi.at[its_d], gi_ref.at[:, my_f], sib)))
    t.add("gj", ["gj0"], lambda: [], gi_done.start)

    run_tasks(t)

    for c in ends:
        l.take(c)
    for c in (go_done, gi_done, out_done, gt_done):
        c.wait()
    for c in l.started:
        c.wait_send()


def hand_over(*refs):
    results, targets, held, (arrive, leave) = refs[:4], refs[4:8], refs[8:12], refs[12:]
    ins, outs = [], []
    for src, dst, mid in zip(results, targets, held):
        parts = 4 if src.shape[0] > BLK else 1
        rows = src.shape[0] // parts
        for p in range(parts):
            at, i = pl.ds(p * rows, rows), len(ins)
            ins.append(pltpu.make_async_copy(src.at[at], mid.at[at], arrive.at[i]))
            outs.append(pltpu.make_async_copy(mid.at[at], dst.at[at], leave.at[i]))
    for c in ins:
        c.start()
    for c, d in zip(ins, outs):
        c.wait()
        d.start()
    for d in outs:
        d.wait()


def local(tokens, weight_in, weight_out, cotangent):
    results = block(tokens, weight_in, weight_out, cotangent)
    any_space = pl.BlockSpec(memory_space=pl.ANY)
    return pl.pallas_call(
        hand_over,
        out_shape=tuple(jax.ShapeDtypeStruct(r.shape, r.dtype) for r in results),
        in_specs=[any_space] * 4,
        out_specs=(any_space,) * 4,
        scratch_shapes=[pltpu.VMEM(r.shape, r.dtype) for r in results] + [pltpu.SemaphoreType.DMA((10,))] * 2,
        compiler_params=pltpu.CompilerParams(vmem_limit_bytes=60 * 1024 * 1024),
    )(*results)


def block(tokens, weight_in, weight_out, cotangent):
    any_space = pl.BlockSpec(memory_space=pl.ANY)
    shape = jax.ShapeDtypeStruct
    vmem = pltpu.VMEM
    return pl.pallas_call(
        kernel,
        out_shape=(
            shape((BLK, DC), BF16),
            shape((BLK, DC), BF16),
            shape((DC, 2 * FH), BF16),
            shape((2 * FH, DC), BF16),
        ),
        in_specs=[any_space] * 4,
        out_specs=(any_space,) * 4,
        scratch_shapes=[
            vmem((TOK, DP), BF16), vmem((TOK, DP), BF16), vmem((DP, FH), BF16), vmem((FH, DP), BF16),
            vmem((TOK, FH), F32), vmem((TOK, FH), F32), vmem((TOK, FH), BF16), vmem((TOK, FH), BF16),
            vmem((10, BLK, FA), BF16), vmem((10, BLK, FA), BF16),
            vmem((5, BLK, FB), BF16), vmem((5, BLK, FB), BF16),
            vmem((10, BLK // 2, FB), BF16), vmem((10, BLK // 2, FB), BF16),
            vmem((BLK, FH), F32), vmem((TOK, FH), BF16), vmem((TOK, FH), BF16),
            vmem((2, TOK, DC), F32), vmem((2, TOK, DC), BF16),
            vmem((2, 10, BLK, DC), BF16),
            vmem((DP, FH), BF16), vmem((FH, DP), BF16), vmem((2, BLK, DC), BF16), vmem((DP, TOK), BF16),
            pltpu.SemaphoreType.DMA((COPIES,)), pltpu.SemaphoreType.DMA((COPIES,)),
            pltpu.SemaphoreType.DMA((8,)),
        ],
        compiler_params=pltpu.CompilerParams(
            collective_id=0, has_side_effects=True, vmem_limit_bytes=60 * 1024 * 1024
        ),
        cost_estimate=pl.CostEstimate(flops=14_500_000_000, bytes_accessed=12_000_000, transcendentals=400_000),
    )(tokens, weight_in, weight_out, cotangent)


def solution(mesh):
    placed = (P("row", "col"), P("col", "row"), P("row", "col"), P("row", "col"))
    return jax.shard_map(
        local,
        mesh=mesh,
        in_specs=placed,
        out_specs=(P("row", "col"), P("row", "col"), P("col", "row"), P("row", "col")),
        check_vma=False,
    )
```

```python
import functools

import jax
import jax.numpy as jnp
from jax import lax
from jax.experimental import pallas as pl
from jax.experimental.pallas import tpu as pltpu
from jax.sharding import PartitionSpec as P

F32 = jnp.float32
BF16 = jnp.bfloat16

TOK = 1024
BLK = 128
DC = 384
DP = 2 * DC
FH = 1536
FA_H = 768
FA_G = 896
FA_D = 256

COPIES = 128
ROWS = 16
C_GELU = 0.7978845608028654
C_CUBE = 0.044715


def row_loop(rows, chunk, body):
    def step(i, carry):
        body(pl.multiple_of(i * chunk, chunk))
        return carry

    lax.fori_loop(0, rows // chunk, step, 0)


def tiles(count, body):
    def step(i, carry):
        body(i)
        return carry

    lax.fori_loop(0, count, step, 0)


class Links:
    def __init__(self, send, recv):
        self.send, self.recv, self.used = send, recv, 0
        self.started, self.taken = [], []
        row, col = lax.axis_index("row"), lax.axis_index("col")
        self.x, self.yh = row // 2, row % 2
        self.yl, self.z, self.k = col // 8, (col // 2) % 4, col % 2

    def device(self, **moved):
        at = {n: moved.get(n, getattr(self, n)) for n in ("x", "yh", "yl", "z", "k")}
        return (at["x"] * 2 + at["yh"], at["yl"] * 8 + at["z"] * 2 + at["k"])

    def ring(self, axis, step):
        return self.device(**{axis: lax.rem(getattr(self, axis) + step + 4, 4)})

    def other(self, axis):
        return self.device(**{axis: 1 - getattr(self, axis)})

    def copy(self, src, dst, device):
        c = self.plan(src, dst, device)
        c.start()
        return c

    def plan(self, src, dst, device, slot=None):
        i = self.used if slot is None else slot
        self.used += slot is None
        c = pltpu.make_async_remote_copy(
            src_ref=src,
            dst_ref=dst,
            send_sem=self.send.at[i],
            recv_sem=self.recv.at[i],
            device_id=device,
            device_id_type=pl.DeviceIdType.MESH,
        )
        if slot is None:
            self.started.append(c)
        return c

    def take(self, c):
        if all(c is not d for d in self.taken):
            c.wait_recv()
            self.taken.append(c)

    def place(self, axis, step):
        return lax.rem(getattr(self, axis) + step + 4, 4)


def rows_of(place, member, count=BLK, skip=0):
    return pl.ds(pl.multiple_of(place * (2 * BLK) + member * BLK + skip, 16), count)


class GatherRingLast:
    def __init__(self, links, ring, pair, buf, cols, source=None):
        self.l, self.ring, self.pair, self.buf, self.cols = links, ring, pair, buf, cols
        self.mine, self.source = getattr(links, pair), source

    def at(self, step, member):
        return self.buf.at[rows_of(self.l.place(self.ring, step), member), self.cols]

    def send(self, ref, step, source=None):
        to = self.l.ring(self.ring, step) if step else self.l.other(self.pair)
        return self.l.copy(ref if source is None else source, ref, to)

    def start(self):
        own = self.at(0, self.mine)
        self.y = self.send(own, 0, self.source)
        self.own_p = self.send(own, 1, self.source)
        self.own_m = self.send(own, -1, self.source)

    def second(self):
        theirs = self.at(0, 1 - self.mine)
        self.oth_p = self.send(theirs, 1)
        self.oth_m = self.send(theirs, -1)

    def onward_p(self):
        self.far_p = self.send(self.at(-1, self.mine), 1)

    def onward_m(self):
        self.far_m = self.send(self.at(1, 1 - self.mine), -1)

    def arrived(self, step):
        if step == 0:
            return [self.y]
        if step == 2:
            return [self.far_p, self.far_m]
        return [self.own_p, self.oth_p] if step == -1 else [self.own_m, self.oth_m]

    def tasks(self, t, name, after):
        t.add(name + "0", after, lambda: [], self.start)
        t.add(name + "1", [name + "0"], lambda: [self.y], self.second)
        t.add(name + "p", [name + "0"], lambda: [self.own_p], self.onward_p)
        t.add(name + "m", [name + "1"], lambda: [self.oth_m], self.onward_m)


class GatherRingFirst:
    def __init__(self, links, ring, pair, buf, cols):
        self.l, self.ring, self.pair, self.buf, self.cols = links, ring, pair, buf, cols
        self.mine = getattr(links, pair)

    def at(self, step, count=BLK, skip=0):
        return self.buf.at[rows_of(self.l.place(self.ring, step), self.mine, count, skip), self.cols]

    def send(self, ref, step):
        to = self.l.ring(self.ring, step) if step else self.l.other(self.pair)
        return self.l.copy(ref, ref, to)

    def start(self):
        own = self.at(0)
        self.own_p = self.send(own, 1)
        self.own_m = self.send(own, -1)
        self.y0 = self.send(own, 0)

    def onward_p(self):
        self.far_p = self.send(self.at(-1, BLK // 2), 1)
        self.yp = self.send(self.at(-1), 0)

    def onward_m(self):
        self.far_m = self.send(self.at(1, BLK // 2, BLK // 2), -1)
        self.ym = self.send(self.at(1), 0)

    def across_p(self):
        self.yfp = self.send(self.at(2, BLK // 2), 0)

    def across_m(self):
        self.yfm = self.send(self.at(2, BLK // 2, BLK // 2), 0)

    def arrived(self, step):
        if step == 0:
            return [self.y0]
        if step == 2:
            return [self.yfp, self.yfm]
        return [self.yp] if step == -1 else [self.ym]

    def tasks(self, t, name, after):
        t.add(name + "0", after, lambda: [], self.start)
        t.add(name + "p", [name + "0"], lambda: [self.own_p], self.onward_p)
        t.add(name + "m", [name + "0"], lambda: [self.own_m], self.onward_m)
        t.add(name + "yp", [name + "p"], lambda: [self.far_p], self.across_p)
        t.add(name + "ym", [name + "m"], lambda: [self.far_m], self.across_m)


class ReduceRingFirst:
    def __init__(self, links, ring, pair, part, out, col, out_col, width, slots):
        self.l, self.ring, self.pair = links, ring, pair
        self.part, self.out, self.col, self.width, self.slots = part, out, col, width, slots
        self.out_cols = pl.ds(out_col, width)
        self.mine = getattr(links, pair)

    def block(self, step, member):
        return self.out.at[rows_of(self.l.place(self.ring, step), member), self.out_cols]

    def plan(self):
        l = self.l
        self.p2 = l.plan(self.block(2, 0), self.slots.at[0], l.ring(self.ring, 1))
        self.m2 = l.plan(self.block(2, 1), self.slots.at[1], l.ring(self.ring, -1))
        self.p1 = l.plan(self.block(1, 1), self.slots.at[2], l.ring(self.ring, 1))
        self.m1 = l.plan(self.block(-1, 0), self.slots.at[3], l.ring(self.ring, -1))

    def sent(self):
        for c in (self.p2, self.m2, self.p1, self.m1):
            c.start()

    def sent_pair(self, place):
        step = lax.rem(place - getattr(self.l, self.ring) + 4, 4)

        @pl.when(step == 2)
        def _():
            self.p2.start()
            self.m2.start()

        @pl.when(step == 1)
        def _():
            self.p1.start()

        @pl.when(step == 3)
        def _():
            self.m1.start()

    def add(self, dst, start, *slots):
        def body(r):
            total = self.part[pl.ds(start + r, ROWS), pl.ds(self.col, self.width)]
            for s in slots:
                total = total + self.slots[s, pl.ds(r, ROWS), :].astype(F32)
            dst(r, total)

        row_loop(BLK, ROWS, body)

    def start_of(self, step, member):
        return pl.multiple_of(self.l.place(self.ring, step) * (2 * BLK) + member * BLK, BLK)

    def to_slot(self, slot):
        def put(r, total):
            self.slots[slot, pl.ds(r, ROWS), :] = total.astype(BF16)

        return put

    def combine_p(self):
        self.add(self.to_slot(7), self.start_of(1, 0), 0)
        self.pc = self.l.copy(self.slots.at[7], self.slots.at[4], self.l.ring(self.ring, 1))

    def combine_m(self):
        self.add(self.to_slot(8), self.start_of(-1, 1), 1)
        self.mc = self.l.copy(self.slots.at[8], self.slots.at[5], self.l.ring(self.ring, -1))

    def across(self):
        for member, slots in ((0, (4, 3)), (1, (2, 5))):
            start = self.start_of(0, member)

            def put(r, total, start=start):
                self.part[pl.ds(start + r, ROWS), pl.ds(self.col, self.width)] = total

            self.add(put, start, *slots)
        self.add(self.to_slot(9), self.start_of(0, 1 - self.mine))
        self.y = self.l.copy(self.slots.at[9], self.slots.at[6], self.l.other(self.pair))

    def tasks(self, t, name, put, after, final):
        t.add(name + "p", [after], lambda: [self.p2], self.combine_p)
        t.add(name + "m", [after], lambda: [self.m2], self.combine_m)
        t.add(
            name + "y", [after, name + "p", name + "m"],
            lambda: [self.p1, self.m1, self.pc, self.mc], self.across,
        )
        t.add(
            name + "f", [name + "y"] + final, lambda: [self.y],
            lambda: self.add(put, self.start_of(0, self.mine), 6),
        )


class ReducePairFirst:
    def __init__(self, links, ring, pair, part, out, col, out_col, width, slots, halves):
        self.l, self.ring, self.pair = links, ring, pair
        self.part, self.out, self.col, self.width = part, out, col, width
        self.out_cols = pl.ds(out_col, width)
        self.slots, self.halves = slots, halves
        self.mine = getattr(links, pair)

    def plan(self):
        self.y = [self.to_pair(self.l.place("x", i), i) for i in range(4)]
        self.first = self.l.used - 4

    def to_pair(self, place, i, slot=None):
        block = self.out.at[rows_of(place, 1 - self.mine), self.out_cols]
        return self.l.plan(block, self.slots.at[i], self.l.other(self.pair), slot)

    def from_x(self, step):
        return lax.rem(self.l.place(self.ring, step) - self.l.x + 4, 4)

    def came(self, step):
        i = self.from_x(step)
        return [self.to_pair(self.l.place(self.ring, step), i, self.first + i)]

    def add(self, dst, step, skip, count, *halves):
        start = pl.multiple_of(self.l.place(self.ring, step) * (2 * BLK) + self.mine * BLK + skip, 64)
        slot = self.from_x(step)

        def body(r):
            total = self.part[pl.ds(start + r, ROWS), pl.ds(self.col, self.width)]
            total = total + self.slots[slot, pl.ds(skip + r, ROWS), :].astype(F32)
            for h in halves:
                total = total + self.halves[h, pl.ds(r, ROWS), :].astype(F32)
            dst(r, total)

        row_loop(count, ROWS, body)

    def to_half(self, half):
        def put(r, total):
            self.halves[half, pl.ds(r, ROWS), :] = total.astype(BF16)

        return put

    def ring_copy(self, src, dst, step):
        return self.l.copy(src, self.halves.at[dst], self.l.ring(self.ring, step))

    def far(self):
        def put(r, total):
            self.slots[4, pl.ds(r, ROWS), :] = total.astype(BF16)

        self.add(put, 2, 0, BLK)
        self.p2 = self.ring_copy(self.slots.at[4, pl.ds(0, BLK // 2)], 0, 1)
        self.m2 = self.ring_copy(self.slots.at[4, pl.ds(BLK // 2, BLK // 2)], 1, -1)

    def near_p(self):
        self.add(self.to_half(6), 1, BLK // 2, BLK // 2)
        self.p1 = self.ring_copy(self.halves.at[6], 2, 1)

    def near_m(self):
        self.add(self.to_half(7), -1, 0, BLK // 2)
        self.m1 = self.ring_copy(self.halves.at[7], 3, -1)

    def combine_p(self):
        self.add(self.to_half(8), 1, 0, BLK // 2, 0)
        self.pc = self.ring_copy(self.halves.at[8], 4, 1)

    def combine_m(self):
        self.add(self.to_half(9), -1, BLK // 2, BLK // 2, 1)
        self.mc = self.ring_copy(self.halves.at[9], 5, -1)

    def finish(self, put):
        half = BLK // 2
        self.add(put, 0, 0, half, 4, 3)
        self.add(lambda r, total: put(half + r, total), 0, half, half, 2, 5)

    def tasks(self, t, name, put, after, final):
        t.add(name + "2", [after], lambda: self.came(2), self.far)
        t.add(name + "1", [after], lambda: self.came(1), self.near_p)
        t.add(name + "3", [after], lambda: self.came(-1), self.near_m)
        t.add(name + "p", [name + "2", name + "1"], lambda: [self.p2], self.combine_p)
        t.add(name + "m", [name + "2", name + "3"], lambda: [self.m2], self.combine_m)
        t.add(
            name + "f", [after, name + "p", name + "m"] + final,
            lambda: self.came(0) + [self.p1, self.m1, self.pc, self.mc],
            lambda: self.finish(put),
        )


class Tasks:
    def __init__(self, links):
        self.l, self.all = links, {}

    def add(self, name, after, waits, do):
        self.all[name] = (after, waits, do)

    def step(self, name):
        _, waits, do = self.all[name]
        for c in waits():
            self.l.take(c)
        do()


ORDER = (
    "t0", "tp", "t1", "ts0", "c0", "ts1", "hpart0", "tm", "ts-1", "c1", "cs0", "hpart1", "ts2", "hpart-1",
    "cm", "cs1", "cp", "hpart2", "cs-1", "gpart0", "gpart1", "cs2", "gpart-1", "turn", "gpart2", "hap", "ham",
    "gam", "hb1", "hb2", "gap", "hay", "hb3", "hbm", "hbp", "gay", "gb3", "gb2", "gb1", "haf", "hbf", "hA0",
    "hB0", "gaf", "gA0", "hBm", "gbp", "gbm", "hBp", "hA1", "gbf", "gB0", "hAm", "hByp", "ox0", "hAp", "ox1",
    "hBym", "ox-1", "gA1", "ix0", "gBm", "om0", "om1", "gBp", "om-1", "ox2", "gAp", "go0", "gAm", "ix1",
    "om2", "or", "gByp", "im0", "gBym", "ix-1", "go1", "odm", "im-1", "ix2", "im1", "odp", "gj0", "im2", "ir",
    "ie1", "ie2", "ie3", "go", "ody", "idm", "idp", "gi0", "gi", "idy", "odf", "iem", "iep", "ief", "idf",
)


def run_tasks(t):
    done = set()
    for name in ORDER:
        assert done.issuperset(t.all[name][0]), name
        t.step(name)
        done.add(name)
    assert len(done) == len(t.all)


def dot(a, b, left, right):
    return lax.dot_general(a, b, (((left,), (right,)), ((), ())), preferred_element_type=F32)


STEPS = (2, 1, -1, 0)
ARRIVAL = (0, 1, -1, 2)


def kernel(
    tok_in, wi_in, wo_in, cot_in,
    out_ref, gt_ref, gi_ref, go_ref,
    tok, cot, wi, wo,
    part_h, part_g, send_h, send_g,
    ra_h, ra_g, rb_h, rb_g, rh_h, rh_g,
    hid, acts, ghid,
    sib_in, rbuf, rd_h, rd_g, re_g, rf_g,
    gi, go, turned,
    send, recv, local,
):
    l = Links(send, recv)
    t = Tasks(l)
    k = l.k
    sib = l.other("k")

    barrier = pltpu.get_barrier_semaphore()
    near = [sib, l.other("yl"), l.other("yh")]
    near += [l.ring(a, s) for a in ("z", "x") for s in (1, -1)]
    for d in near:
        pl.semaphore_signal(barrier, inc=1, device_id=d, device_id_type=pl.DeviceIdType.MESH)

    my_d = pl.ds(pl.multiple_of(k * DC, 128), DC)
    its_d = pl.ds(pl.multiple_of((1 - k) * DC, 128), DC)
    my_f = pl.ds(pl.multiple_of(k * FH, 128), FH)
    its_f = pl.ds(pl.multiple_of((1 - k) * FH, 128), FH)
    own_rows = rows_of(l.x, l.yh)

    load_tok = pltpu.make_async_copy(tok_in, tok.at[own_rows, my_d], local.at[0])
    load_cot = pltpu.make_async_copy(cot_in, cot.at[own_rows, my_d], local.at[1])
    load_wi = pltpu.make_async_copy(wi_in.at[:, my_f], wi.at[my_d], local.at[2])
    load_wo = pltpu.make_async_copy(wo_in.at[my_f], wo.at[:, my_d], local.at[3])
    for c in (load_tok, load_wi, load_cot, load_wo):
        c.start()
    pl.semaphore_wait(barrier, len(near))

    def pair_rows(axis, step):
        return pl.ds(pl.multiple_of(l.place(axis, step) * (2 * BLK), 2 * BLK), 2 * BLK)

    shared = {}

    def gather_tokens(name, buf, source, load, weight, target, after):
        g = GatherRingLast(l, "x", "yh", buf, my_d, source)

        def start():
            g.start()
            shared[name + "w"] = l.copy(weight, target, sib)

        g.tasks(t, name, after)
        t.add(name + "0", after, lambda: [], start)

        def share(step):
            def do():
                if step == 0:
                    load.wait()
                ref = buf.at[pair_rows("x", step), my_d]
                shared[name + str(step)] = l.copy(ref, ref, sib)

            return do

        for step, before in ((0, ["1"]), (1, ["1"]), (-1, ["1"]), (2, ["p", "m"])):
            t.add(
                name + "s" + str(step), [name + b for b in before],
                lambda step=step: g.arrived(step), share(step),
            )

    gather_tokens("t", tok, tok_in, load_tok, wi_in.at[:, its_f], wi.at[my_d], [])
    gather_tokens("c", cot, cot_in, load_cot, wo_in.at[its_f], wo.at[:, my_d], ["t1"])

    def put_hidden(col, width):
        cols = pl.ds(col, width)

        def put(r, h):
            hid[pl.ds(r, ROWS), cols] = h
            tanh = jnp.tanh(C_GELU * (h + C_CUBE * (h * h * h)))
            acts[pl.ds(own + r, ROWS), cols] = (0.5 * h * (1.0 + tanh)).astype(BF16)

        return put

    def put_grad(col, width):
        cols = pl.ds(col, width)

        def put(r, total):
            h = hid[pl.ds(r, ROWS), cols]
            square = h * h
            tanh = jnp.tanh(C_GELU * (h + C_CUBE * (square * h)))
            slope = 0.5 * (1.0 + tanh)
            slope += (0.5 * C_GELU) * h * (1.0 - tanh * tanh) * (1.0 + 3.0 * C_CUBE * square)
            ghid[pl.ds(own + r, ROWS), cols] = (total * slope).astype(BF16)

        return put

    own = pl.multiple_of(l.z * (2 * BLK) + l.yl * BLK, BLK)

    def reduction(name, fa, source, load, product, part, out, slots_a, slots_b, halves, put, gathered, final):
        ring = ReduceRingFirst(l, "z", "yl", part, out, 0, 0, fa, slots_a)
        pair = ReducePairFirst(l, "z", "yl", part, out, fa, fa, FH - fa, slots_b, halves)

        def partial(step):
            def do():
                if step == ARRIVAL[0]:
                    load.wait()
                    ring.plan()
                    pair.plan()
                rows = pair_rows("x", step)

                def tile(n):
                    cols = pl.ds(pl.multiple_of(n * 256, 256), 256)
                    total = product(rows, cols)
                    part[rows, cols] = total
                    out[rows, cols] = total.astype(BF16)

                tiles(FH // 256, tile)
                pair.y[step % 4].start()
                ring.sent_pair(l.place("x", step))

            return do

        for i, step in enumerate(ARRIVAL):
            before = [source + "s" + str(step)] + [name + "part" + str(ARRIVAL[i - 1])] * (i > 0)
            t.add(
                name + "part" + str(step), before,
                lambda step=step: [shared[source + "w"], shared[source + str(step)]], partial(step),
            )
        last = name + "part" + str(ARRIVAL[-1])
        ring.tasks(t, name + "a", put(0, fa), last, final)
        pair.tasks(t, name + "b", put(fa, FH - fa), last, final)
        a = GatherRingLast(l, "z", "yl", gathered, pl.ds(0, fa))
        b = GatherRingFirst(l, "z", "yl", gathered, pl.ds(fa, FH - fa))
        a.tasks(t, name + "A", [name + "af"])
        b.tasks(t, name + "B", [name + "bf"])
        return a, b

    gathers_h = reduction(
        "h", FA_H, "t", load_wi, lambda rows, cols: dot(tok[rows, :], wi[:, cols], 1, 0),
        part_h, send_h, ra_h, rb_h, rh_h, put_hidden, acts, [],
    )
    gathers_g = reduction(
        "g", FA_G, "c", load_wo, lambda rows, cols: dot(cot[rows, :], wo[cols, :], 1, 1),
        part_g, send_g, ra_g, rb_g, rh_g, put_grad, ghid, ["haf", "hbf"],
    )

    merged = {}

    def projection(name, which, before, gathers, part, lhs, weight, right, target, slots, split_slots):
        wide = FA_D if split_slots else DC
        ring = ReduceRingFirst(l, "x", "yh", part, rbuf.at[which], DP, 0, wide, slots)
        pair = split_slots and ReducePairFirst(
            l, "x", "yh", part, rbuf.at[which], DP + wide, wide, DC - wide, *split_slots
        )

        def project(step):
            def do():
                rows = pair_rows("z", step)

                def tile(n):
                    cols = pl.ds(pl.multiple_of(n * 256, 256), 256)
                    part[rows, cols] = dot(lhs[rows, :], weight[(cols, slice(None))[::2 * right - 1]], 1, right)

                tiles(DP // 256, tile)
                merged[name + str(step)] = l.copy(part.at[rows, its_d], sib_in.at[which, rows], sib)

            return do

        def merge(step):
            def do():
                start = pl.multiple_of(l.place("z", step) * (2 * BLK), 2 * BLK)

                def body(r):
                    at = pl.ds(start + r, ROWS)
                    total = part[at, my_d] + sib_in[which, at, :]
                    part[at, pl.ds(DP, DC)] = total
                    rbuf[which, at, :] = total.astype(BF16)

                row_loop(2 * BLK, ROWS, body)

            return do

        for step, need in ((0, ["A1", "B0"]), (1, ["A1", "Bm"]), (-1, ["A1", "Bp"]), (2, ["Ap", "Am", "Byp", "Bym"])):
            t.add(
                name + "x" + str(step), [before + n for n in need] + [before + "af", before + "bf"],
                lambda step=step: gathers[0].arrived(step) + gathers[1].arrived(step), project(step),
            )
            t.add(
                name + "m" + str(step), [name + "x" + str(step)],
                lambda step=step: [merged[name + str(step)]], merge(step),
            )

        def go_round():
            ring.plan()
            ring.sent()
            if pair:
                pair.plan()
                for i in (2, 1, 3, 0):
                    pair.y[i].start()

        merges = [name + "m" + str(s) for s in STEPS]
        t.add(name + "r", merges, lambda: [], go_round)

        def put(col, width):
            def body(r, total):
                target[pl.ds(r, ROWS), pl.ds(col, width)] = total.astype(BF16)

            return body

        ring.tasks(t, name + "d", put(0, wide), name + "r", [])
        if pair:
            pair.tasks(t, name + "e", put(wide, DC - wide), name + "r", [])

    projection("o", 0, "h", gathers_h, part_h, acts, wo, 0, out_ref, rd_h, ())
    projection("i", 1, "g", gathers_g, part_g, ghid, wi, 1, gt_ref, rd_g, (re_g, rf_g))

    whole_h = ["ox" + str(s) for s in STEPS] + ["cs" + str(s) for s in STEPS]
    whole_g = ["ix" + str(s) for s in STEPS]

    def grad_out_tiles(half):
        def tile(n):
            cols = pl.ds(pl.multiple_of(half * (FH // 2) + n * 256, 256), 256)
            go[cols, :] = dot(acts[:, cols], cot[...], 0, 0).astype(BF16)

        return lambda: tiles(FH // 512, tile)

    for half in range(2):
        t.add("go" + str(half), whole_h + ["gpart2"], lambda: [], grad_out_tiles(half))
    ends = []

    def send_go():
        ends.append(l.copy(go.at[:, its_d], go_ref.at[my_f], sib))
        own_start = pl.multiple_of(k * FH, 128)

        def keep(r):
            go_ref[pl.ds(own_start + r, 32), :] = go[pl.ds(r, 32), my_d]

        row_loop(FH, 32, keep)

    t.add("go", ["go0", "go1"], lambda: [], send_go)

    def turn_tokens():
        def tile(n):
            cols = pl.ds(pl.multiple_of(n * 128, 128), 128)
            turned[cols, :] = tok[:, cols].T

        tiles(DP // 128, tile)

    t.add("turn", ["hpart2"], lambda: [], turn_tokens)

    def grad_in_tiles(rows, start, target):
        def tile(n):
            cols = pl.ds(pl.multiple_of(n * 256, 256), 256)
            at = pl.ds(pl.multiple_of(start + n * 256, 128), 256)
            target[:, at] = dot(turned[rows, :], ghid[:, cols], 1, 0).astype(BF16)

        return lambda: tiles(FH // 256, tile)

    t.add("gi0", whole_g + ["turn"], lambda: [], grad_in_tiles(its_d, 0, gi))
    t.add("gj0", whole_g + ["turn"], lambda: [], grad_in_tiles(my_d, k * FH, gi_ref))
    t.add("gi", ["gi0"], lambda: [], lambda: ends.append(l.copy(gi, gi_ref.at[:, my_f], sib)))

    run_tasks(t)

    for c in ends:
        l.take(c)
    for c in l.started:
        c.wait_send()


def hand_over(*refs):
    sems = refs[-1]
    copies = []
    for src, dst in zip(refs[:4], refs[4:8]):
        parts = 4 if src.shape[0] > BLK else 1
        rows = src.shape[0] // parts
        for p in range(parts):
            at = pl.ds(p * rows, rows)
            copies.append(pltpu.make_async_copy(src.at[at], dst.at[at], sems.at[len(copies)]))
    for c in copies:
        c.start()
    for c in copies:
        c.wait()


def local(tokens, weight_in, weight_out, cotangent):
    results = block(tokens, weight_in, weight_out, cotangent)
    any_space = pl.BlockSpec(memory_space=pl.ANY)
    return pl.pallas_call(
        hand_over,
        out_shape=tuple(jax.ShapeDtypeStruct(r.shape, r.dtype) for r in results),
        in_specs=[pl.BlockSpec(memory_space=pltpu.VMEM)] * 4,
        out_specs=(any_space,) * 4,
        scratch_shapes=[pltpu.SemaphoreType.DMA((10,))],
    )(*results)


def block(tokens, weight_in, weight_out, cotangent):
    any_space = pl.BlockSpec(memory_space=pl.ANY)
    shape = jax.ShapeDtypeStruct
    vmem = pltpu.VMEM
    return pl.pallas_call(
        kernel,
        out_shape=(
            vmem((BLK, DC), BF16),
            vmem((BLK, DC), BF16),
            vmem((DC, 2 * FH), BF16),
            vmem((2 * FH, DC), BF16),
        ),
        in_specs=[any_space] * 4,
        out_specs=(pl.BlockSpec(memory_space=pltpu.VMEM),) * 4,
        scratch_shapes=[
            vmem((TOK, DP), BF16), vmem((TOK, DP), BF16), vmem((DP, FH), BF16), vmem((FH, DP), BF16),
            vmem((TOK, FH), F32), vmem((TOK, FH), F32), vmem((TOK, FH), BF16), vmem((TOK, FH), BF16),
            vmem((10, BLK, FA_H), BF16), vmem((10, BLK, FA_G), BF16),
            vmem((5, BLK, FH - FA_H), BF16), vmem((5, BLK, FH - FA_G), BF16),
            vmem((10, BLK // 2, FH - FA_H), BF16), vmem((10, BLK // 2, FH - FA_G), BF16),
            vmem((BLK, FH), F32), vmem((TOK, FH), BF16), vmem((TOK, FH), BF16),
            vmem((2, TOK, DC), F32), vmem((2, TOK, DC), BF16),
            vmem((10, BLK, DC), BF16), vmem((10, BLK, FA_D), BF16),
            vmem((5, BLK, DC - FA_D), BF16), vmem((10, BLK // 2, DC - FA_D), BF16),
            vmem((DC, FH), BF16), vmem((FH, DP), BF16), vmem((DP, TOK), BF16),
            pltpu.SemaphoreType.DMA((COPIES,)), pltpu.SemaphoreType.DMA((COPIES,)),
            pltpu.SemaphoreType.DMA((4,)),
        ],
        compiler_params=pltpu.CompilerParams(
            collective_id=0, has_side_effects=True, vmem_limit_bytes=55 * 1024 * 1024
        ),
        cost_estimate=pl.CostEstimate(flops=14_500_000_000, bytes_accessed=12_000_000, transcendentals=400_000),
    )(tokens, weight_in, weight_out, cotangent)


def solution(mesh):
    placed = (P("row", "col"), P("col", "row"), P("row", "col"), P("row", "col"))
    return jax.shard_map(
        local,
        mesh=mesh,
        in_specs=placed,
        out_specs=(P("row", "col"), P("row", "col"), P("col", "row"), P("row", "col")),
        check_vma=False,
    )
```

```python
import functools

import jax
import jax.numpy as jnp
from jax import lax
from jax.experimental import pallas as pl
from jax.experimental.pallas import tpu as pltpu
from jax.sharding import PartitionSpec as P

F32 = jnp.float32
BF16 = jnp.bfloat16

TOK = 1024
BLK = 128
DC = 384
DP = 2 * DC
FH = 1536
FA_H = 768
FA_G = 896
FA_D = 256

COPIES = 128
ROWS = 16
C_GELU = 0.7978845608028654
C_CUBE = 0.044715


def row_loop(rows, chunk, body):
    def step(i, carry):
        body(pl.multiple_of(i * chunk, chunk))
        return carry

    lax.fori_loop(0, rows // chunk, step, 0)


def tiles(count, body):
    def step(i, carry):
        body(i)
        return carry

    lax.fori_loop(0, count, step, 0)


class Links:
    def __init__(self, send, recv):
        self.send, self.recv, self.used = send, recv, 0
        self.started, self.taken = [], []
        row, col = lax.axis_index("row"), lax.axis_index("col")
        self.x, self.yh = row // 2, row % 2
        self.yl, self.z, self.k = col // 8, (col // 2) % 4, col % 2

    def device(self, **moved):
        at = {n: moved.get(n, getattr(self, n)) for n in ("x", "yh", "yl", "z", "k")}
        return (at["x"] * 2 + at["yh"], at["yl"] * 8 + at["z"] * 2 + at["k"])

    def ring(self, axis, step):
        return self.device(**{axis: lax.rem(getattr(self, axis) + step + 4, 4)})

    def other(self, axis):
        return self.device(**{axis: 1 - getattr(self, axis)})

    def copy(self, src, dst, device):
        c = self.plan(src, dst, device)
        c.start()
        return c

    def plan(self, src, dst, device, slot=None):
        i = self.used if slot is None else slot
        self.used += slot is None
        c = pltpu.make_async_remote_copy(
            src_ref=src,
            dst_ref=dst,
            send_sem=self.send.at[i],
            recv_sem=self.recv.at[i],
            device_id=device,
            device_id_type=pl.DeviceIdType.MESH,
        )
        if slot is None:
            self.started.append(c)
        return c

    def take(self, c):
        if all(c is not d for d in self.taken):
            c.wait_recv()
            self.taken.append(c)

    def place(self, axis, step):
        return lax.rem(getattr(self, axis) + step + 4, 4)


def rows_of(place, member, count=BLK, skip=0):
    return pl.ds(pl.multiple_of(place * (2 * BLK) + member * BLK + skip, 16), count)


class GatherRingLast:
    def __init__(self, links, ring, pair, buf, cols, source=None):
        self.l, self.ring, self.pair, self.buf, self.cols = links, ring, pair, buf, cols
        self.mine, self.source = getattr(links, pair), source

    def at(self, step, member):
        return self.buf.at[rows_of(self.l.place(self.ring, step), member), self.cols]

    def send(self, ref, step, source=None):
        to = self.l.ring(self.ring, step) if step else self.l.other(self.pair)
        return self.l.copy(ref if source is None else source, ref, to)

    def start(self):
        own = self.at(0, self.mine)
        self.y = self.send(own, 0, self.source)
        self.own_p = self.send(own, 1, self.source)
        self.own_m = self.send(own, -1, self.source)

    def second(self):
        theirs = self.at(0, 1 - self.mine)
        self.oth_p = self.send(theirs, 1)
        self.oth_m = self.send(theirs, -1)

    def onward_p(self):
        self.far_p = self.send(self.at(-1, self.mine), 1)

    def onward_m(self):
        self.far_m = self.send(self.at(1, 1 - self.mine), -1)

    def arrived(self, step):
        if step == 0:
            return [self.y]
        if step == 2:
            return [self.far_p, self.far_m]
        return [self.own_p, self.oth_p] if step == -1 else [self.own_m, self.oth_m]

    def tasks(self, t, name, after):
        t.add(name + "0", after, lambda: [], self.start)
        t.add(name + "1", [name + "0"], lambda: [self.y], self.second)
        t.add(name + "p", [name + "0"], lambda: [self.own_p], self.onward_p)
        t.add(name + "m", [name + "1"], lambda: [self.oth_m], self.onward_m)


class GatherRingFirst:
    def __init__(self, links, ring, pair, buf, cols):
        self.l, self.ring, self.pair, self.buf, self.cols = links, ring, pair, buf, cols
        self.mine = getattr(links, pair)

    def at(self, step, count=BLK, skip=0):
        return self.buf.at[rows_of(self.l.place(self.ring, step), self.mine, count, skip), self.cols]

    def send(self, ref, step):
        to = self.l.ring(self.ring, step) if step else self.l.other(self.pair)
        return self.l.copy(ref, ref, to)

    def start(self):
        own = self.at(0)
        self.own_p = self.send(own, 1)
        self.own_m = self.send(own, -1)
        self.y0 = self.send(own, 0)

    def onward_p(self):
        self.far_p = self.send(self.at(-1, BLK // 2), 1)
        self.yp = self.send(self.at(-1), 0)

    def onward_m(self):
        self.far_m = self.send(self.at(1, BLK // 2, BLK // 2), -1)
        self.ym = self.send(self.at(1), 0)

    def across_p(self):
        self.yfp = self.send(self.at(2, BLK // 2), 0)

    def across_m(self):
        self.yfm = self.send(self.at(2, BLK // 2, BLK // 2), 0)

    def arrived(self, step):
        if step == 0:
            return [self.y0]
        if step == 2:
            return [self.yfp, self.yfm]
        return [self.yp] if step == -1 else [self.ym]

    def tasks(self, t, name, after):
        t.add(name + "0", after, lambda: [], self.start)
        t.add(name + "p", [name + "0"], lambda: [self.own_p], self.onward_p)
        t.add(name + "m", [name + "0"], lambda: [self.own_m], self.onward_m)
        t.add(name + "yp", [name + "p"], lambda: [self.far_p], self.across_p)
        t.add(name + "ym", [name + "m"], lambda: [self.far_m], self.across_m)


class ReduceRingFirst:
    def __init__(self, links, ring, pair, part, out, col, out_col, width, slots):
        self.l, self.ring, self.pair = links, ring, pair
        self.part, self.out, self.col, self.width, self.slots = part, out, col, width, slots
        self.out_cols = pl.ds(out_col, width)
        self.mine = getattr(links, pair)

    def block(self, step, member):
        return self.out.at[rows_of(self.l.place(self.ring, step), member), self.out_cols]

    def plan(self):
        l = self.l
        self.p2 = l.plan(self.block(2, 0), self.slots.at[0], l.ring(self.ring, 1))
        self.m2 = l.plan(self.block(2, 1), self.slots.at[1], l.ring(self.ring, -1))
        self.p1 = l.plan(self.block(1, 1), self.slots.at[2], l.ring(self.ring, 1))
        self.m1 = l.plan(self.block(-1, 0), self.slots.at[3], l.ring(self.ring, -1))

    def sent(self):
        for c in (self.p2, self.m2, self.p1, self.m1):
            c.start()

    def sent_pair(self, place):
        step = lax.rem(place - getattr(self.l, self.ring) + 4, 4)

        @pl.when(step == 2)
        def _():
            self.p2.start()
            self.m2.start()

        @pl.when(step == 1)
        def _():
            self.p1.start()

        @pl.when(step == 3)
        def _():
            self.m1.start()

    def add(self, dst, start, *slots):
        def body(r):
            total = self.part[pl.ds(start + r, ROWS), pl.ds(self.col, self.width)]
            for s in slots:
                total = total + self.slots[s, pl.ds(r, ROWS), :].astype(F32)
            dst(r, total)

        row_loop(BLK, ROWS, body)

    def start_of(self, step, member):
        return pl.multiple_of(self.l.place(self.ring, step) * (2 * BLK) + member * BLK, BLK)

    def to_slot(self, slot):
        def put(r, total):
            self.slots[slot, pl.ds(r, ROWS), :] = total.astype(BF16)

        return put

    def combine_p(self):
        self.add(self.to_slot(7), self.start_of(1, 0), 0)
        self.pc = self.l.copy(self.slots.at[7], self.slots.at[4], self.l.ring(self.ring, 1))

    def combine_m(self):
        self.add(self.to_slot(8), self.start_of(-1, 1), 1)
        self.mc = self.l.copy(self.slots.at[8], self.slots.at[5], self.l.ring(self.ring, -1))

    def across(self):
        for member, slots in ((0, (4, 3)), (1, (2, 5))):
            start = self.start_of(0, member)

            def put(r, total, start=start):
                self.part[pl.ds(start + r, ROWS), pl.ds(self.col, self.width)] = total

            self.add(put, start, *slots)
        self.add(self.to_slot(9), self.start_of(0, 1 - self.mine))
        self.y = self.l.copy(self.slots.at[9], self.slots.at[6], self.l.other(self.pair))

    def tasks(self, t, name, put, after, final):
        t.add(name + "p", [after], lambda: [self.p2], self.combine_p)
        t.add(name + "m", [after], lambda: [self.m2], self.combine_m)
        t.add(
            name + "y", [after, name + "p", name + "m"],
            lambda: [self.p1, self.m1, self.pc, self.mc], self.across,
        )
        t.add(
            name + "f", [name + "y"] + final, lambda: [self.y],
            lambda: self.add(put, self.start_of(0, self.mine), 6),
        )


class ReducePairFirst:
    def __init__(self, links, ring, pair, part, out, col, out_col, width, slots, halves):
        self.l, self.ring, self.pair = links, ring, pair
        self.part, self.out, self.col, self.width = part, out, col, width
        self.out_cols = pl.ds(out_col, width)
        self.slots, self.halves = slots, halves
        self.mine = getattr(links, pair)

    def plan(self):
        self.y = [self.to_pair(self.l.place("x", i), i) for i in range(4)]
        self.first = self.l.used - 4

    def to_pair(self, place, i, slot=None):
        block = self.out.at[rows_of(place, 1 - self.mine), self.out_cols]
        return self.l.plan(block, self.slots.at[i], self.l.other(self.pair), slot)

    def from_x(self, step):
        return lax.rem(self.l.place(self.ring, step) - self.l.x + 4, 4)

    def came(self, step):
        i = self.from_x(step)
        return [self.to_pair(self.l.place(self.ring, step), i, self.first + i)]

    def add(self, dst, step, skip, count, *halves):
        start = pl.multiple_of(self.l.place(self.ring, step) * (2 * BLK) + self.mine * BLK + skip, 64)
        slot = self.from_x(step)

        def body(r):
            total = self.part[pl.ds(start + r, ROWS), pl.ds(self.col, self.width)]
            total = total + self.slots[slot, pl.ds(skip + r, ROWS), :].astype(F32)
            for h in halves:
                total = total + self.halves[h, pl.ds(r, ROWS), :].astype(F32)
            dst(r, total)

        row_loop(count, ROWS, body)

    def to_half(self, half):
        def put(r, total):
            self.halves[half, pl.ds(r, ROWS), :] = total.astype(BF16)

        return put

    def ring_copy(self, src, dst, step):
        return self.l.copy(src, self.halves.at[dst], self.l.ring(self.ring, step))

    def far(self):
        def put(r, total):
            self.slots[4, pl.ds(r, ROWS), :] = total.astype(BF16)

        self.add(put, 2, 0, BLK)
        self.p2 = self.ring_copy(self.slots.at[4, pl.ds(0, BLK // 2)], 0, 1)
        self.m2 = self.ring_copy(self.slots.at[4, pl.ds(BLK // 2, BLK // 2)], 1, -1)

    def near_p(self):
        self.add(self.to_half(6), 1, BLK // 2, BLK // 2)
        self.p1 = self.ring_copy(self.halves.at[6], 2, 1)

    def near_m(self):
        self.add(self.to_half(7), -1, 0, BLK // 2)
        self.m1 = self.ring_copy(self.halves.at[7], 3, -1)

    def combine_p(self):
        self.add(self.to_half(8), 1, 0, BLK // 2, 0)
        self.pc = self.ring_copy(self.halves.at[8], 4, 1)

    def combine_m(self):
        self.add(self.to_half(9), -1, BLK // 2, BLK // 2, 1)
        self.mc = self.ring_copy(self.halves.at[9], 5, -1)

    def finish(self, put):
        half = BLK // 2
        self.add(put, 0, 0, half, 4, 3)
        self.add(lambda r, total: put(half + r, total), 0, half, half, 2, 5)

    def tasks(self, t, name, put, after, final):
        t.add(name + "2", [after], lambda: self.came(2), self.far)
        t.add(name + "1", [after], lambda: self.came(1), self.near_p)
        t.add(name + "3", [after], lambda: self.came(-1), self.near_m)
        t.add(name + "p", [name + "2", name + "1"], lambda: [self.p2], self.combine_p)
        t.add(name + "m", [name + "2", name + "3"], lambda: [self.m2], self.combine_m)
        t.add(
            name + "f", [after, name + "p", name + "m"] + final,
            lambda: self.came(0) + [self.p1, self.m1, self.pc, self.mc],
            lambda: self.finish(put),
        )


class Tasks:
    def __init__(self, links):
        self.l, self.all = links, {}

    def add(self, name, after, waits, do):
        self.all[name] = (after, waits, do)

    def step(self, name):
        _, waits, do = self.all[name]
        for c in waits():
            self.l.take(c)
        do()


ORDER = (
    "t0", "tp", "t1", "ts0", "c0", "ts1", "hpart0", "tm", "ts-1", "c1", "cs0", "hpart1", "ts2", "hpart-1",
    "cs1", "cp", "cs-1", "cm", "hpart2", "gpart0", "gpart1", "cs2", "gpart-1", "gpart2", "hap", "ham", "gam",
    "hb1", "hb2", "gap", "hb3", "hay", "hbm", "hbp", "gay", "gb2", "gb3", "turn", "gb1", "haf", "hbf", "hA0",
    "hB0", "gaf", "gbp", "gA0", "hBm", "gbm", "hA1", "hBp", "gbf", "gB0", "hAm", "hAp", "hByp", "ox0", "ox1",
    "hBym", "ox-1", "gA1", "ix0", "gBm", "om1", "om0", "gBp", "gAp", "om-1", "ox2", "go0", "gAm", "ix1",
    "om2", "or", "gByp", "gBym", "ix-1", "go1", "ix2", "odp", "odm", "im0", "im-1", "im1", "go", "im2", "ir",
    "gj0", "ody", "idm", "idp", "ie2", "gi0", "gi", "ie3", "idy", "ie1", "odf", "iem", "iep", "ief", "idf",
)


def run_tasks(t):
    done = set()
    for name in ORDER:
        assert done.issuperset(t.all[name][0]), name
        t.step(name)
        done.add(name)
    assert len(done) == len(t.all)


def dot(a, b, left, right):
    return lax.dot_general(a, b, (((left,), (right,)), ((), ())), preferred_element_type=F32)


STEPS = (2, 1, -1, 0)
ARRIVAL = (0, 1, -1, 2)


def kernel(
    tok_in, wi_in, wo_in, cot_in,
    out_ref, gt_ref, gi_ref, go_ref,
    tok, cot, wi, wo,
    part_h, part_g, send_h, send_g,
    ra_h, ra_g, rb_h, rb_g, rh_h, rh_g,
    hid, acts, ghid,
    sib_in, rbuf, rd_h, rd_g, re_g, rf_g,
    gi, go, turned,
    send, recv, local,
):
    l = Links(send, recv)
    t = Tasks(l)
    k = l.k
    sib = l.other("k")

    barrier = pltpu.get_barrier_semaphore()
    near = [sib, l.other("yl"), l.other("yh")]
    near += [l.ring(a, s) for a in ("z", "x") for s in (1, -1)]
    for d in near:
        pl.semaphore_signal(barrier, inc=1, device_id=d, device_id_type=pl.DeviceIdType.MESH)

    my_d = pl.ds(pl.multiple_of(k * DC, 128), DC)
    its_d = pl.ds(pl.multiple_of((1 - k) * DC, 128), DC)
    my_f = pl.ds(pl.multiple_of(k * FH, 128), FH)
    its_f = pl.ds(pl.multiple_of((1 - k) * FH, 128), FH)
    own_rows = rows_of(l.x, l.yh)

    load_tok = pltpu.make_async_copy(tok_in, tok.at[own_rows, my_d], local.at[0])
    load_cot = pltpu.make_async_copy(cot_in, cot.at[own_rows, my_d], local.at[1])
    load_wi = pltpu.make_async_copy(wi_in.at[:, my_f], wi.at[my_d], local.at[2])
    load_wo = pltpu.make_async_copy(wo_in.at[my_f], wo.at[:, my_d], local.at[3])
    for c in (load_tok, load_wi, load_cot, load_wo):
        c.start()
    pl.semaphore_wait(barrier, len(near))

    def pair_rows(axis, step):
        return pl.ds(pl.multiple_of(l.place(axis, step) * (2 * BLK), 2 * BLK), 2 * BLK)

    shared = {}

    def gather_tokens(name, buf, source, load, weight, target, after):
        g = GatherRingLast(l, "x", "yh", buf, my_d, source)

        def start():
            g.start()
            shared[name + "w"] = l.copy(weight, target, sib)

        g.tasks(t, name, after)
        t.add(name + "0", after, lambda: [], start)

        def share(step):
            def do():
                if step == 0:
                    load.wait()
                ref = buf.at[pair_rows("x", step), my_d]
                shared[name + str(step)] = l.copy(ref, ref, sib)

            return do

        for step, before in ((0, ["1"]), (1, ["1"]), (-1, ["1"]), (2, ["p", "m"])):
            t.add(
                name + "s" + str(step), [name + b for b in before],
                lambda step=step: g.arrived(step), share(step),
            )

    gather_tokens("t", tok, tok_in, load_tok, wi_in.at[:, its_f], wi.at[my_d], [])
    gather_tokens("c", cot, cot_in, load_cot, wo_in.at[its_f], wo.at[:, my_d], ["t1"])

    def put_hidden(col, width):
        cols = pl.ds(col, width)

        def put(r, h):
            hid[pl.ds(r, ROWS), cols] = h
            tanh = jnp.tanh(C_GELU * (h + C_CUBE * (h * h * h)))
            acts[pl.ds(own + r, ROWS), cols] = (0.5 * h * (1.0 + tanh)).astype(BF16)

        return put

    def put_grad(col, width):
        cols = pl.ds(col, width)

        def put(r, total):
            h = hid[pl.ds(r, ROWS), cols]
            square = h * h
            tanh = jnp.tanh(C_GELU * (h + C_CUBE * (square * h)))
            slope = 0.5 * (1.0 + tanh)
            slope += (0.5 * C_GELU) * h * (1.0 - tanh * tanh) * (1.0 + 3.0 * C_CUBE * square)
            ghid[pl.ds(own + r, ROWS), cols] = (total * slope).astype(BF16)

        return put

    own = pl.multiple_of(l.z * (2 * BLK) + l.yl * BLK, BLK)

    def reduction(name, fa, source, load, product, part, out, slots_a, slots_b, halves, put, gathered, final):
        ring = ReduceRingFirst(l, "z", "yl", part, out, 0, 0, fa, slots_a)
        pair = ReducePairFirst(l, "z", "yl", part, out, fa, fa, FH - fa, slots_b, halves)

        def partial(step):
            def do():
                if step == ARRIVAL[0]:
                    load.wait()
                    ring.plan()
                    pair.plan()
                rows = pair_rows("x", step)

                def tile(n):
                    cols = pl.ds(pl.multiple_of(n * 256, 256), 256)
                    total = product(rows, cols)
                    part[rows, cols] = total
                    out[rows, cols] = total.astype(BF16)

                tiles(FH // 256, tile)
                pair.y[step % 4].start()
                ring.sent_pair(l.place("x", step))

            return do

        for i, step in enumerate(ARRIVAL):
            before = [source + "s" + str(step)] + [name + "part" + str(ARRIVAL[i - 1])] * (i > 0)
            t.add(
                name + "part" + str(step), before,
                lambda step=step: [shared[source + "w"], shared[source + str(step)]], partial(step),
            )
        last = name + "part" + str(ARRIVAL[-1])
        ring.tasks(t, name + "a", put(0, fa), last, final)
        pair.tasks(t, name + "b", put(fa, FH - fa), last, final)
        a = GatherRingLast(l, "z", "yl", gathered, pl.ds(0, fa))
        b = GatherRingFirst(l, "z", "yl", gathered, pl.ds(fa, FH - fa))
        a.tasks(t, name + "A", [name + "af"])
        b.tasks(t, name + "B", [name + "bf"])
        return a, b

    gathers_h = reduction(
        "h", FA_H, "t", load_wi, lambda rows, cols: dot(tok[rows, :], wi[:, cols], 1, 0),
        part_h, send_h, ra_h, rb_h, rh_h, put_hidden, acts, [],
    )
    gathers_g = reduction(
        "g", FA_G, "c", load_wo, lambda rows, cols: dot(cot[rows, :], wo[cols, :], 1, 1),
        part_g, send_g, ra_g, rb_g, rh_g, put_grad, ghid, ["haf", "hbf"],
    )

    merged = {}

    def projection(name, which, before, gathers, part, lhs, weight, right, target, slots, split_slots):
        wide = FA_D if split_slots else DC
        ring = ReduceRingFirst(l, "x", "yh", part, rbuf.at[which], DP, 0, wide, slots)
        pair = split_slots and ReducePairFirst(
            l, "x", "yh", part, rbuf.at[which], DP + wide, wide, DC - wide, *split_slots
        )

        def project(step):
            def do():
                rows = pair_rows("z", step)

                def tile(n):
                    cols = pl.ds(pl.multiple_of(n * 256, 256), 256)
                    part[rows, cols] = dot(lhs[rows, :], weight[(cols, slice(None))[::2 * right - 1]], 1, right)

                tiles(DP // 256, tile)
                merged[name + str(step)] = l.copy(part.at[rows, its_d], sib_in.at[which, rows], sib)

            return do

        def merge(step):
            def do():
                start = pl.multiple_of(l.place("z", step) * (2 * BLK), 2 * BLK)

                def body(r):
                    at = pl.ds(start + r, ROWS)
                    total = part[at, my_d] + sib_in[which, at, :]
                    part[at, pl.ds(DP, DC)] = total
                    rbuf[which, at, :] = total.astype(BF16)

                row_loop(2 * BLK, ROWS, body)

            return do

        for step, need in ((0, ["A1", "B0"]), (1, ["A1", "Bm"]), (-1, ["A1", "Bp"]), (2, ["Ap", "Am", "Byp", "Bym"])):
            t.add(
                name + "x" + str(step), [before + n for n in need] + [before + "af", before + "bf"],
                lambda step=step: gathers[0].arrived(step) + gathers[1].arrived(step), project(step),
            )
            t.add(
                name + "m" + str(step), [name + "x" + str(step)],
                lambda step=step: [merged[name + str(step)]], merge(step),
            )

        def go_round():
            ring.plan()
            ring.sent()
            if pair:
                pair.plan()
                for i in (2, 1, 3, 0):
                    pair.y[i].start()

        merges = [name + "m" + str(s) for s in STEPS]
        t.add(name + "r", merges, lambda: [], go_round)

        def put(col, width):
            def body(r, total):
                target[pl.ds(r, ROWS), pl.ds(col, width)] = total.astype(BF16)

            return body

        ring.tasks(t, name + "d", put(0, wide), name + "r", [])
        if pair:
            pair.tasks(t, name + "e", put(wide, DC - wide), name + "r", [])

    projection("o", 0, "h", gathers_h, part_h, acts, wo, 0, out_ref, rd_h, ())
    projection("i", 1, "g", gathers_g, part_g, ghid, wi, 1, gt_ref, rd_g, (re_g, rf_g))

    whole_h = ["ox" + str(s) for s in STEPS] + ["cs" + str(s) for s in STEPS]
    whole_g = ["ix" + str(s) for s in STEPS]

    def grad_out_tiles(half):
        def tile(n):
            cols = pl.ds(pl.multiple_of(half * (FH // 2) + n * 256, 256), 256)
            go[cols, :] = dot(acts[:, cols], cot[...], 0, 0).astype(BF16)

        return lambda: tiles(FH // 512, tile)

    for half in range(2):
        t.add("go" + str(half), whole_h + ["gpart2"], lambda: [], grad_out_tiles(half))
    ends = []

    def send_go():
        ends.append(l.copy(go.at[:, its_d], go_ref.at[my_f], sib))
        own_start = pl.multiple_of(k * FH, 128)

        def keep(r):
            go_ref[pl.ds(own_start + r, 32), :] = go[pl.ds(r, 32), my_d]

        row_loop(FH, 32, keep)

    t.add("go", ["go0", "go1"], lambda: [], send_go)

    def turn_tokens():
        def tile(n):
            cols = pl.ds(pl.multiple_of(n * 128, 128), 128)
            turned[cols, :] = tok[:, cols].T

        tiles(DP // 128, tile)

    t.add("turn", ["hpart2"], lambda: [], turn_tokens)

    def grad_in_tiles(rows, start, target):
        def tile(n):
            cols = pl.ds(pl.multiple_of(n * 256, 256), 256)
            at = pl.ds(pl.multiple_of(start + n * 256, 128), 256)
            target[:, at] = dot(turned[rows, :], ghid[:, cols], 1, 0).astype(BF16)

        return lambda: tiles(FH // 256, tile)

    t.add("gi0", whole_g + ["turn"], lambda: [], grad_in_tiles(its_d, 0, gi))
    t.add("gj0", whole_g + ["turn"], lambda: [], grad_in_tiles(my_d, k * FH, gi_ref))
    t.add("gi", ["gi0"], lambda: [], lambda: ends.append(l.copy(gi, gi_ref.at[:, my_f], sib)))

    run_tasks(t)

    for c in ends:
        l.take(c)
    for c in l.started:
        c.wait_send()


def hand_over(*refs):
    sems = refs[-1]
    copies = []
    for src, dst in zip(refs[:4], refs[4:8]):
        parts = 4 if src.shape[0] > BLK else 1
        rows = src.shape[0] // parts
        for p in range(parts):
            at = pl.ds(p * rows, rows)
            copies.append(pltpu.make_async_copy(src.at[at], dst.at[at], sems.at[len(copies)]))
    for c in copies:
        c.start()
    for c in copies:
        c.wait()


def local(tokens, weight_in, weight_out, cotangent):
    results = block(tokens, weight_in, weight_out, cotangent)
    any_space = pl.BlockSpec(memory_space=pl.ANY)
    return pl.pallas_call(
        hand_over,
        out_shape=tuple(jax.ShapeDtypeStruct(r.shape, r.dtype) for r in results),
        in_specs=[any_space] * 4,
        out_specs=(any_space,) * 4,
        scratch_shapes=[pltpu.SemaphoreType.DMA((10,))],
        compiler_params=pltpu.CompilerParams(vmem_limit_bytes=2 * 1024 * 1024),
    )(*results)


def block(tokens, weight_in, weight_out, cotangent):
    any_space = pl.BlockSpec(memory_space=pl.ANY)
    shape = jax.ShapeDtypeStruct
    vmem = pltpu.VMEM
    return pl.pallas_call(
        kernel,
        out_shape=(
            vmem((BLK, DC), BF16),
            vmem((BLK, DC), BF16),
            vmem((DC, 2 * FH), BF16),
            vmem((2 * FH, DC), BF16),
        ),
        in_specs=[any_space] * 4,
        out_specs=(pl.BlockSpec(memory_space=pltpu.VMEM),) * 4,
        scratch_shapes=[
            vmem((TOK, DP), BF16), vmem((TOK, DP), BF16), vmem((DP, FH), BF16), vmem((FH, DP), BF16),
            vmem((TOK, FH), F32), vmem((TOK, FH), F32), vmem((TOK, FH), BF16), vmem((TOK, FH), BF16),
            vmem((10, BLK, FA_H), BF16), vmem((10, BLK, FA_G), BF16),
            vmem((5, BLK, FH - FA_H), BF16), vmem((5, BLK, FH - FA_G), BF16),
            vmem((10, BLK // 2, FH - FA_H), BF16), vmem((10, BLK // 2, FH - FA_G), BF16),
            vmem((BLK, FH), F32), vmem((TOK, FH), BF16), vmem((TOK, FH), BF16),
            vmem((2, TOK, DC), F32), vmem((2, TOK, DC), BF16),
            vmem((10, BLK, DC), BF16), vmem((10, BLK, FA_D), BF16),
            vmem((5, BLK, DC - FA_D), BF16), vmem((10, BLK // 2, DC - FA_D), BF16),
            vmem((DC, FH), BF16), vmem((FH, DP), BF16), vmem((DP, TOK), BF16),
            pltpu.SemaphoreType.DMA((COPIES,)), pltpu.SemaphoreType.DMA((COPIES,)),
            pltpu.SemaphoreType.DMA((4,)),
        ],
        compiler_params=pltpu.CompilerParams(
            collective_id=0, has_side_effects=True, vmem_limit_bytes=55 * 1024 * 1024
        ),
        cost_estimate=pl.CostEstimate(flops=14_500_000_000, bytes_accessed=12_000_000, transcendentals=400_000),
    )(tokens, weight_in, weight_out, cotangent)


def solution(mesh):
    placed = (P("row", "col"), P("col", "row"), P("row", "col"), P("row", "col"))
    return jax.shard_map(
        local,
        mesh=mesh,
        in_specs=placed,
        out_specs=(P("row", "col"), P("row", "col"), P("col", "row"), P("row", "col")),
        check_vma=False,
    )
```
